32 devices in a mesh: dp: 16 (over z, y, x), ctx: 2 (over core).
Axes of the slice: x: 2, y: 2, z: 4, core: 2. Of those that a mesh axis runs over, the one named last changes fastest.
Arguments:
- queries: bfloat16 [16, 256, 128], P('dp', 'ctx'), may hold values from -6 to 6
- key_vectors: bfloat16 [16, 256, 128], P('dp', 'ctx'), may hold values from -6 to 6
- value_vectors: bfloat16 [16, 256, 128], P('dp', 'ctx'), may hold values from -6 to 6
- log_decay: float32 [16, 256, 128], P('dp', 'ctx'), may hold values from -2 to 0, as said below
- out_weight: bfloat16 [5120, 128], replicated, may hold values from -0.5 to 0.5
- cotangent: bfloat16 [16, 256, 5120], P('dp', 'ctx'), may hold values from -0.3984375 to 0.3984375
Outputs:
- grad_queries: bfloat16 [16, 256, 128], P('dp', 'ctx')
- grad_keys: bfloat16 [16, 256, 128], P('dp', 'ctx')
- grad_values: bfloat16 [16, 256, 128], P('dp', 'ctx')
- grad_decay: float32 [16, 256, 128], P('dp', 'ctx')
- grad_weight: float32 [5120, 128], P('dp')
The draws below stay inside these ranges and needn't reach their ends.
Inputs may be any that keep to these rules, and one draw needn't show every extreme that they name: `log_decay`: every entry is negative.
All inputs are finite; a program needn't handle non-finite values.
Results may differ from the reference program's by a relative error of at most 0.0029.
Values sent between devices are 32-bit elements; how exact they have to be, the bound alone decides.
No kernel may reach another device: no remote copies, remote signals or barrier semaphores. Data moves between devices by JAX's collectives and lax.ppermute only.
A program may use at most 64 MiB of HBM per device.

```python
import jax
import jax.numpy as jnp
from jax import lax

D = 5120
DK = 128
HEADS = 1
BLK = 128
TOK_DEV = 128
HK = 128
SEQUENCE_LENGTH = 256
BATCH = 16


def draw_log_decay(key, part):
    subkeys = jax.random.split(jax.random.fold_in(key, 17), 7)
    fast_share = 0.5
    is_fast = jax.random.uniform(subkeys[0], (BATCH, 1, HK)) < fast_share
    fast_rate = jnp.exp(jax.random.uniform(subkeys[1], (BATCH, 1, HK), minval=jnp.log(1.0 / 50.0), maxval=jnp.log(1.0 / 30.0)))
    slow_rate = jnp.exp(jax.random.uniform(subkeys[2], (BATCH, 1, HK), minval=jnp.log(0.05 / SEQUENCE_LENGTH), maxval=jnp.log(0.3 / SEQUENCE_LENGTH)))
    decay_speed = jnp.where(is_fast, fast_rate, slow_rate)
    segments = SEQUENCE_LENGTH // TOK_DEV
    device_multiplier = jnp.exp(jax.random.uniform(subkeys[3], (BATCH, segments, 1, HK), minval=jnp.log(0.5), maxval=jnp.log(2.0)))
    device_multiplier = jnp.broadcast_to(device_multiplier, (BATCH, segments, TOK_DEV, HK)).reshape(BATCH, SEQUENCE_LENGTH, HK)
    token_multiplier = jnp.exp(jax.random.uniform(subkeys[4], (BATCH, SEQUENCE_LENGTH, HK), minval=jnp.log(0.5), maxval=jnp.log(2.0)))
    token_positions = jax.random.randint(subkeys[5], (BATCH, 2, 1), 0, SEQUENCE_LENGTH)
    spike_strength = jax.random.uniform(subkeys[6], (BATCH, 2, 1), minval=jnp.log(0.5), maxval=jnp.log(0.8))
    during_spike = jnp.arange(SEQUENCE_LENGTH)[None, None, :] == token_positions
    spike_log_decay = jnp.sum(jnp.where(during_spike, spike_strength, 0.0), axis=1)[:, :, None]
    return (-decay_speed * device_multiplier * token_multiplier + spike_log_decay).astype(jnp.float32)


def spiked(array, stream_key, source, target, blocks, factor):
    def block_of(axis_at):
        return (jnp.arange(array.shape[axis_at]) // (array.shape[axis_at] // blocks)).reshape((-1,) + (1,) * (array.ndim - 1 - axis_at))

    near = jax.random.permutation(stream_key, blocks)[block_of(target)]
    second = (block_of(target) + blocks // 2) % blocks
    return jnp.where((block_of(source) == near) | (block_of(source) == second), factor * array, array)


def levels(rng, shape, pieces, low, top_value):
    def one(axis_at, parts):
        steps = jax.random.uniform(jax.random.fold_in(jax.random.fold_in(rng, 6), axis_at), (parts,), jnp.float32, low / len(pieces), top_value / len(pieces))
        return jnp.repeat(jnp.exp(steps), shape[axis_at] // parts).reshape((-1,) + (1,) * (len(shape) - axis_at - 1))

    loudness = one(*pieces[0])
    for cut in pieces[1:]:
        loudness = loudness * one(*cut)
    return loudness


def noise(rng, dims, deviation, reach, cuts=(), kind=jnp.bfloat16):
    values = deviation * jax.random.normal(rng, dims, jnp.float32)
    if cuts:
        values = values * levels(rng, dims, cuts, -0.22, 0.18)
    return jnp.clip(values, -reach, reach).astype(kind)


def noise_with(own_key, shape, width, most, pieces, heavy, held_as=jnp.bfloat16):
    array = width * jax.random.normal(own_key, shape, jnp.float32)
    if pieces:
        array = array * levels(own_key, shape, pieces, -0.22, 0.18)
    return jnp.clip(spiked(array, jax.random.fold_in(own_key, 3), *heavy), -most, most).astype(held_as)


def setup_inputs(seed: int = 0) -> dict:
    arg_keys = jax.random.split(jax.random.key(seed), 7)
    return {
        "queries": noise(arg_keys[0], (BATCH, SEQUENCE_LENGTH, HK), 1.0, 6.0, ((0, 16), (1, 2))),
        "key_vectors": noise(arg_keys[1], (BATCH, SEQUENCE_LENGTH, HK), 1.0, 6.0, ((0, 16), (1, 2))),
        "value_vectors": noise(arg_keys[2], (BATCH, SEQUENCE_LENGTH, HK), 1.0, 6.0, ((0, 16), (1, 2))),
        "log_decay": draw_log_decay(jax.random.fold_in(arg_keys[6], 71), 0),
        "out_weight": noise(arg_keys[4], (D, HK), HK ** -0.5, 0.5),
        "cotangent": noise_with(arg_keys[5], (BATCH, SEQUENCE_LENGTH, D), 0.05, 0.3984375, ((0, 16), (1, 2)), (0, 2, 16, 2.0)),
    }


EPSILON = 1e-05
PRECISE = lax.Precision.HIGHEST

def normalize_heads(output):
    return output * lax.rsqrt(lax.optimization_barrier(jnp.mean(output * output, axis=-1, keepdims=True)) + EPSILON)

def attend(query_rows, key_rows, value_rows, decay_rows):
    blocks = query_rows.shape[0] // BLK
    shaped = (blocks, BLK, HEADS, DK)
    query_blk = query_rows.reshape(shaped)
    key_blk = key_rows.reshape(shaped)
    value_blk = value_rows.reshape(shaped)
    decay_blk = decay_rows.reshape(shaped)
    cumul = jnp.cumsum(decay_blk, axis=1)
    totals = cumul[:, -1]
    query_scaled = query_blk * jnp.exp(cumul)
    key_scaled = key_blk * jnp.exp(-cumul)
    key_to_end = key_blk * jnp.exp(totals[:, None] - cumul)
    causal = jnp.tril(jnp.ones((BLK, BLK), jnp.float32))
    scores = jnp.einsum('nihc,njhc->nhij', query_scaled, key_scaled, precision=PRECISE) * causal
    within = jnp.einsum('nhij,njhe->nihe', scores, value_blk, precision=PRECISE)
    block_states = jnp.einsum('njhc,njhe->nhce', key_to_end, value_blk, precision=PRECISE)

    def advance(carry, inputs):
        block_decay, block_state = inputs
        return (jnp.exp(block_decay)[..., None] * carry + block_state, carry)
    initial = jnp.zeros((HEADS, DK, DK), jnp.float32)
    last_state, entries = lax.scan(advance, initial, (totals, block_states))
    across = jnp.einsum('nihc,nhce->nihe', query_scaled, entries, precision=PRECISE)
    return normalize_heads(within + across).reshape(blocks * BLK, HEADS * DK)

def reference(queries, key_vectors, value_vectors, log_decay, out_weight, cotangent):

    def one_sequence(weight_sum, inputs):
        query_row, key_row, value_row, decay_row, upstream_row = inputs
        normed, pullback = jax.vjp(attend, query_row.astype(jnp.float32), key_row.astype(jnp.float32), value_row.astype(jnp.float32), decay_row)
        grad_normed = jnp.dot(upstream_row, out_weight, preferred_element_type=jnp.float32)
        grad_query, grad_key, grad_value, grad_gate = pullback(grad_normed)
        rounded = normed.astype(jnp.bfloat16)
        contribution = jnp.dot(upstream_row.T, rounded, preferred_element_type=jnp.float32)
        outputs = (grad_query.astype(jnp.bfloat16), grad_key.astype(jnp.bfloat16), grad_value.astype(jnp.bfloat16), grad_gate)
        return (weight_sum + contribution, outputs)
    initial = jnp.zeros((D, HEADS * DK), jnp.float32)
    grad_weight, grads = lax.scan(one_sequence, initial, (queries, key_vectors, value_vectors, log_decay, cotangent))
    return (grads[0], grads[1], grads[2], grads[3], grad_weight)
```

```python
import functools

import jax
import jax.numpy as jnp
from jax import lax
from jax.experimental import pallas as pl
from jax.experimental.pallas import tpu as pltpu
from jax.sharding import PartitionSpec as P

EPSILON = 1e-05
VMEM_BYTES = 24 * 1024 * 1024
F32 = jnp.float32
BF16 = jnp.bfloat16
BOTH = ("dp", "ctx")


def split(value, parts):
    pieces = []
    for index in range(parts):
        piece = value.astype(BF16)
        pieces.append(piece)
        if index + 1 < parts:
            value = value - piece.astype(F32)
    return pieces


def product(left, right, left_axis, right_axis):
    dims = (((left_axis,), (right_axis,)), ((), ()))
    most = max(len(left), len(right))
    total = None
    for order in reversed(range(most)):
        for i, l in enumerate(left):
            j = order - i
            if 0 <= j < len(right):
                term = lax.dot_general(l, right[j], dims, preferred_element_type=F32)
                total = term if total is None else total + term
    return total


def lower_mask(length):
    rows = lax.broadcasted_iota(jnp.int32, (length, length), 0)
    columns = lax.broadcasted_iota(jnp.int32, (length, length), 1)
    return rows >= columns


def cumulate(decay):
    lower = lower_mask(decay.shape[0]).astype(F32).astype(BF16)
    return product([lower], split(decay, 3), 1, 0)


def state_kernel(key_ref, value_ref, decay_ref, state_ref):
    cumul = cumulate(decay_ref[0])
    to_end = jnp.exp(cumul[-1:] - cumul)
    key_to_end = key_ref[0].astype(F32) * to_end
    state_ref[...] = product(split(key_to_end, 2), [value_ref[0]], 0, 0)


def within_kernel(query_ref, key_ref, value_ref, decay_ref, within_ref, scores_ref, cumul_ref):
    cumul = cumulate(decay_ref[0])
    cumul_ref[...] = cumul
    query_scaled = query_ref[0].astype(F32) * jnp.exp(cumul)
    key_scaled = key_ref[0].astype(F32) * jnp.exp(-cumul)
    scores = product(split(query_scaled, 2), split(key_scaled, 2), 1, 1)
    scores = jnp.where(lower_mask(cumul.shape[0]), scores, 0.0)
    scores_ref[...] = scores
    within_ref[...] = product(split(scores, 2), [value_ref[0]], 1, 0)


def normed_kernel(query_ref, cumul_ref, within_ref, state_ref, normed_ref, scale_ref, rounded_ref):
    query_scaled = query_ref[0].astype(F32) * jnp.exp(cumul_ref[...])
    output = within_ref[...] + product(split(query_scaled, 2), split(state_ref[...], 2), 1, 0)
    scale_inv = lax.rsqrt(jnp.mean(output * output, axis=-1, keepdims=True) + EPSILON)
    normed = output * scale_inv
    normed_ref[...] = normed
    scale_ref[...] = jnp.broadcast_to(scale_inv, normed.shape)
    rounded_ref[...] = normed.astype(BF16).astype(F32)


def grads_kernel(
    query_ref, key_ref, value_ref, cumul_ref, scores_ref, state_ref, normed_ref, scale_ref,
    upstream_ref, weight_ref,
    grad_query_ref, grad_key_ref, grad_value_ref, gate_ref, sent_ref,
):
    query = query_ref[0].astype(F32)
    key = key_ref[0].astype(F32)
    value = value_ref[0]
    cumul = cumul_ref[...]
    rising = jnp.exp(cumul)
    falling = jnp.exp(-cumul)
    normed = normed_ref[...]
    grad_normed = jnp.dot(upstream_ref[0], weight_ref[...], preferred_element_type=F32)
    grad_output = scale_ref[...] * (
        grad_normed - normed * jnp.mean(grad_normed * normed, axis=-1, keepdims=True)
    )
    grad_output = split(grad_output, 2)
    query_scaled = split(query * rising, 2)
    key_scaled = split(key * falling, 2)
    pairs = product(grad_output, [value], 1, 1)
    pairs = split(jnp.where(lower_mask(cumul.shape[0]), pairs, 0.0), 2)
    grad_query = rising * (
        product(pairs, key_scaled, 1, 0) + product(grad_output, split(state_ref[...], 2), 1, 1)
    )
    grad_query_ref[0] = grad_query.astype(BF16)
    grad_key = falling * product(pairs, query_scaled, 0, 0)
    grad_key_ref[...] = grad_key
    grad_value_ref[...] = product(split(scores_ref[...], 2), grad_output, 0, 0)
    gate = query * grad_query - key * grad_key
    gate_ref[...] = gate
    width = query.shape[1]
    sent_ref[:width] = product(query_scaled, grad_output, 0, 0)
    sent_ref[width:] = jnp.broadcast_to(
        jnp.sum(gate, axis=0, keepdims=True), (sent_ref.shape[0] - width, width)
    )


def finish_kernel(
    key_ref, value_ref, cumul_ref, grad_key_ref, grad_value_ref, gate_ref, later_ref,
    key_out_ref, value_out_ref, decay_out_ref,
):
    key = key_ref[0].astype(F32)
    cumul = cumul_ref[...]
    width = key.shape[1]
    to_end = jnp.exp(cumul[-1:] - cumul)
    grad_in = split(later_ref[:width], 2)
    extra = to_end * product([value_ref[0]], grad_in, 1, 1)
    key_out_ref[0] = (grad_key_ref[...] + extra).astype(BF16)
    grad_value = grad_value_ref[...] + product(split(key * to_end, 2), grad_in, 1, 0)
    value_out_ref[0] = grad_value.astype(BF16)
    gate = gate_ref[...] - key * extra
    lower = lower_mask(cumul.shape[0]).astype(F32).astype(BF16)
    decay_out_ref[0] = product([lower], split(gate, 3), 0, 0) + later_ref[width:width + 1]


def local_call(kernel, shapes, *operands, name, flops, scratch=()):
    outs = [jax.ShapeDtypeStruct(shape, dtype) for shape, dtype in shapes]
    moved = sum(array.size * array.dtype.itemsize for array in [*operands, *outs])
    return pl.pallas_call(
        kernel,
        out_shape=outs,
        scratch_shapes=list(scratch),
        compiler_params=pltpu.CompilerParams(vmem_limit_bytes=VMEM_BYTES),
        cost_estimate=pl.CostEstimate(flops=flops, bytes_accessed=moved, transcendentals=0),
        name=name,
    )(*operands)


def swap(value):
    return lax.ppermute(value, "ctx", [(0, 1), (1, 0)])


def halving_plan(count, rows):
    bits = count.bit_length() - 1
    last = rows // 3 // 16 * 16
    rest = list(range(3, bits))
    return [
        (rows - last, ([0, 1, 2] + rest, [1, 0, 2] + rest)),
        (last, ([2, 0, 1] + rest, [2, 1, 0] + rest)),
    ]


def relative(place, order):
    top = len(order) - 1
    return sum(((place >> (top - step)) & 1) << bit for step, bit in enumerate(order))


def turn_kernel(count, plan, upstream_ref, state_ref, own_ref, send_ref, turned):
    del state_ref

    me, core = lax.axis_index("dp"), lax.axis_index("ctx")
    lanes = 128
    for start in range(0, turned.shape[0], lanes):
        block = upstream_ref[0, :, start:start + lanes].astype(F32)
        turned[start:start + lanes] = jnp.transpose(block)
    share = turned.shape[0] // count
    half = share // 2
    at = offset = 0
    for rows, orders in plan:
        for place in range(count):
            masks = [relative(place, order) for order in orders]
            for target, ref in ((core, own_ref), (1 - core, send_ref)):
                owner = me ^ (masks[0] + target * (masks[1] - masks[0]))
                begin = pl.multiple_of(owner * share + target * half + offset, 16)
                ref[at:at + rows] = turned[pl.ds(begin, rows)].astype(ref.dtype)
            at += rows
        offset += rows


def share_kernel(own_ref, received_ref, rounded_ref, other_ref, *outs):
    rounded = jnp.concatenate([rounded_ref[...], other_ref[...]], axis=0).astype(BF16)
    at = 0
    for out in outs:
        rows = out.shape[0]
        left = jnp.concatenate(
            [own_ref[at:at + rows], received_ref[at:at + rows].astype(BF16)], axis=1
        )
        out[...] = jnp.dot(left, rounded, preferred_element_type=F32)
        at += rows


def exchanged(value, count, bits):
    pairs = [
        (device * 2 + core, (device ^ (1 << bits[core])) * 2 + core)
        for device in range(count)
        for core in range(2)
    ]
    return lax.ppermute(value, BOTH, pairs)


def halving(chunks, plan, count, beside):
    beside = dict(beside)
    stages = len(plan[0][1][0])
    joined = 3
    for stage in range(joined):
        arrived = [
            exchanged(sent, count, [order[stage] for order in orders])
            for (_, sent), (_, orders) in zip(chunks, plan)
        ]
        if stage in beside:
            arrived[-1], beside[stage] = lax.optimization_barrier((arrived[-1], beside[stage]))
        chunks = [
            (kept[: len(kept) // 2] + new[: len(kept) // 2], kept[len(kept) // 2:] + new[len(kept) // 2:])
            if stage + 1 < stages
            else (kept + new, None)
            for (kept, _), new in zip(chunks, arrived)
        ]
    kept = [chunk[0] for chunk in chunks]
    sent = [chunk[1] for chunk in chunks]
    for stage in range(joined, stages):
        sizes = [len(part) for part in sent]
        new = exchanged(jnp.concatenate(sent), count, [stage] * 2)
        starts = [sum(sizes[:index]) for index in range(len(sizes))]
        sums = [part + new[at:at + size] for part, at, size in zip(kept, starts, sizes)]
        kept = [part[: len(part) // 2] if stage + 1 < stages else part for part in sums]
        sent = [part[len(part) // 2:] for part in sums]
    return jnp.concatenate(kept), beside


def shifted(value, axis, steps):
    count = lax.axis_size(axis)
    leading, last = (max(0, -steps), min(count, count - steps))
    return lax.ppermute(value, axis, [(source, source + steps) for source in range(leading, last)])


def body(queries, key_vectors, value_vectors, log_decay, out_weight, cotangent):
    length, width = queries.shape[1:]
    model = cotangent.shape[2]
    shards, count = lax.axis_size("ctx"), lax.axis_size("dp")
    square = (length, width)
    flops = 8 * length * width * model
    rows = model // count // 2
    paired = shards == 2 and count >= 8 and count & (count - 1) == 0 and rows % 16 == 0

    (local_state,) = local_call(
        state_kernel, [((width, width), F32)], key_vectors, value_vectors, log_decay, name="state", flops=flops // 2
    )
    state_in = shifted(local_state, "ctx", 1)
    if paired:
        plan = halving_plan(count, rows)
        own, send = local_call(
            functools.partial(turn_kernel, count, plan),
            [((rows * count, length), BF16), ((rows * count, length), F32)],
            cotangent, local_state,
            name="turn", flops=flops // 2,
            scratch=[pltpu.VMEM((model, length), F32)],
        )
        received = swap(send)
    within, scores, cumul = local_call(
        within_kernel,
        [(square, F32), ((length, length), F32), (square, F32)],
        queries, key_vectors, value_vectors, log_decay,
        name="within", flops=flops // 2,
    )
    device_decay = jnp.exp(cumul[-1])[:, None]
    for _ in range(shards - 2):
        state_in = shifted(local_state + device_decay * state_in, "ctx", 1)
    normed, scale_inv, rounded = local_call(
        normed_kernel, [(square, F32)] * 3, queries, cumul, within, state_in, name="normed", flops=flops // 4
    )
    grad_query, grad_key_zero, grad_value_zero, gate, sent = local_call(
        grads_kernel,
        [
            (queries.shape, BF16), (square, F32), (square, F32), (square, F32),
            ((width + 8, width), F32),
        ],
        queries, key_vectors, value_vectors, cumul, scores, state_in, normed, scale_inv,
        cotangent, out_weight,
        name="grads", flops=2 * flops,
    )
    later = shifted(sent, "ctx", -1)
    for _ in range(shards - 2):
        grad_in = later[:width]
        own_sum = sent[width:] - jnp.sum(grad_in * local_state, axis=-1)[None]
        later = shifted(
            jnp.concatenate([sent[:width] + device_decay * grad_in, own_sum + later[width:]]),
            "ctx",
            -1,
        )
    grad_key, grad_value, grad_decay = local_call(
        finish_kernel,
        [(queries.shape, BF16), (queries.shape, BF16), (queries.shape, F32)],
        key_vectors, value_vectors, cumul, grad_key_zero, grad_value_zero, gate, later,
        name="finish", flops=flops,
    )
    if paired:
        sizes = [count // 2 * part for part, _ in plan for _ in range(2)]
        pieces = local_call(
            share_kernel,
            [((size, width), F32) for size in sizes],
            own, received, rounded, swap(rounded),
            name="shares", flops=flops // 2,
        )
        mine, beside = halving(
            list(zip(pieces[::2], pieces[1::2])), plan, count, {0: grad_query, 1: grad_decay}
        )
        grad_query, grad_decay = beside[0], beside[1]
        theirs = swap(mine)
        first = lax.axis_index("ctx") == 0
        grad_weight = jnp.concatenate(
            [jnp.where(first, mine, theirs), jnp.where(first, theirs, mine)], axis=0
        )
    else:
        share = jnp.einsum(
            "td,tk->dk", cotangent[0], rounded.astype(BF16), preferred_element_type=F32
        )
        share = lax.psum_scatter(share, "dp", scatter_dimension=0, tiled=True)
        grad_weight = lax.psum(share, "ctx")

    return grad_query, grad_key, grad_value, grad_decay, grad_weight


def solution(mesh):
    placed = (
        P("dp", "ctx", None),
        P("dp", "ctx", None),
        P("dp", "ctx", None),
        P("dp", "ctx", None),
        P(),
        P("dp", "ctx", None),
    )
    return jax.shard_map(
        body,
        mesh=mesh,
        in_specs=placed,
        out_specs=(
            P("dp", "ctx", None),
            P("dp", "ctx", None),
            P("dp", "ctx", None),
            P("dp", "ctx", None),
            P("dp", None),
        ),
        check_vma=False,
    )
```

```python
import functools

import jax
import jax.numpy as jnp
from jax import lax
from jax.experimental import pallas as pl
from jax.experimental.pallas import tpu as pltpu
from jax.sharding import PartitionSpec as P

EPSILON = 1e-05
VMEM_BYTES = 24 * 1024 * 1024
PACK_BYTES = 58 * 1024 * 1024
F32 = jnp.float32
BF16 = jnp.bfloat16
BOTH = ("dp", "ctx")


def split(value, parts):
    pieces = []
    for index in range(parts):
        piece = value.astype(BF16)
        pieces.append(piece)
        if index + 1 < parts:
            value = value - piece.astype(F32)
    return pieces


def product(left, right, left_axis, right_axis):
    dims = (((left_axis,), (right_axis,)), ((), ()))
    most = max(len(left), len(right))
    total = None
    for order in reversed(range(most)):
        for i, l in enumerate(left):
            j = order - i
            if 0 <= j < len(right):
                term = lax.dot_general(l, right[j], dims, preferred_element_type=F32)
                total = term if total is None else total + term
    return total


def lower_mask(length):
    rows = lax.broadcasted_iota(jnp.int32, (length, length), 0)
    columns = lax.broadcasted_iota(jnp.int32, (length, length), 1)
    return rows >= columns


def cumulate(decay):
    lower = lower_mask(decay.shape[0]).astype(F32).astype(BF16)
    return product([lower], split(decay, 3), 1, 0)


def state_kernel(key_ref, value_ref, decay_ref, state_ref):
    cumul = cumulate(decay_ref[0])
    to_end = jnp.exp(cumul[-1:] - cumul)
    key_to_end = key_ref[0].astype(F32) * to_end
    state_ref[...] = product(split(key_to_end, 2), [value_ref[0]], 0, 0)


def within_kernel(query_ref, key_ref, value_ref, decay_ref, within_ref, scores_ref, cumul_ref):
    cumul = cumulate(decay_ref[0])
    cumul_ref[...] = cumul
    query_scaled = query_ref[0].astype(F32) * jnp.exp(cumul)
    key_scaled = key_ref[0].astype(F32) * jnp.exp(-cumul)
    scores = product(split(query_scaled, 2), split(key_scaled, 2), 1, 1)
    scores = jnp.where(lower_mask(cumul.shape[0]), scores, 0.0)
    scores_ref[...] = scores
    within_ref[...] = product(split(scores, 2), [value_ref[0]], 1, 0)


def normed_kernel(query_ref, cumul_ref, within_ref, state_ref, normed_ref, scale_ref, rounded_ref):
    query_scaled = query_ref[0].astype(F32) * jnp.exp(cumul_ref[...])
    output = within_ref[...] + product(split(query_scaled, 2), split(state_ref[...], 2), 1, 0)
    scale_inv = lax.rsqrt(jnp.mean(output * output, axis=-1, keepdims=True) + EPSILON)
    normed = output * scale_inv
    normed_ref[...] = normed
    scale_ref[...] = jnp.broadcast_to(scale_inv, normed.shape)
    rounded_ref[...] = normed.astype(BF16).astype(F32)


def grads_kernel(
    packed_ref, cumul_ref, scores_ref, state_ref, normed_ref, scale_ref,
    upstream_ref, weight_ref,
    grad_query_ref, grad_key_ref, grad_value_ref, gate_ref, sent_ref,
):
    query = packed_ref[0]
    key = packed_ref[1]
    value = packed_ref[2].astype(BF16)
    cumul = cumul_ref[...]
    rising = jnp.exp(cumul)
    falling = jnp.exp(-cumul)
    normed = normed_ref[...]
    grad_normed = jnp.dot(upstream_ref[0], weight_ref[...], preferred_element_type=F32)
    grad_output = scale_ref[...] * (
        grad_normed - normed * jnp.mean(grad_normed * normed, axis=-1, keepdims=True)
    )
    grad_output = split(grad_output, 2)
    query_scaled = split(query * rising, 2)
    key_scaled = split(key * falling, 2)
    pairs = product(grad_output, [value], 1, 1)
    pairs = split(jnp.where(lower_mask(cumul.shape[0]), pairs, 0.0), 2)
    grad_query = rising * (
        product(pairs, key_scaled, 1, 0) + product(grad_output, split(state_ref[...], 2), 1, 1)
    )
    grad_query_ref[0] = grad_query.astype(BF16)
    grad_key = falling * product(pairs, query_scaled, 0, 0)
    grad_key_ref[...] = grad_key
    grad_value_ref[...] = product(split(scores_ref[...], 2), grad_output, 0, 0)
    gate = query * grad_query - key * grad_key
    gate_ref[...] = gate
    width = query.shape[1]
    sent_ref[:width] = product(query_scaled, grad_output, 0, 0)
    sent_ref[width:] = jnp.broadcast_to(
        jnp.sum(gate, axis=0, keepdims=True), (sent_ref.shape[0] - width, width)
    )


def finish_kernel(
    packed_ref, cumul_ref, grad_key_ref, grad_value_ref, gate_ref, later_ref,
    key_out_ref, value_out_ref, decay_out_ref,
):
    key = packed_ref[1]
    cumul = cumul_ref[...]
    width = key.shape[1]
    to_end = jnp.exp(cumul[-1:] - cumul)
    grad_in = split(later_ref[:width], 2)
    extra = to_end * product([packed_ref[2].astype(BF16)], grad_in, 1, 1)
    key_out_ref[0] = (grad_key_ref[...] + extra).astype(BF16)
    grad_value = grad_value_ref[...] + product(split(key * to_end, 2), grad_in, 1, 0)
    value_out_ref[0] = grad_value.astype(BF16)
    gate = gate_ref[...] - key * extra
    lower = lower_mask(cumul.shape[0]).astype(F32).astype(BF16)
    decay_out_ref[0] = product([lower], split(gate, 3), 0, 0) + later_ref[width:width + 1]


def local_call(kernel, shapes, *operands, name, flops, scratch=(), space=pltpu.VMEM, limit=VMEM_BYTES):
    outs = [jax.ShapeDtypeStruct(shape, dtype) for shape, dtype in shapes]
    moved = sum(array.size * array.dtype.itemsize for array in [*operands, *outs])
    return pl.pallas_call(
        kernel,
        out_shape=outs,
        in_specs=[pl.BlockSpec(memory_space=space)] * len(operands),
        scratch_shapes=list(scratch),
        compiler_params=pltpu.CompilerParams(vmem_limit_bytes=limit),
        cost_estimate=pl.CostEstimate(flops=flops, bytes_accessed=moved, transcendentals=0),
        name=name,
    )(*operands)


def swap(value):
    return lax.ppermute(value, "ctx", [(0, 1), (1, 0)])


def halving_plan(count, rows):
    bits = count.bit_length() - 1
    last = rows // 3 // 16 * 16
    rest = list(range(3, bits))
    return [
        (rows - last, ([0, 1, 2] + rest, [1, 0, 2] + rest)),
        (last, ([2, 0, 1] + rest, [2, 1, 0] + rest)),
    ]


def relative(place, order):
    top = len(order) - 1
    return sum(((place >> (top - step)) & 1) << bit for step, bit in enumerate(order))


def pack_kernel(query_ref, key_ref, value_ref, decay_ref, packed_ref, query, key, value, semaphores):
    pairs = [
        (decay_ref.at[0], packed_ref.at[3]), (query_ref.at[0], query),
        (key_ref.at[0], key), (value_ref.at[0], value),
    ]
    copies = [
        pltpu.make_async_copy(source, target, semaphores.at[index])
        for index, (source, target) in enumerate(pairs)
    ]
    for copy in copies:
        copy.start()
    for copy in copies:
        copy.wait()
    packed_ref[0] = query[...].astype(F32)
    packed_ref[1] = key[...].astype(F32)
    packed_ref[2] = value[...].astype(F32)


def turn_kernel(count, plan, upstream_ref, own_ref, first_ref, second_ref, turned):
    me, core = lax.axis_index("dp"), lax.axis_index("ctx")
    model = turned.shape[0]
    lanes = 128
    for start in range(0, model, lanes):
        turned[start:start + lanes] = jnp.transpose(upstream_ref[0, :, start:start + lanes].astype(F32))
    share = model // count
    half = share // 2
    at = 0
    for ref, places in ((first_ref, range(count // 2, count)), (second_ref, range(count // 2))):
        offset = sent = 0
        for rows, orders in plan:
            for place in places:
                masks = [relative(place, order) for order in orders]
                mine = me ^ (masks[0] + core * (masks[1] - masks[0]))
                other = me ^ (masks[1] + core * (masks[0] - masks[1]))
                begin = pl.multiple_of(mine * share + core * half + offset, 16)
                own_ref[at:at + rows] = turned[pl.ds(begin, rows)].astype(BF16)
                begin = pl.multiple_of(other * share + (1 - core) * half + offset, 16)
                ref[sent:sent + rows] = turned[pl.ds(begin, rows)]
                at += rows
                sent += rows
            offset += rows


def joint_kernel(
    own_ref, other_ref,
    cumul_ref, scores_ref, state_ref, normed_ref, scale_ref, rounded_ref,
):
    first = lax.axis_index("ctx") == 0
    length = cumul_ref.shape[0]
    lower = lower_mask(length)

    def scaled(block):
        query, key, value, decay = block
        cumul = cumulate(decay)
        query_scaled = split(query * jnp.exp(cumul), 2)
        key_scaled = split(key * jnp.exp(-cumul), 2)
        return cumul, query_scaled, key_scaled, value.astype(BF16)

    def within(query_scaled, key_scaled, value):
        scores = jnp.where(lower, product(query_scaled, key_scaled, 1, 1), 0.0)
        return scores, product(split(scores, 2), [value], 1, 0)

    def normalized(output):
        scale_inv = lax.rsqrt(jnp.mean(output * output, axis=-1, keepdims=True) + EPSILON)
        normed = output * scale_inv
        return normed, jnp.broadcast_to(scale_inv, normed.shape), normed.astype(BF16)

    early = [jnp.where(first, own_ref[i], other_ref[i]) for i in range(4)]
    late = [jnp.where(first, other_ref[i], own_ref[i]) for i in range(4)]
    cumul_early, queries_early, keys_early, values_early = scaled(early)
    cumul_late, queries_late, keys_late, values_late = scaled(late)
    to_end = jnp.exp(cumul_early[-1:] - cumul_early)
    state = product(split(early[1] * to_end, 2), [values_early], 0, 0)
    scores_early, output_early = within(queries_early, keys_early, values_early)
    scores_late, output_late = within(queries_late, keys_late, values_late)
    output_late += product(queries_late, split(state, 2), 1, 0)
    done_early = normalized(output_early)
    done_late = normalized(output_late)
    cumul_ref[...] = jnp.where(first, cumul_early, cumul_late)
    scores_ref[...] = jnp.where(first, scores_early, scores_late)
    state_ref[...] = jnp.where(first, 0.0, state)
    normed_ref[...] = jnp.where(first, done_early[0], done_late[0])
    scale_ref[...] = jnp.where(first, done_early[1], done_late[1])
    rounded_ref[:length] = jnp.where(first, done_early[2], done_late[2])
    rounded_ref[length:] = jnp.where(first, done_late[2], done_early[2])


def share_kernel(begin, own_ref, received_ref, rounded_ref, *outs):
    at = 0
    for out in outs:
        rows = out.shape[0]
        left = jnp.concatenate(
            [own_ref[begin + at:begin + at + rows], received_ref[at:at + rows].astype(BF16)], axis=1
        )
        out[...] = jnp.dot(left, rounded_ref[...], preferred_element_type=F32)
        at += rows


def exchanged(value, count, bits):
    pairs = [
        (device * 2 + core, (device ^ (1 << bits[core])) * 2 + core)
        for device in range(count)
        for core in range(2)
    ]
    return lax.ppermute(value, BOTH, pairs)


def halving(kept, sent, plan, count, beside):
    stages = len(plan[0][1][0])
    joined = 3
    for stage in range(joined):
        arrived = [
            exchanged(part, count, [order[stage] for order in orders])
            for part, (_, orders) in zip(sent, plan)
        ]
        if stage in beside:
            arrived = beside[stage](arrived)
        half = [len(part) // 2 if stage + 1 < stages else len(part) for part in kept]
        sums = [
            (old[:size] + new[:size], old[size:] + new[size:])
            for old, new, size in zip(kept, arrived, half)
        ]
        kept = [pair[0] for pair in sums]
        sent = [pair[1] for pair in sums]
    for stage in range(joined, stages):
        sizes = [len(part) for part in sent]
        new = exchanged(jnp.concatenate(sent), count, [stage] * 2)
        starts = [sum(sizes[:index]) for index in range(len(sizes))]
        sums = [part + new[at:at + size] for part, at, size in zip(kept, starts, sizes)]
        kept = [part[: len(part) // 2] if stage + 1 < stages else part for part in sums]
        sent = [part[len(part) // 2:] for part in sums]
    return jnp.concatenate(kept)


def shifted(value, axis, steps):
    count = lax.axis_size(axis)
    leading, last = (max(0, -steps), min(count, count - steps))
    return lax.ppermute(value, axis, [(source, source + steps) for source in range(leading, last)])


def body(queries, key_vectors, value_vectors, log_decay, out_weight, cotangent):
    length, width = queries.shape[1:]
    model = cotangent.shape[2]
    shards, count = lax.axis_size("ctx"), lax.axis_size("dp")
    square = (length, width)
    rows = model // count // 2
    flops = 8 * length * width * model
    paired = shards == 2 and count >= 8 and count & (count - 1) == 0 and rows % 16 == 0

    (packed,) = local_call(
        pack_kernel,
        [((4, length, width), F32)],
        queries, key_vectors, value_vectors, log_decay,
        name="pack", flops=20 * flops, space=pltpu.HBM, limit=PACK_BYTES,
        scratch=[pltpu.VMEM(square, BF16)] * 3 + [pltpu.SemaphoreType.DMA((4,))],
    )
    if paired:
        plan = halving_plan(count, rows)
        part_rows = rows * count // 2
        own, send_first, send_second = local_call(
            functools.partial(turn_kernel, count, plan),
            [((2 * part_rows, length), BF16), ((part_rows, length), F32), ((part_rows, length), F32)],
            cotangent,
            name="turn", flops=20 * flops,
            scratch=[pltpu.VMEM((model, length), F32)],
        )
        others = swap(packed)
        received_first = swap(send_first)
        received_second = swap(send_second)
        cumul, scores, state_in, normed, scale_inv, rounded = local_call(
            joint_kernel,
            [
                (square, F32), ((length, length), F32), ((width, width), F32), (square, F32),
                (square, F32), ((2 * length, width), BF16),
            ],
            packed, others,
            name="joint", flops=40 * flops,
        )
        sent = local_call(
            functools.partial(share_kernel, 0),
            [((count // 2 * part, width), F32) for part, _ in plan],
            own, received_first, rounded,
            name="sent_shares", flops=flops // 4,
        )
        kept = local_call(
            functools.partial(share_kernel, part_rows),
            [((count // 2 * part, width), F32) for part, _ in plan],
            own, received_second, rounded,
            name="kept_shares", flops=flops // 4,
        )
    else:
        (local_state,) = local_call(
            state_kernel, [((width, width), F32)], key_vectors, value_vectors, log_decay,
            name="state", flops=flops // 2,
        )
        state_in = shifted(local_state, "ctx", 1)
        within, scores, cumul = local_call(
            within_kernel,
            [(square, F32), ((length, length), F32), (square, F32)],
            queries, key_vectors, value_vectors, log_decay,
            name="within", flops=flops // 2,
        )
        device_decay = jnp.exp(cumul[-1])[:, None]
        for _ in range(shards - 2):
            state_in = shifted(local_state + device_decay * state_in, "ctx", 1)
        normed, scale_inv, rounded = local_call(
            normed_kernel, [(square, F32)] * 3, queries, cumul, within, state_in,
            name="normed", flops=flops // 4,
        )

    grad_query, grad_key_zero, grad_value_zero, gate, grad_sent = local_call(
        grads_kernel,
        [
            (queries.shape, BF16), (square, F32), (square, F32), (square, F32),
            ((width + 8, width), F32),
        ],
        packed, cumul, scores, state_in, normed, scale_inv,
        cotangent, out_weight,
        name="grads", flops=2 * flops,
    )
    later = shifted(grad_sent, "ctx", -1)

    def finish(later):
        return local_call(
            finish_kernel,
            [(queries.shape, BF16), (queries.shape, BF16), (queries.shape, F32)],
            packed, cumul, grad_key_zero, grad_value_zero, gate, later,
            name="finish", flops=flops,
        )

    if paired:
        held = {}

        def beside_first(arrived):
            large, small = arrived
            small, held["query"] = lax.optimization_barrier((small, grad_query))
            large, held["later"] = lax.optimization_barrier((large, later))
            return [large, small]

        def beside_second(arrived):
            large, small = arrived
            key, value, decay = finish(held["later"])
            large, decay = lax.optimization_barrier((large, decay))
            held["finished"] = key, value, decay
            return [large, small]

        mine = halving(kept=kept, sent=sent, plan=plan, count=count, beside={0: beside_first, 1: beside_second})
        grad_query = held["query"]
        grad_key, grad_value, grad_decay = held["finished"]
        theirs = swap(mine)
        first = lax.axis_index("ctx") == 0
        grad_weight = jnp.concatenate(
            [jnp.where(first, mine, theirs), jnp.where(first, theirs, mine)], axis=0
        )
    else:
        for _ in range(shards - 2):
            grad_in = later[:width]
            own_sum = grad_sent[width:] - jnp.sum(grad_in * local_state, axis=-1)[None]
            later = shifted(
                jnp.concatenate([grad_sent[:width] + device_decay * grad_in, own_sum + later[width:]]),
                "ctx",
                -1,
            )
        grad_key, grad_value, grad_decay = finish(later)
        share = jnp.einsum(
            "td,tk->dk", cotangent[0], rounded.astype(BF16), preferred_element_type=F32
        )
        share = lax.psum_scatter(share, "dp", scatter_dimension=0, tiled=True)
        grad_weight = lax.psum(share, "ctx")

    return grad_query, grad_key, grad_value, grad_decay, grad_weight


def solution(mesh):
    placed = (
        P("dp", "ctx", None),
        P("dp", "ctx", None),
        P("dp", "ctx", None),
        P("dp", "ctx", None),
        P(),
        P("dp", "ctx", None),
    )
    return jax.shard_map(
        body,
        mesh=mesh,
        in_specs=placed,
        out_specs=(
            P("dp", "ctx", None),
            P("dp", "ctx", None),
            P("dp", "ctx", None),
            P("dp", "ctx", None),
            P("dp", None),
        ),
        check_vma=False,
    )
```

```python
import functools

import jax
import jax.numpy as jnp
from jax import lax
from jax.experimental import pallas as pl
from jax.experimental.pallas import tpu as pltpu
from jax.sharding import PartitionSpec as P

EPSILON = 1e-05
VMEM_BYTES = 24 * 1024 * 1024
PACK_BYTES = 58 * 1024 * 1024
F32 = jnp.float32
BF16 = jnp.bfloat16
BOTH = ("dp", "ctx")


def split(value, parts):
    pieces = []
    for index in range(parts):
        piece = value.astype(BF16)
        pieces.append(piece)
        if index + 1 < parts:
            value = value - piece.astype(F32)
    return pieces


def product(left, right, left_axis, right_axis):
    dims = (((left_axis,), (right_axis,)), ((), ()))
    most = max(len(left), len(right))
    total = None
    for order in reversed(range(most)):
        for i, l in enumerate(left):
            j = order - i
            if 0 <= j < len(right):
                term = lax.dot_general(l, right[j], dims, preferred_element_type=F32)
                total = term if total is None else total + term
    return total


def lower_mask(length):
    rows = lax.broadcasted_iota(jnp.int32, (length, length), 0)
    columns = lax.broadcasted_iota(jnp.int32, (length, length), 1)
    return rows >= columns


def cumulate(decay):
    lower = lower_mask(decay.shape[0]).astype(F32).astype(BF16)
    return product([lower], split(decay, 3), 1, 0)


def state_kernel(key_ref, value_ref, decay_ref, state_ref):
    cumul = cumulate(decay_ref[0])
    to_end = jnp.exp(cumul[-1:] - cumul)
    key_to_end = key_ref[0].astype(F32) * to_end
    state_ref[...] = product(split(key_to_end, 2), [value_ref[0]], 0, 0)


def within_kernel(query_ref, key_ref, value_ref, decay_ref, within_ref, scores_ref, cumul_ref):
    cumul = cumulate(decay_ref[0])
    cumul_ref[...] = cumul
    query_scaled = query_ref[0].astype(F32) * jnp.exp(cumul)
    key_scaled = key_ref[0].astype(F32) * jnp.exp(-cumul)
    scores = product(split(query_scaled, 2), split(key_scaled, 2), 1, 1)
    scores = jnp.where(lower_mask(cumul.shape[0]), scores, 0.0)
    scores_ref[...] = scores
    within_ref[...] = product(split(scores, 2), [value_ref[0]], 1, 0)


def normed_kernel(query_ref, cumul_ref, within_ref, state_ref, normed_ref, scale_ref, rounded_ref):
    query_scaled = query_ref[0].astype(F32) * jnp.exp(cumul_ref[...])
    output = within_ref[...] + product(split(query_scaled, 2), split(state_ref[...], 2), 1, 0)
    scale_inv = lax.rsqrt(jnp.mean(output * output, axis=-1, keepdims=True) + EPSILON)
    normed = output * scale_inv
    normed_ref[...] = normed
    scale_ref[...] = jnp.broadcast_to(scale_inv, normed.shape)
    rounded_ref[...] = normed.astype(BF16).astype(F32)


def grads_kernel(
    packed_ref, cumul_ref, scores_ref, state_ref, normed_ref, scale_ref,
    upstream_ref, weight_ref,
    grad_query_ref, grad_key_ref, grad_value_ref, gate_ref, sent_ref,
):
    query = packed_ref[0]
    key = packed_ref[1]
    value = packed_ref[2].astype(BF16)
    cumul = cumul_ref[...]
    rising = jnp.exp(cumul)
    falling = jnp.exp(-cumul)
    normed = normed_ref[...]
    grad_normed = jnp.dot(upstream_ref[0], weight_ref[...], preferred_element_type=F32)
    grad_output = scale_ref[...] * (
        grad_normed - normed * jnp.mean(grad_normed * normed, axis=-1, keepdims=True)
    )
    grad_output = split(grad_output, 2)
    query_scaled = split(query * rising, 2)
    key_scaled = split(key * falling, 2)
    pairs = product(grad_output, [value], 1, 1)
    pairs = split(jnp.where(lower_mask(cumul.shape[0]), pairs, 0.0), 2)
    grad_query = rising * (
        product(pairs, key_scaled, 1, 0) + product(grad_output, split(state_ref[...], 2), 1, 1)
    )
    grad_query_ref[0] = grad_query.astype(BF16)
    grad_key = falling * product(pairs, query_scaled, 0, 0)
    grad_key_ref[...] = grad_key
    grad_value_ref[...] = product(split(scores_ref[...], 2), grad_output, 0, 0)
    gate = query * grad_query - key * grad_key
    gate_ref[...] = gate
    width = query.shape[1]
    sent_ref[:width] = product(query_scaled, grad_output, 0, 0)
    sent_ref[width:] = jnp.broadcast_to(
        jnp.sum(gate, axis=0, keepdims=True), (sent_ref.shape[0] - width, width)
    )


def finish_kernel(
    packed_ref, cumul_ref, grad_key_ref, grad_value_ref, gate_ref, later_ref,
    key_out_ref, value_out_ref, decay_out_ref,
):
    key = packed_ref[1]
    cumul = cumul_ref[...]
    width = key.shape[1]
    to_end = jnp.exp(cumul[-1:] - cumul)
    grad_in = split(later_ref[:width], 2)
    extra = to_end * product([packed_ref[2].astype(BF16)], grad_in, 1, 1)
    key_out_ref[0] = (grad_key_ref[...] + extra).astype(BF16)
    grad_value = grad_value_ref[...] + product(split(key * to_end, 2), grad_in, 1, 0)
    value_out_ref[0] = grad_value.astype(BF16)
    gate = gate_ref[...] - key * extra
    lower = lower_mask(cumul.shape[0]).astype(F32).astype(BF16)
    decay_out_ref[0] = product([lower], split(gate, 3), 0, 0) + later_ref[width:width + 1]


def local_call(kernel, shapes, *operands, name, flops, scratch=(), space=pltpu.VMEM, limit=VMEM_BYTES):
    outs = [jax.ShapeDtypeStruct(shape, dtype) for shape, dtype in shapes]
    moved = sum(array.size * array.dtype.itemsize for array in [*operands, *outs])
    return pl.pallas_call(
        kernel,
        out_shape=outs,
        in_specs=[pl.BlockSpec(memory_space=space)] * len(operands),
        scratch_shapes=list(scratch),
        compiler_params=pltpu.CompilerParams(vmem_limit_bytes=limit),
        cost_estimate=pl.CostEstimate(flops=flops, bytes_accessed=moved, transcendentals=0),
        name=name,
    )(*operands)


def swap(value):
    return lax.ppermute(value, "ctx", [(0, 1), (1, 0)])


def halving_plan(count, rows):
    bits = count.bit_length() - 1
    last = rows // 32 * 16
    rest = list(range(3, bits))
    return [
        (rows - last, ([0, 1, 2] + rest, [1, 0, 2] + rest)),
        (last, ([1, 2, 0] + rest, [2, 0, 1] + rest)),
    ]


def relative(place, order):
    top = len(order) - 1
    return sum(((place >> (top - step)) & 1) << bit for step, bit in enumerate(order))


def pack_kernel(query_ref, key_ref, value_ref, decay_ref, packed_ref, query, key, value, semaphores):
    pairs = [
        (decay_ref.at[0], packed_ref.at[3]), (query_ref.at[0], query),
        (key_ref.at[0], key), (value_ref.at[0], value),
    ]
    copies = [
        pltpu.make_async_copy(source, target, semaphores.at[index])
        for index, (source, target) in enumerate(pairs)
    ]
    for copy in copies:
        copy.start()
    for copy in copies:
        copy.wait()
    packed_ref[0] = query[...].astype(F32)
    packed_ref[1] = key[...].astype(F32)
    packed_ref[2] = value[...].astype(F32)


def turn_kernel(count, plan, upstream_ref, own_ref, first_ref, second_ref, turned):
    me, core = lax.axis_index("dp"), lax.axis_index("ctx")
    model = turned.shape[0]
    lanes = 128
    for start in range(0, model, lanes):
        turned[start:start + lanes] = jnp.transpose(upstream_ref[0, :, start:start + lanes].astype(F32))
    share = model // count
    half = share // 2
    at = 0
    for ref, places in ((first_ref, range(count // 2, count)), (second_ref, range(count // 2))):
        offset = sent = 0
        for rows, orders in plan:
            for place in places:
                masks = [relative(place, order) for order in orders]
                mine = me ^ (masks[0] + core * (masks[1] - masks[0]))
                other = me ^ (masks[1] + core * (masks[0] - masks[1]))
                begin = pl.multiple_of(mine * share + core * half + offset, 16)
                own_ref[at:at + rows] = turned[pl.ds(begin, rows)].astype(BF16)
                begin = pl.multiple_of(other * share + (1 - core) * half + offset, 16)
                ref[sent:sent + rows] = turned[pl.ds(begin, rows)]
                at += rows
                sent += rows
            offset += rows


def joint_kernel(
    own_ref, other_ref,
    cumul_ref, scores_ref, state_ref, normed_ref, scale_ref, rounded_ref,
):
    first = lax.axis_index("ctx") == 0
    length = cumul_ref.shape[0]
    lower = lower_mask(length)

    def scaled(block):
        query, key, value, decay = block
        cumul = cumulate(decay)
        query_scaled = split(query * jnp.exp(cumul), 2)
        key_scaled = split(key * jnp.exp(-cumul), 2)
        return cumul, query_scaled, key_scaled, value.astype(BF16)

    def within(query_scaled, key_scaled, value):
        scores = jnp.where(lower, product(query_scaled, key_scaled, 1, 1), 0.0)
        return scores, product(split(scores, 2), [value], 1, 0)

    def normalized(output):
        scale_inv = lax.rsqrt(jnp.mean(output * output, axis=-1, keepdims=True) + EPSILON)
        normed = output * scale_inv
        return normed, jnp.broadcast_to(scale_inv, normed.shape), normed.astype(BF16)

    early = [jnp.where(first, own_ref[i], other_ref[i]) for i in range(4)]
    late = [jnp.where(first, other_ref[i], own_ref[i]) for i in range(4)]
    cumul_early, queries_early, keys_early, values_early = scaled(early)
    cumul_late, queries_late, keys_late, values_late = scaled(late)
    to_end = jnp.exp(cumul_early[-1:] - cumul_early)
    state = product(split(early[1] * to_end, 2), [values_early], 0, 0)
    scores_early, output_early = within(queries_early, keys_early, values_early)
    scores_late, output_late = within(queries_late, keys_late, values_late)
    output_late += product(queries_late, split(state, 2), 1, 0)
    done_early = normalized(output_early)
    done_late = normalized(output_late)
    cumul_ref[...] = jnp.where(first, cumul_early, cumul_late)
    scores_ref[...] = jnp.where(first, scores_early, scores_late)
    state_ref[...] = jnp.where(first, 0.0, state)
    normed_ref[...] = jnp.where(first, done_early[0], done_late[0])
    scale_ref[...] = jnp.where(first, done_early[1], done_late[1])
    rounded_ref[:length] = jnp.where(first, done_early[2], done_late[2])
    rounded_ref[length:] = jnp.where(first, done_late[2], done_early[2])


def share_kernel(begin, own_ref, received_ref, rounded_ref, *outs):
    at = 0
    for out in outs:
        rows = out.shape[0]
        left = jnp.concatenate(
            [own_ref[begin + at:begin + at + rows], received_ref[at:at + rows].astype(BF16)], axis=1
        )
        out[...] = jnp.dot(left, rounded_ref[...], preferred_element_type=F32)
        at += rows


def exchanged(value, count, bits):
    pairs = [
        (device * 2 + core, (device ^ (1 << bits[core])) * 2 + core)
        for device in range(count)
        for core in range(2)
    ]
    return lax.ppermute(value, BOTH, pairs)


def halving(kept, sent, plan, count, beside):
    stages = len(plan[0][1][0])
    joined = 3
    for stage in range(joined):
        arrived = [
            exchanged(part, count, [order[stage] for order in orders])
            for part, (_, orders) in zip(sent, plan)
        ]
        if stage in beside:
            arrived = beside[stage](arrived)
        half = [len(part) // 2 if stage + 1 < stages else len(part) for part in kept]
        sums = [
            (old[:size] + new[:size], old[size:] + new[size:])
            for old, new, size in zip(kept, arrived, half)
        ]
        kept = [pair[0] for pair in sums]
        sent = [pair[1] for pair in sums]
    for stage in range(joined, stages):
        sizes = [len(part) for part in sent]
        new = exchanged(jnp.concatenate(sent), count, [stage] * 2)
        if stage in beside:
            new = beside[stage](new)
        starts = [sum(sizes[:index]) for index in range(len(sizes))]
        sums = [part + new[at:at + size] for part, at, size in zip(kept, starts, sizes)]
        kept = [part[: len(part) // 2] if stage + 1 < stages else part for part in sums]
        sent = [part[len(part) // 2:] for part in sums]
    return jnp.concatenate(kept)


def shifted(value, axis, steps):
    count = lax.axis_size(axis)
    leading, last = (max(0, -steps), min(count, count - steps))
    return lax.ppermute(value, axis, [(source, source + steps) for source in range(leading, last)])


def body(queries, key_vectors, value_vectors, log_decay, out_weight, cotangent):
    length, width = queries.shape[1:]
    model = cotangent.shape[2]
    shards, count = lax.axis_size("ctx"), lax.axis_size("dp")
    square = (length, width)
    rows = model // count // 2
    flops = 8 * length * width * model
    paired = shards == 2 and count >= 16 and count & (count - 1) == 0 and rows % 16 == 0

    (packed,) = local_call(
        pack_kernel,
        [((4, length, width), F32)],
        queries, key_vectors, value_vectors, log_decay,
        name="pack", flops=20 * flops, space=pltpu.HBM, limit=PACK_BYTES,
        scratch=[pltpu.VMEM(square, BF16)] * 3 + [pltpu.SemaphoreType.DMA((4,))],
    )
    if paired:
        plan = halving_plan(count, rows)
        part_rows = rows * count // 2
        own, send_first, send_second = local_call(
            functools.partial(turn_kernel, count, plan),
            [((2 * part_rows, length), BF16), ((part_rows, length), F32), ((part_rows, length), F32)],
            cotangent,
            name="turn", flops=20 * flops,
            scratch=[pltpu.VMEM((model, length), F32)],
        )
        others = swap(packed)
        received_first = swap(send_first)
        received_second = swap(send_second)
        cumul, scores, state_in, normed, scale_inv, rounded = local_call(
            joint_kernel,
            [
                (square, F32), ((length, length), F32), ((width, width), F32), (square, F32),
                (square, F32), ((2 * length, width), BF16),
            ],
            packed, others,
            name="joint", flops=40 * flops,
        )
        sent = local_call(
            functools.partial(share_kernel, 0),
            [((count // 2 * part, width), F32) for part, _ in plan],
            own, received_first, rounded,
            name="sent_shares", flops=flops // 4,
        )
        kept = local_call(
            functools.partial(share_kernel, part_rows),
            [((count // 2 * part, width), F32) for part, _ in plan],
            own, received_second, rounded,
            name="kept_shares", flops=flops // 4,
        )
    else:
        (local_state,) = local_call(
            state_kernel, [((width, width), F32)], key_vectors, value_vectors, log_decay,
            name="state", flops=flops // 2,
        )
        state_in = shifted(local_state, "ctx", 1)
        within, scores, cumul = local_call(
            within_kernel,
            [(square, F32), ((length, length), F32), (square, F32)],
            queries, key_vectors, value_vectors, log_decay,
            name="within", flops=flops // 2,
        )
        device_decay = jnp.exp(cumul[-1])[:, None]
        for _ in range(shards - 2):
            state_in = shifted(local_state + device_decay * state_in, "ctx", 1)
        normed, scale_inv, rounded = local_call(
            normed_kernel, [(square, F32)] * 3, queries, cumul, within, state_in,
            name="normed", flops=flops // 4,
        )

    grad_query, grad_key_zero, grad_value_zero, gate, grad_sent = local_call(
        grads_kernel,
        [
            (queries.shape, BF16), (square, F32), (square, F32), (square, F32),
            ((width + 8, width), F32),
        ],
        packed, cumul, scores, state_in, normed, scale_inv,
        cotangent, out_weight,
        name="grads", flops=2 * flops,
    )
    later = shifted(grad_sent, "ctx", -1)

    def finish(later):
        return local_call(
            finish_kernel,
            [(queries.shape, BF16), (queries.shape, BF16), (queries.shape, F32)],
            packed, cumul, grad_key_zero, grad_value_zero, gate, later,
            name="finish", flops=flops,
        )

    if paired:
        held = {}

        def beside_first(arrived):
            large, small = arrived
            small, held["query"] = lax.optimization_barrier((small, grad_query))
            return [large, small]

        def beside_third(arrived):
            large, small = arrived
            large, held["later"] = lax.optimization_barrier((large, later))
            return [large, small]

        def beside_last(arrived):
            key, value, decay = finish(held["later"])
            arrived, decay = lax.optimization_barrier((arrived, decay))
            held["finished"] = key, value, decay
            return arrived

        beside = {0: beside_first, 2: beside_third, 3: beside_last}
        mine = halving(kept, sent, plan, count, beside)
        grad_query = held["query"]
        grad_key, grad_value, grad_decay = held["finished"]
        theirs = swap(mine)
        first = lax.axis_index("ctx") == 0
        grad_weight = jnp.concatenate(
            [jnp.where(first, mine, theirs), jnp.where(first, theirs, mine)], axis=0
        )
    else:
        for _ in range(shards - 2):
            grad_in = later[:width]
            own_sum = grad_sent[width:] - jnp.sum(grad_in * local_state, axis=-1)[None]
            later = shifted(
                jnp.concatenate([grad_sent[:width] + device_decay * grad_in, own_sum + later[width:]]),
                "ctx",
                -1,
            )
        grad_key, grad_value, grad_decay = finish(later)
        share = jnp.einsum(
            "td,tk->dk", cotangent[0], rounded.astype(BF16), preferred_element_type=F32
        )
        share = lax.psum_scatter(share, "dp", scatter_dimension=0, tiled=True)
        grad_weight = lax.psum(share, "ctx")

    return grad_query, grad_key, grad_value, grad_decay, grad_weight


def solution(mesh):
    placed = (
        P("dp", "ctx", None),
        P("dp", "ctx", None),
        P("dp", "ctx", None),
        P("dp", "ctx", None),
        P(),
        P("dp", "ctx", None),
    )
    return jax.shard_map(
        body,
        mesh=mesh,
        in_specs=placed,
        out_specs=(
            P("dp", "ctx", None),
            P("dp", "ctx", None),
            P("dp", "ctx", None),
            P("dp", "ctx", None),
            P("dp", None),
        ),
        check_vma=False,
    )
```

```python
import functools

import jax
import jax.numpy as jnp
from jax import lax
from jax.experimental import pallas as pl
from jax.experimental.pallas import tpu as pltpu
from jax.sharding import PartitionSpec as P

EPSILON = 1e-05
VMEM_BYTES = 24 * 1024 * 1024
PACK_BYTES = 58 * 1024 * 1024
F32 = jnp.float32
BF16 = jnp.bfloat16
BOTH = ("dp", "ctx")


def split(value, parts):
    pieces = []
    for index in range(parts):
        piece = value.astype(BF16)
        pieces.append(piece)
        if index + 1 < parts:
            value = value - piece.astype(F32)
    return pieces


def product(left, right, left_axis, right_axis):
    dims = (((left_axis,), (right_axis,)), ((), ()))
    most = max(len(left), len(right))
    total = None
    for order in reversed(range(most)):
        for i, l in enumerate(left):
            j = order - i
            if 0 <= j < len(right):
                term = lax.dot_general(l, right[j], dims, preferred_element_type=F32)
                total = term if total is None else total + term
    return total


def lower_mask(length):
    rows = lax.broadcasted_iota(jnp.int32, (length, length), 0)
    columns = lax.broadcasted_iota(jnp.int32, (length, length), 1)
    return rows >= columns


def cumulate(decay):
    lower = lower_mask(decay.shape[0]).astype(F32).astype(BF16)
    return product([lower], split(decay, 3), 1, 0)


def state_kernel(key_ref, value_ref, decay_ref, state_ref):
    cumul = cumulate(decay_ref[0])
    to_end = jnp.exp(cumul[-1:] - cumul)
    key_to_end = key_ref[0].astype(F32) * to_end
    state_ref[...] = product(split(key_to_end, 2), [value_ref[0]], 0, 0)


def within_kernel(query_ref, key_ref, value_ref, decay_ref, within_ref, scores_ref, cumul_ref):
    cumul = cumulate(decay_ref[0])
    cumul_ref[...] = cumul
    query_scaled = query_ref[0].astype(F32) * jnp.exp(cumul)
    key_scaled = key_ref[0].astype(F32) * jnp.exp(-cumul)
    scores = product(split(query_scaled, 2), split(key_scaled, 2), 1, 1)
    scores = jnp.where(lower_mask(cumul.shape[0]), scores, 0.0)
    scores_ref[...] = scores
    within_ref[...] = product(split(scores, 2), [value_ref[0]], 1, 0)


def normed_kernel(query_ref, cumul_ref, within_ref, state_ref, normed_ref, scale_ref, rounded_ref):
    query_scaled = query_ref[0].astype(F32) * jnp.exp(cumul_ref[...])
    output = within_ref[...] + product(split(query_scaled, 2), split(state_ref[...], 2), 1, 0)
    scale_inv = lax.rsqrt(jnp.mean(output * output, axis=-1, keepdims=True) + EPSILON)
    normed = output * scale_inv
    normed_ref[...] = normed
    scale_ref[...] = jnp.broadcast_to(scale_inv, normed.shape)
    rounded_ref[...] = normed.astype(BF16).astype(F32)


def grads_kernel(
    packed_ref, cumul_ref, scores_ref, state_ref, normed_ref, scale_ref,
    upstream_ref, weight_ref,
    grad_query_ref, grad_key_ref, grad_value_ref, gate_ref, sent_ref,
):
    query = packed_ref[0]
    key = packed_ref[1]
    value = packed_ref[2].astype(BF16)
    cumul = cumul_ref[...]
    rising = jnp.exp(cumul)
    falling = jnp.exp(-cumul)
    normed = normed_ref[...]
    grad_normed = jnp.dot(upstream_ref[0], weight_ref[...], preferred_element_type=F32)
    grad_output = scale_ref[...] * (
        grad_normed - normed * jnp.mean(grad_normed * normed, axis=-1, keepdims=True)
    )
    grad_output = split(grad_output, 2)
    query_scaled = split(query * rising, 2)
    key_scaled = split(key * falling, 2)
    pairs = product(grad_output, [value], 1, 1)
    pairs = split(jnp.where(lower_mask(cumul.shape[0]), pairs, 0.0), 2)
    grad_query = rising * (
        product(pairs, key_scaled, 1, 0) + product(grad_output, split(state_ref[...], 2), 1, 1)
    )
    grad_query_ref[0] = grad_query.astype(BF16)
    grad_key = falling * product(pairs, query_scaled, 0, 0)
    grad_key_ref[...] = grad_key
    grad_value_ref[...] = product(split(scores_ref[...], 2), grad_output, 0, 0)
    gate = query * grad_query - key * grad_key
    gate_ref[...] = gate
    width = query.shape[1]
    sent_ref[:width] = product(query_scaled, grad_output, 0, 0)
    sent_ref[width:] = jnp.broadcast_to(
        jnp.sum(gate, axis=0, keepdims=True), (sent_ref.shape[0] - width, width)
    )


def finish_kernel(
    packed_ref, cumul_ref, grad_key_ref, grad_value_ref, gate_ref, later_ref,
    key_out_ref, value_out_ref, decay_out_ref,
):
    key = packed_ref[1]
    cumul = cumul_ref[...]
    width = key.shape[1]
    to_end = jnp.exp(cumul[-1:] - cumul)
    last = lax.axis_index("ctx") == lax.axis_size("ctx") - 1
    later = jnp.where(last, 0.0, later_ref[...])
    grad_in = split(later[:width], 2)
    extra = to_end * product([packed_ref[2].astype(BF16)], grad_in, 1, 1)
    key_out_ref[0] = (grad_key_ref[...] + extra).astype(BF16)
    grad_value = grad_value_ref[...] + product(split(key * to_end, 2), grad_in, 1, 0)
    value_out_ref[0] = grad_value.astype(BF16)
    gate = gate_ref[...] - key * extra
    lower = lower_mask(cumul.shape[0]).astype(F32).astype(BF16)
    decay_out_ref[0] = product([lower], split(gate, 3), 0, 0) + later[width:width + 1]


def local_call(kernel, shapes, *operands, name, flops, scratch=(), space=pltpu.VMEM, limit=VMEM_BYTES):
    outs = [jax.ShapeDtypeStruct(shape, dtype) for shape, dtype in shapes]
    moved = sum(array.size * array.dtype.itemsize for array in [*operands, *outs])
    return pl.pallas_call(
        kernel,
        out_shape=outs,
        in_specs=[pl.BlockSpec(memory_space=space)] * len(operands),
        scratch_shapes=list(scratch),
        compiler_params=pltpu.CompilerParams(vmem_limit_bytes=limit),
        cost_estimate=pl.CostEstimate(flops=flops, bytes_accessed=moved, transcendentals=0),
        name=name,
    )(*operands)


def swap(value):
    return lax.ppermute(value, "ctx", [(0, 1), (1, 0)])


def halving_plan(count, rows):
    bits = count.bit_length() - 1
    last = rows // 32 * 16
    rest = list(range(3, bits))
    return [
        (rows - last, ([0, 1, 2] + rest, [1, 0, 2] + rest)),
        (last, ([2, 0, 1] + rest, [1, 2, 0] + rest)),
    ]


def relative(place, order):
    top = len(order) - 1
    return sum(((place >> (top - step)) & 1) << bit for step, bit in enumerate(order))


def pack_kernel(query_ref, key_ref, value_ref, decay_ref, packed_ref, query, key, value, semaphores):
    pairs = [
        (decay_ref.at[0], packed_ref.at[3]), (query_ref.at[0], query),
        (key_ref.at[0], key), (value_ref.at[0], value),
    ]
    copies = [
        pltpu.make_async_copy(source, target, semaphores.at[index])
        for index, (source, target) in enumerate(pairs)
    ]
    for copy in copies:
        copy.start()
    for copy in copies:
        copy.wait()
    packed_ref[0] = query[...].astype(F32)
    packed_ref[1] = key[...].astype(F32)
    packed_ref[2] = value[...].astype(F32)


def turn_kernel(count, plan, upstream_ref, own_ref, first_ref, second_ref, turned):
    me, core = lax.axis_index("dp"), lax.axis_index("ctx")
    model = turned.shape[0]
    lanes = 128
    for start in range(0, model, lanes):
        turned[start:start + lanes] = jnp.transpose(upstream_ref[0, :, start:start + lanes].astype(F32))
    share = model // count
    half = share // 2
    at = 0
    for ref, places in ((first_ref, range(count // 2, count)), (second_ref, range(count // 2))):
        offset = sent = 0
        for rows, orders in plan:
            for place in places:
                masks = [relative(place, order) for order in orders]
                mine = me ^ (masks[0] + core * (masks[1] - masks[0]))
                other = me ^ (masks[1] + core * (masks[0] - masks[1]))
                begin = pl.multiple_of(mine * share + core * half + offset, 16)
                own_ref[at:at + rows] = turned[pl.ds(begin, rows)].astype(BF16)
                begin = pl.multiple_of(other * share + (1 - core) * half + offset, 16)
                ref[sent:sent + rows] = turned[pl.ds(begin, rows)]
                at += rows
                sent += rows
            offset += rows


def joint_kernel(
    own_ref, other_ref,
    cumul_ref, scores_ref, state_ref, normed_ref, scale_ref, rounded_ref,
):
    first = lax.axis_index("ctx") == 0
    length = cumul_ref.shape[0]
    lower = lower_mask(length)

    def scaled(block):
        query, key, value, decay = block
        cumul = cumulate(decay)
        query_scaled = split(query * jnp.exp(cumul), 2)
        key_scaled = split(key * jnp.exp(-cumul), 2)
        return cumul, query_scaled, key_scaled, value.astype(BF16)

    def within(query_scaled, key_scaled, value):
        scores = jnp.where(lower, product(query_scaled, key_scaled, 1, 1), 0.0)
        return scores, product(split(scores, 2), [value], 1, 0)

    def normalized(output):
        scale_inv = lax.rsqrt(jnp.mean(output * output, axis=-1, keepdims=True) + EPSILON)
        normed = output * scale_inv
        return normed, jnp.broadcast_to(scale_inv, normed.shape), normed.astype(BF16)

    early = [jnp.where(first, own_ref[i], other_ref[i]) for i in range(4)]
    late = [jnp.where(first, other_ref[i], own_ref[i]) for i in range(4)]
    cumul_early, queries_early, keys_early, values_early = scaled(early)
    cumul_late, queries_late, keys_late, values_late = scaled(late)
    to_end = jnp.exp(cumul_early[-1:] - cumul_early)
    state = product(split(early[1] * to_end, 2), [values_early], 0, 0)
    scores_early, output_early = within(queries_early, keys_early, values_early)
    scores_late, output_late = within(queries_late, keys_late, values_late)
    output_late += product(queries_late, split(state, 2), 1, 0)
    done_early = normalized(output_early)
    done_late = normalized(output_late)
    cumul_ref[...] = jnp.where(first, cumul_early, cumul_late)
    scores_ref[...] = jnp.where(first, scores_early, scores_late)
    state_ref[...] = jnp.where(first, 0.0, state)
    normed_ref[...] = jnp.where(first, done_early[0], done_late[0])
    scale_ref[...] = jnp.where(first, done_early[1], done_late[1])
    rounded_ref[:length] = jnp.where(first, done_early[2], done_late[2])
    rounded_ref[length:] = jnp.where(first, done_late[2], done_early[2])


def share_kernel(begin, own_ref, received_ref, rounded_ref, *outs):
    at = 0
    for out in outs:
        rows = out.shape[0]
        left = jnp.concatenate(
            [own_ref[begin + at:begin + at + rows], received_ref[at:at + rows].astype(BF16)], axis=1
        )
        out[...] = jnp.dot(left, rounded_ref[...], preferred_element_type=F32)
        at += rows


def exchanged(value, count, bits):
    pairs = [
        (device * 2 + core, (device ^ (1 << bits[core])) * 2 + core)
        for device in range(count)
        for core in range(2)
    ]
    return lax.ppermute(value, BOTH, pairs)


def halving(kept, sent, plan, count, beside):
    stages = len(plan[0][1][0])
    joined = 3
    for stage in range(joined):
        arrived = [
            exchanged(part, count, [order[stage] for order in orders])
            for part, (_, orders) in zip(sent, plan)
        ]
        if stage in beside:
            arrived = beside[stage](arrived)
        half = [len(part) // 2 if stage + 1 < stages else len(part) for part in kept]
        sums = [
            (old[:size] + new[:size], old[size:] + new[size:])
            for old, new, size in zip(kept, arrived, half)
        ]
        kept = [pair[0] for pair in sums]
        sent = [pair[1] for pair in sums]
    for stage in range(joined, stages):
        sizes = [len(part) for part in sent]
        new = exchanged(jnp.concatenate(sent), count, [stage] * 2)
        if stage in beside:
            new = beside[stage](new)
        starts = [sum(sizes[:index]) for index in range(len(sizes))]
        sums = [part + new[at:at + size] for part, at, size in zip(kept, starts, sizes)]
        kept = [part[: len(part) // 2] if stage + 1 < stages else part for part in sums]
        sent = [part[len(part) // 2:] for part in sums]
    return jnp.concatenate(kept)


def shifted(value, axis, steps):
    count = lax.axis_size(axis)
    leading, last = (max(0, -steps), min(count, count - steps))
    return lax.ppermute(value, axis, [(source, source + steps) for source in range(leading, last)])


def body(queries, key_vectors, value_vectors, log_decay, out_weight, cotangent):
    length, width = queries.shape[1:]
    model = cotangent.shape[2]
    shards, count = lax.axis_size("ctx"), lax.axis_size("dp")
    square = (length, width)
    rows = model // count // 2
    flops = 8 * length * width * model
    paired = shards == 2 and count >= 16 and count & (count - 1) == 0 and rows % 16 == 0

    (packed,) = local_call(
        pack_kernel,
        [((4, length, width), F32)],
        queries, key_vectors, value_vectors, log_decay,
        name="pack", flops=20 * flops, space=pltpu.HBM, limit=PACK_BYTES,
        scratch=[pltpu.VMEM(square, BF16)] * 3 + [pltpu.SemaphoreType.DMA((4,))],
    )
    if paired:
        plan = halving_plan(count, rows)
        part_rows = rows * count // 2
        own, send_first, send_second = local_call(
            functools.partial(turn_kernel, count, plan),
            [((2 * part_rows, length), BF16), ((part_rows, length), F32), ((part_rows, length), F32)],
            cotangent,
            name="turn", flops=20 * flops,
            scratch=[pltpu.VMEM((model, length), F32)],
        )
        others = swap(packed)
        received_first = swap(send_first)
        others, send_second = lax.optimization_barrier((others, send_second))
        received_second = swap(send_second)
        cumul, scores, state_in, normed, scale_inv, rounded = local_call(
            joint_kernel,
            [
                (square, F32), ((length, length), F32), ((width, width), F32), (square, F32),
                (square, F32), ((2 * length, width), BF16),
            ],
            packed, others,
            name="joint", flops=40 * flops,
        )
        sent = local_call(
            functools.partial(share_kernel, 0),
            [((count // 2 * part, width), F32) for part, _ in plan],
            own, received_first, rounded,
            name="sent_shares", flops=flops // 4,
        )
        kept = local_call(
            functools.partial(share_kernel, part_rows),
            [((count // 2 * part, width), F32) for part, _ in plan],
            own, received_second, rounded,
            name="kept_shares", flops=flops // 4,
        )
    else:
        (local_state,) = local_call(
            state_kernel, [((width, width), F32)], key_vectors, value_vectors, log_decay,
            name="state", flops=flops // 2,
        )
        state_in = shifted(local_state, "ctx", 1)
        within, scores, cumul = local_call(
            within_kernel,
            [(square, F32), ((length, length), F32), (square, F32)],
            queries, key_vectors, value_vectors, log_decay,
            name="within", flops=flops // 2,
        )
        device_decay = jnp.exp(cumul[-1])[:, None]
        for _ in range(shards - 2):
            state_in = shifted(local_state + device_decay * state_in, "ctx", 1)
        normed, scale_inv, rounded = local_call(
            normed_kernel, [(square, F32)] * 3, queries, cumul, within, state_in,
            name="normed", flops=flops // 4,
        )

    grad_query, grad_key_zero, grad_value_zero, gate, grad_sent = local_call(
        grads_kernel,
        [
            (queries.shape, BF16), (square, F32), (square, F32), (square, F32),
            ((width + 8, width), F32),
        ],
        packed, cumul, scores, state_in, normed, scale_inv,
        cotangent, out_weight,
        name="grads", flops=2 * flops,
    )
    later = swap(grad_sent) if paired else shifted(grad_sent, "ctx", -1)

    def finish(later):
        return local_call(
            finish_kernel,
            [(queries.shape, BF16), (queries.shape, BF16), (queries.shape, F32)],
            packed, cumul, grad_key_zero, grad_value_zero, gate, later,
            name="finish", flops=flops,
        )

    if paired:
        held = {}

        def beside_first(arrived):
            large, small = arrived
            small, held["query"] = lax.optimization_barrier((small, grad_query))
            return [large, small]

        def beside_third(arrived):
            large, small = arrived
            large, held["later"] = lax.optimization_barrier((large, later))
            return [large, small]

        def beside_last(arrived):
            key, value, decay = finish(held["later"])
            arrived, decay = lax.optimization_barrier((arrived, decay))
            held["finished"] = key, value, decay
            return arrived

        beside = {0: beside_first, 2: beside_third, 3: beside_last}
        mine = halving(kept, sent, plan, count, beside)
        grad_query = held["query"]
        grad_key, grad_value, grad_decay = held["finished"]
        theirs = swap(mine)
        first = lax.axis_index("ctx") == 0
        grad_weight = jnp.concatenate(
            [jnp.where(first, mine, theirs), jnp.where(first, theirs, mine)], axis=0
        )
    else:
        for _ in range(shards - 2):
            grad_in = later[:width]
            own_sum = grad_sent[width:] - jnp.sum(grad_in * local_state, axis=-1)[None]
            later = shifted(
                jnp.concatenate([grad_sent[:width] + device_decay * grad_in, own_sum + later[width:]]),
                "ctx",
                -1,
            )
        grad_key, grad_value, grad_decay = finish(later)
        share = jnp.einsum(
            "td,tk->dk", cotangent[0], rounded.astype(BF16), preferred_element_type=F32
        )
        share = lax.psum_scatter(share, "dp", scatter_dimension=0, tiled=True)
        grad_weight = lax.psum(share, "ctx")

    return grad_query, grad_key, grad_value, grad_decay, grad_weight


def solution(mesh):
    placed = (
        P("dp", "ctx", None),
        P("dp", "ctx", None),
        P("dp", "ctx", None),
        P("dp", "ctx", None),
        P(),
        P("dp", "ctx", None),
    )
    return jax.shard_map(
        body,
        mesh=mesh,
        in_specs=placed,
        out_specs=(
            P("dp", "ctx", None),
            P("dp", "ctx", None),
            P("dp", "ctx", None),
            P("dp", "ctx", None),
            P("dp", None),
        ),
        check_vma=False,
    )
```

```python
import functools

import jax
import jax.numpy as jnp
from jax import lax
from jax.experimental import pallas as pl
from jax.experimental.pallas import tpu as pltpu
from jax.sharding import PartitionSpec as P

EPSILON = 1e-05
VMEM_BYTES = 24 * 1024 * 1024
F32 = jnp.float32
BF16 = jnp.bfloat16
BOTH = ("dp", "ctx")


def split(value, parts):
    pieces = []
    for index in range(parts):
        piece = value.astype(BF16)
        pieces.append(piece)
        if index + 1 < parts:
            value = value - piece.astype(F32)
    return pieces


def product(left, right, left_axis, right_axis):
    dims = (((left_axis,), (right_axis,)), ((), ()))
    most = max(len(left), len(right))
    total = None
    for order in reversed(range(most)):
        for i, l in enumerate(left):
            j = order - i
            if 0 <= j < len(right):
                term = lax.dot_general(l, right[j], dims, preferred_element_type=F32)
                total = term if total is None else total + term
    return total


def lower_mask(length):
    rows = lax.broadcasted_iota(jnp.int32, (length, length), 0)
    columns = lax.broadcasted_iota(jnp.int32, (length, length), 1)
    return rows >= columns


def cumulate(decay, lower=None):
    if lower is None:
        lower = lower_mask(decay.shape[0]).astype(F32).astype(BF16)
    return product([lower], split(decay, 3), 1, 0)


def state_kernel(key_ref, value_ref, decay_ref, state_ref):
    cumul = cumulate(decay_ref[0])
    to_end = jnp.exp(cumul[-1:] - cumul)
    key_to_end = key_ref[0].astype(F32) * to_end
    state_ref[...] = product(split(key_to_end, 2), [value_ref[0]], 0, 0)


def within_kernel(query_ref, key_ref, value_ref, decay_ref, within_ref, scores_ref, cumul_ref):
    cumul = cumulate(decay_ref[0])
    cumul_ref[...] = cumul
    query_scaled = query_ref[0].astype(F32) * jnp.exp(cumul)
    key_scaled = key_ref[0].astype(F32) * jnp.exp(-cumul)
    scores = product(split(query_scaled, 2), split(key_scaled, 2), 1, 1)
    scores = jnp.where(lower_mask(cumul.shape[0]), scores, 0.0)
    scores_ref[...] = scores
    within_ref[...] = product(split(scores, 2), [value_ref[0]], 1, 0)


def normed_kernel(query_ref, cumul_ref, within_ref, state_ref, normed_ref, scale_ref, rounded_ref):
    query_scaled = query_ref[0].astype(F32) * jnp.exp(cumul_ref[...])
    output = within_ref[...] + product(split(query_scaled, 2), split(state_ref[...], 2), 1, 0)
    scale_inv = lax.rsqrt(jnp.mean(output * output, axis=-1, keepdims=True) + EPSILON)
    normed = output * scale_inv
    normed_ref[...] = normed
    scale_ref[...] = jnp.broadcast_to(scale_inv, normed.shape)
    rounded_ref[...] = normed.astype(BF16).astype(F32)


def grads_kernel(
    packed_ref, cumul_ref, scores_ref, state_ref, normed_ref, scale_ref,
    upstream_ref, weight_ref,
    grad_query_ref, grad_key_ref, grad_value_ref, gate_ref, sent_ref,
):
    query = packed_ref[0]
    key = packed_ref[1]
    value = packed_ref[2].astype(BF16)
    cumul = cumul_ref[...]
    rising = jnp.exp(cumul)
    falling = jnp.exp(-cumul)
    normed = normed_ref[...]
    grad_normed = jnp.dot(upstream_ref[0], weight_ref[...], preferred_element_type=F32)
    grad_output = scale_ref[...] * (
        grad_normed - normed * jnp.mean(grad_normed * normed, axis=-1, keepdims=True)
    )
    grad_output = split(grad_output, 2)
    query_scaled = split(query * rising, 2)
    key_scaled = split(key * falling, 2)
    pairs = product(grad_output, [value], 1, 1)
    pairs = split(jnp.where(lower_mask(cumul.shape[0]), pairs, 0.0), 2)
    grad_query = rising * (
        product(pairs, key_scaled, 1, 0) + product(grad_output, split(state_ref[...], 2), 1, 1)
    )
    grad_query_ref[0] = grad_query.astype(BF16)
    grad_key = falling * product(pairs, query_scaled, 0, 0)
    grad_key_ref[...] = grad_key
    grad_value_ref[...] = product(split(scores_ref[...], 2), grad_output, 0, 0)
    gate = query * grad_query - key * grad_key
    gate_ref[...] = gate
    width = query.shape[1]
    sent_ref[:width] = product(query_scaled, grad_output, 0, 0)
    sent_ref[width:] = jnp.broadcast_to(
        jnp.sum(gate, axis=0, keepdims=True), (sent_ref.shape[0] - width, width)
    )


def finish_kernel(
    packed_ref, cumul_ref, grad_key_ref, grad_value_ref, gate_ref, later_ref,
    key_out_ref, value_out_ref, decay_out_ref,
):
    key = packed_ref[1]
    cumul = cumul_ref[...]
    width = key.shape[1]
    to_end = jnp.exp(cumul[-1:] - cumul)
    last = lax.axis_index("ctx") == lax.axis_size("ctx") - 1
    later = jnp.where(last, 0.0, later_ref[...])
    grad_in = split(later[:width], 2)
    extra = to_end * product([packed_ref[2].astype(BF16)], grad_in, 1, 1)
    key_out_ref[0] = (grad_key_ref[...] + extra).astype(BF16)
    grad_value = grad_value_ref[...] + product(split(key * to_end, 2), grad_in, 1, 0)
    value_out_ref[0] = grad_value.astype(BF16)
    gate = gate_ref[...] - key * extra
    lower = lower_mask(cumul.shape[0]).astype(F32).astype(BF16)
    decay_out_ref[0] = product([lower], split(gate, 3), 0, 0) + later[width:width + 1]


def local_call(kernel, shapes, *operands, name, flops, scratch=(), space=pltpu.VMEM, limit=VMEM_BYTES):
    outs = [jax.ShapeDtypeStruct(shape, dtype) for shape, dtype in shapes]
    moved = sum(array.size * array.dtype.itemsize for array in [*operands, *outs])
    return pl.pallas_call(
        kernel,
        out_shape=outs,
        in_specs=[pl.BlockSpec(memory_space=space)] * len(operands),
        scratch_shapes=list(scratch),
        compiler_params=pltpu.CompilerParams(vmem_limit_bytes=limit),
        cost_estimate=pl.CostEstimate(flops=flops, bytes_accessed=moved, transcendentals=0),
        name=name,
    )(*operands)


def swap(value):
    return lax.ppermute(value, "ctx", [(0, 1), (1, 0)])


def halving_plan(count, rows):
    bits = count.bit_length() - 1
    last = rows // 32 * 16
    rest = list(range(3, bits))
    return [
        (rows - last, ([0, 1, 2] + rest, [1, 0, 2] + rest)),
        (last, ([2, 0, 1] + rest, [1, 2, 0] + rest)),
    ]


def relative(place, order):
    top = len(order) - 1
    return sum(((place >> (top - step)) & 1) << bit for step, bit in enumerate(order))


def lower_kernel(lower_ref):
    lower_ref[...] = lower_mask(lower_ref.shape[0]).astype(F32).astype(BF16)


def turn_kernel(count, plan, upstream_ref, own_ref, first_ref, second_ref, turned):
    me, core = lax.axis_index("dp"), lax.axis_index("ctx")
    model = turned.shape[0]
    lanes = 128
    for start in range(0, model, lanes):
        turned[start:start + lanes] = jnp.transpose(upstream_ref[0, :, start:start + lanes].astype(F32))
    share = model // count
    half = share // 2
    at = 0
    for ref, places in ((first_ref, range(count // 2, count)), (second_ref, range(count // 2))):
        offset = sent = 0
        for rows, orders in plan:
            for place in places:
                masks = [relative(place, order) for order in orders]
                mine = me ^ (masks[0] + core * (masks[1] - masks[0]))
                other = me ^ (masks[1] + core * (masks[0] - masks[1]))
                begin = pl.multiple_of(mine * share + core * half + offset, 16)
                own_ref[at:at + rows] = turned[pl.ds(begin, rows)].astype(BF16)
                begin = pl.multiple_of(other * share + (1 - core) * half + offset, 16)
                ref[sent:sent + rows] = turned[pl.ds(begin, rows)]
                at += rows
                sent += rows
            offset += rows


def joint_kernel(
    own_ref, other_ref, lower_ref,
    cumul_ref, scores_ref, state_ref, normed_ref, scale_ref, rounded_ref,
):
    first = lax.axis_index("ctx") == 0
    length = cumul_ref.shape[0]
    lower = lower_mask(length)

    def scaled(block):
        query, key, value, decay = block
        cumul = cumulate(decay, lower_ref[...])
        query_scaled = split(query * jnp.exp(cumul), 2)
        key_scaled = split(key * jnp.exp(-cumul), 2)
        return cumul, query_scaled, key_scaled, value.astype(BF16)

    def within(query_scaled, key_scaled, value):
        scores = jnp.where(lower, product(query_scaled, key_scaled, 1, 1), 0.0)
        return scores, product(split(scores, 2), [value], 1, 0)

    def normalized(output):
        scale_inv = lax.rsqrt(jnp.mean(output * output, axis=-1, keepdims=True) + EPSILON)
        normed = output * scale_inv
        return normed, jnp.broadcast_to(scale_inv, normed.shape), normed.astype(BF16)

    early = [jnp.where(first, own_ref[i], other_ref[i]) for i in range(4)]
    late = [jnp.where(first, other_ref[i], own_ref[i]) for i in range(4)]
    cumul_early, queries_early, keys_early, values_early = scaled(early)
    cumul_late, queries_late, keys_late, values_late = scaled(late)
    to_end = jnp.exp(cumul_early[-1:] - cumul_early)
    state = product(split(early[1] * to_end, 2), [values_early], 0, 0)
    scores_early, output_early = within(queries_early, keys_early, values_early)
    scores_late, output_late = within(queries_late, keys_late, values_late)
    output_late += product(queries_late, split(state, 2), 1, 0)
    done_early = normalized(output_early)
    done_late = normalized(output_late)
    cumul_ref[...] = jnp.where(first, cumul_early, cumul_late)
    scores_ref[...] = jnp.where(first, scores_early, scores_late)
    state_ref[...] = jnp.where(first, 0.0, state)
    normed_ref[...] = jnp.where(first, done_early[0], done_late[0])
    scale_ref[...] = jnp.where(first, done_early[1], done_late[1])
    rounded_ref[:length] = jnp.where(first, done_early[2], done_late[2])
    rounded_ref[length:] = jnp.where(first, done_late[2], done_early[2])


def share_kernel(begin, own_ref, received_ref, rounded_ref, *outs):
    at = 0
    for out in outs:
        rows = out.shape[0]
        left = jnp.concatenate(
            [own_ref[begin + at:begin + at + rows], received_ref[at:at + rows].astype(BF16)], axis=1
        )
        out[...] = jnp.dot(left, rounded_ref[...], preferred_element_type=F32)
        at += rows


def exchanged(value, count, bits):
    pairs = [
        (device * 2 + core, (device ^ (1 << bits[core])) * 2 + core)
        for device in range(count)
        for core in range(2)
    ]
    return lax.ppermute(value, BOTH, pairs)


def halving(kept, sent, plan, count, beside):
    stages = len(plan[0][1][0])
    joined = 3
    for stage in range(joined):
        arrived = [
            exchanged(part, count, [order[stage] for order in orders])
            for part, (_, orders) in zip(sent, plan)
        ]
        if stage in beside:
            arrived = beside[stage](arrived)
        half = [len(part) // 2 if stage + 1 < stages else len(part) for part in kept]
        sums = [
            (old[:size] + new[:size], old[size:] + new[size:])
            for old, new, size in zip(kept, arrived, half)
        ]
        kept = [pair[0] for pair in sums]
        sent = [pair[1] for pair in sums]
    for stage in range(joined, stages):
        sizes = [len(part) for part in sent]
        new = exchanged(jnp.concatenate(sent), count, [stage] * 2)
        if stage in beside:
            new = beside[stage](new)
        starts = [sum(sizes[:index]) for index in range(len(sizes))]
        sums = [part + new[at:at + size] for part, at, size in zip(kept, starts, sizes)]
        kept = [part[: len(part) // 2] if stage + 1 < stages else part for part in sums]
        sent = [part[len(part) // 2:] for part in sums]
    return jnp.concatenate(kept)


def shifted(value, axis, steps):
    count = lax.axis_size(axis)
    leading, last = (max(0, -steps), min(count, count - steps))
    return lax.ppermute(value, axis, [(source, source + steps) for source in range(leading, last)])


def body(queries, key_vectors, value_vectors, log_decay, out_weight, cotangent):
    length, width = queries.shape[1:]
    model = cotangent.shape[2]
    shards, count = lax.axis_size("ctx"), lax.axis_size("dp")
    square = (length, width)
    rows = model // count // 2
    flops = 8 * length * width * model
    paired = shards == 2 and count >= 16 and count & (count - 1) == 0 and rows % 16 == 0

    (lower,) = local_call(lower_kernel, [((length, length), BF16)], name="lower", flops=20 * flops)
    inputs = (queries, key_vectors, value_vectors, log_decay)
    *inputs, lower = lax.optimization_barrier((*inputs, lower))
    packed = jnp.concatenate([jnp.concatenate(inputs[:3]).astype(F32), inputs[3]])
    if paired:
        plan = halving_plan(count, rows)
        part_rows = rows * count // 2
        own, send_first, send_second = local_call(
            functools.partial(turn_kernel, count, plan),
            [((2 * part_rows, length), BF16), ((part_rows, length), F32), ((part_rows, length), F32)],
            cotangent,
            name="turn", flops=20 * flops,
            scratch=[pltpu.VMEM((model, length), F32)],
        )
        others = swap(packed)
        received_first = swap(send_first)
        others, send_second = lax.optimization_barrier((others, send_second))
        received_second = swap(send_second)
        cumul, scores, state_in, normed, scale_inv, rounded = local_call(
            joint_kernel,
            [
                (square, F32), ((length, length), F32), ((width, width), F32), (square, F32),
                (square, F32), ((2 * length, width), BF16),
            ],
            packed, others, lower,
            name="joint", flops=40 * flops,
        )
        sent = local_call(
            functools.partial(share_kernel, 0),
            [((count // 2 * part, width), F32) for part, _ in plan],
            own, received_first, rounded,
            name="sent_shares", flops=flops // 4,
        )
        kept = local_call(
            functools.partial(share_kernel, part_rows),
            [((count // 2 * part, width), F32) for part, _ in plan],
            own, received_second, rounded,
            name="kept_shares", flops=flops // 4,
        )
    else:
        (local_state,) = local_call(
            state_kernel, [((width, width), F32)], key_vectors, value_vectors, log_decay,
            name="state", flops=flops // 2,
        )
        state_in = shifted(local_state, "ctx", 1)
        within, scores, cumul = local_call(
            within_kernel,
            [(square, F32), ((length, length), F32), (square, F32)],
            queries, key_vectors, value_vectors, log_decay,
            name="within", flops=flops // 2,
        )
        device_decay = jnp.exp(cumul[-1])[:, None]
        for _ in range(shards - 2):
            state_in = shifted(local_state + device_decay * state_in, "ctx", 1)
        normed, scale_inv, rounded = local_call(
            normed_kernel, [(square, F32)] * 3, queries, cumul, within, state_in,
            name="normed", flops=flops // 4,
        )

    grad_query, grad_key_zero, grad_value_zero, gate, grad_sent = local_call(
        grads_kernel,
        [
            (queries.shape, BF16), (square, F32), (square, F32), (square, F32),
            ((width + 8, width), F32),
        ],
        packed, cumul, scores, state_in, normed, scale_inv,
        cotangent, out_weight,
        name="grads", flops=2 * flops,
    )
    later = swap(grad_sent) if paired else shifted(grad_sent, "ctx", -1)

    def finish(later):
        return local_call(
            finish_kernel,
            [(queries.shape, BF16), (queries.shape, BF16), (queries.shape, F32)],
            packed, cumul, grad_key_zero, grad_value_zero, gate, later,
            name="finish", flops=flops,
        )

    if paired:
        held = {}

        def beside_first(arrived):
            large, small = arrived
            small, held["query"] = lax.optimization_barrier((small, grad_query))
            return [large, small]

        def beside_third(arrived):
            large, small = arrived
            large, held["later"] = lax.optimization_barrier((large, later))
            return [large, small]

        def beside_last(arrived):
            key, value, decay = finish(held["later"])
            arrived, decay = lax.optimization_barrier((arrived, decay))
            held["finished"] = key, value, decay
            return arrived

        beside = {0: beside_first, 2: beside_third, 3: beside_last}
        mine = halving(kept, sent, plan, count, beside)
        grad_query = held["query"]
        grad_key, grad_value, grad_decay = held["finished"]
        theirs = swap(mine)
        first = lax.axis_index("ctx") == 0
        grad_weight = jnp.concatenate(
            [jnp.where(first, mine, theirs), jnp.where(first, theirs, mine)], axis=0
        )
    else:
        for _ in range(shards - 2):
            grad_in = later[:width]
            own_sum = grad_sent[width:] - jnp.sum(grad_in * local_state, axis=-1)[None]
            later = shifted(
                jnp.concatenate([grad_sent[:width] + device_decay * grad_in, own_sum + later[width:]]),
                "ctx",
                -1,
            )
        grad_key, grad_value, grad_decay = finish(later)
        share = jnp.einsum(
            "td,tk->dk", cotangent[0], rounded.astype(BF16), preferred_element_type=F32
        )
        share = lax.psum_scatter(share, "dp", scatter_dimension=0, tiled=True)
        grad_weight = lax.psum(share, "ctx")

    return grad_query, grad_key, grad_value, grad_decay, grad_weight


def solution(mesh):
    placed = (
        P("dp", "ctx", None),
        P("dp", "ctx", None),
        P("dp", "ctx", None),
        P("dp", "ctx", None),
        P(),
        P("dp", "ctx", None),
    )
    return jax.shard_map(
        body,
        mesh=mesh,
        in_specs=placed,
        out_specs=(
            P("dp", "ctx", None),
            P("dp", "ctx", None),
            P("dp", "ctx", None),
            P("dp", "ctx", None),
            P("dp", None),
        ),
        check_vma=False,
    )
```

```python
import functools

import jax
import jax.numpy as jnp
from jax import lax
from jax.experimental import pallas as pl
from jax.experimental.pallas import tpu as pltpu
from jax.sharding import PartitionSpec as P

EPSILON = 1e-05
VMEM_BYTES = 24 * 1024 * 1024
F32 = jnp.float32
BF16 = jnp.bfloat16
BOTH = ("dp", "ctx")


def split(value, parts):
    if value.dtype == BF16:
        return [value]
    pieces = []
    for index in range(parts):
        piece = value.astype(BF16)
        pieces.append(piece)
        if index + 1 < parts:
            value = value - piece.astype(F32)
    return pieces


def product(left, right, left_axis, right_axis):
    dims = (((left_axis,), (right_axis,)), ((), ()))
    most = max(len(left), len(right))
    total = None
    for order in reversed(range(most)):
        for i, l in enumerate(left):
            j = order - i
            if 0 <= j < len(right):
                term = lax.dot_general(l, right[j], dims, preferred_element_type=F32)
                total = term if total is None else total + term
    return total


def lower_mask(length):
    rows = lax.broadcasted_iota(jnp.int32, (length, length), 0)
    columns = lax.broadcasted_iota(jnp.int32, (length, length), 1)
    return rows >= columns


def cumulate(decay):
    lower = lower_mask(decay.shape[0]).astype(F32).astype(BF16)
    return product([lower], split(decay, 3), 1, 0)


def state_kernel(key_ref, value_ref, decay_ref, state_ref):
    cumul = cumulate(decay_ref[0])
    to_end = jnp.exp(cumul[-1:] - cumul)
    key_to_end = key_ref[0].astype(F32) * to_end
    state_ref[...] = product(split(key_to_end, 2), [value_ref[0]], 0, 0)


def within_kernel(query_ref, key_ref, value_ref, decay_ref, within_ref, scores_ref, cumul_ref):
    cumul = cumulate(decay_ref[0])
    cumul_ref[...] = cumul
    query_scaled = query_ref[0].astype(F32) * jnp.exp(cumul)
    key_scaled = key_ref[0].astype(F32) * jnp.exp(-cumul)
    scores = product(split(query_scaled, 2), split(key_scaled, 2), 1, 1)
    scores = jnp.where(lower_mask(cumul.shape[0]), scores, 0.0)
    scores_ref[...] = scores
    within_ref[...] = product(split(scores, 2), [value_ref[0]], 1, 0)


def normed_kernel(query_ref, cumul_ref, within_ref, state_ref, normed_ref, scale_ref, rounded_ref):
    query_scaled = query_ref[0].astype(F32) * jnp.exp(cumul_ref[...])
    output = within_ref[...] + product(split(query_scaled, 2), split(state_ref[...], 2), 1, 0)
    scale_inv = lax.rsqrt(jnp.mean(output * output, axis=-1, keepdims=True) + EPSILON)
    normed = output * scale_inv
    normed_ref[...] = normed
    scale_ref[...] = jnp.broadcast_to(scale_inv, normed.shape)
    rounded_ref[...] = normed.astype(BF16).astype(F32)


def grads_kernel(
    packed_ref, cumul_ref, scores_ref, state_ref, normed_ref, scale_ref,
    upstream_ref, weight_ref,
    grad_query_ref, grad_key_ref, grad_value_ref, gate_ref, sent_ref,
):
    query = packed_ref[0]
    key = packed_ref[1]
    value = packed_ref[2].astype(BF16)
    cumul = cumul_ref[...]
    rising = jnp.exp(cumul)
    falling = jnp.exp(-cumul)
    normed = normed_ref[...]
    grad_normed = jnp.dot(upstream_ref[0], weight_ref[...], preferred_element_type=F32)
    grad_output = scale_ref[...] * (
        grad_normed - normed * jnp.mean(grad_normed * normed, axis=-1, keepdims=True)
    )
    grad_output = split(grad_output, 2)
    query_scaled = split(query * rising, 2)
    key_scaled = split(key * falling, 2)
    pairs = product(grad_output, [value], 1, 1)
    pairs = split(jnp.where(lower_mask(cumul.shape[0]), pairs, 0.0), 2)
    grad_query = rising * (
        product(pairs, key_scaled, 1, 0) + product(grad_output, split(state_ref[...], 2), 1, 1)
    )
    grad_query_ref[0] = grad_query.astype(BF16)
    grad_key = falling * product(pairs, query_scaled, 0, 0)
    grad_key_ref[...] = grad_key
    grad_value_ref[...] = product(split(scores_ref[...], 2), grad_output, 0, 0)
    gate = query * grad_query - key * grad_key
    gate_ref[...] = gate
    width = query.shape[1]
    sent_ref[:width] = product(query_scaled, grad_output, 0, 0)
    sent_ref[width:] = jnp.broadcast_to(
        jnp.sum(gate, axis=0, keepdims=True), (sent_ref.shape[0] - width, width)
    )


def finish_kernel(
    packed_ref, cumul_ref, grad_key_ref, grad_value_ref, gate_ref, later_ref,
    key_out_ref, value_out_ref, decay_out_ref,
):
    key = packed_ref[1]
    cumul = cumul_ref[...]
    width = key.shape[1]
    to_end = jnp.exp(cumul[-1:] - cumul)
    last = lax.axis_index("ctx") == lax.axis_size("ctx") - 1
    later = jnp.where(last, 0.0, later_ref[...])
    grad_in = split(later[:width], 2)
    extra = to_end * product([packed_ref[2].astype(BF16)], grad_in, 1, 1)
    key_out_ref[0] = (grad_key_ref[...] + extra).astype(BF16)
    grad_value = grad_value_ref[...] + product(split(key * to_end, 2), grad_in, 1, 0)
    value_out_ref[0] = grad_value.astype(BF16)
    gate = gate_ref[...] - key * extra
    lower = lower_mask(cumul.shape[0]).astype(F32).astype(BF16)
    decay_out_ref[0] = product([lower], split(gate, 3), 0, 0) + later[width:width + 1]


def local_call(kernel, shapes, *operands, name, flops, scratch=(), space=pltpu.VMEM, limit=VMEM_BYTES):
    outs = [jax.ShapeDtypeStruct(shape, dtype) for shape, dtype in shapes]
    moved = sum(array.size * array.dtype.itemsize for array in [*operands, *outs])
    return pl.pallas_call(
        kernel,
        out_shape=outs,
        in_specs=[pl.BlockSpec(memory_space=space)] * len(operands),
        scratch_shapes=list(scratch),
        compiler_params=pltpu.CompilerParams(vmem_limit_bytes=limit),
        cost_estimate=pl.CostEstimate(flops=flops, bytes_accessed=moved, transcendentals=0),
        name=name,
    )(*operands)


def swap(value):
    return lax.ppermute(value, "ctx", [(0, 1), (1, 0)])


def halving_plan(count, rows):
    bits = count.bit_length() - 1
    last = rows // 32 * 16
    rest = list(range(3, bits))
    return [
        (rows - last, ([0, 1, 2] + rest, [1, 0, 2] + rest)),
        (last, ([2, 0, 1] + rest, [1, 2, 0] + rest)),
    ]


def relative(place, order):
    top = len(order) - 1
    return sum(((place >> (top - step)) & 1) << bit for step, bit in enumerate(order))


def lower_kernel(lower_ref):
    lower_ref[...] = lower_mask(lower_ref.shape[0]).astype(F32).astype(BF16)


def turn_kernel(count, plan, upstream_ref, own_ref, first_ref, second_ref, turned):
    me, core = lax.axis_index("dp"), lax.axis_index("ctx")
    model = turned.shape[0]
    lanes = 128
    for start in range(0, model, lanes):
        turned[start:start + lanes] = jnp.transpose(upstream_ref[0, :, start:start + lanes].astype(F32))
    share = model // count
    half = share // 2
    at = 0
    for ref, places in ((first_ref, range(count // 2, count)), (second_ref, range(count // 2))):
        offset = sent = 0
        for rows, orders in plan:
            for place in places:
                masks = [relative(place, order) for order in orders]
                mine = me ^ (masks[0] + core * (masks[1] - masks[0]))
                other = me ^ (masks[1] + core * (masks[0] - masks[1]))
                begin = pl.multiple_of(mine * share + core * half + offset, 16)
                own_ref[at:at + rows] = turned[pl.ds(begin, rows)].astype(BF16)
                begin = pl.multiple_of(other * share + (1 - core) * half + offset, 16)
                ref[sent:sent + rows] = turned[pl.ds(begin, rows)]
                at += rows
                sent += rows
            offset += rows


def joined(pairs, left_axis, right_axis):
    lefts, rights = [], []
    for left, left_parts, right, right_parts in pairs:
        left, right = split(left, left_parts), split(right, right_parts)
        for i in range(left_parts):
            for j in range(right_parts):
                if i + j < max(left_parts, right_parts):
                    lefts.append(left[i])
                    rights.append(right[j])
    return lax.dot_general(
        jnp.concatenate(lefts, axis=left_axis),
        jnp.concatenate(rights, axis=right_axis),
        (((left_axis,), (right_axis,)), ((), ())),
        preferred_element_type=F32,
    )


def joint_kernel(
    own_ref, other_ref, lower_ref,
    cumul_ref, scores_ref, state_ref, normed_ref, scale_ref, rounded_ref,
):
    first = lax.axis_index("ctx") == 0
    length, width = cumul_ref.shape
    lower = lower_mask(length)

    def normalized(output):
        scale_inv = lax.rsqrt(jnp.mean(output * output, axis=-1, keepdims=True) + EPSILON)
        normed = output * scale_inv
        return normed, jnp.broadcast_to(scale_inv, normed.shape), normed.astype(BF16)

    query, key, value, decay = [
        [jnp.where(first, own_ref[i], other_ref[i]), jnp.where(first, other_ref[i], own_ref[i])]
        for i in range(4)
    ]
    cumuls = joined([(lower_ref[...], 1, jnp.concatenate(decay, axis=1), 3)], 1, 0)
    cumul = [cumuls[:, :width], cumuls[:, width:]]
    scaled = [q * jnp.exp(c) for q, c in zip(query, cumul)]
    scores = [
        jnp.where(lower, joined([(q, 2, k * jnp.exp(-c), 2)], 1, 1), 0.0)
        for q, k, c in zip(scaled, key, cumul)
    ]
    to_end = jnp.exp(cumul[0][-1:] - cumul[0])
    state = joined([(key[0] * to_end, 2, value[0], 1)], 0, 0)
    early = normalized(joined([(scores[0], 2, value[0], 1)], 1, 0))
    late = normalized(joined([(scores[1], 2, value[1], 1), (scaled[1], 2, state, 2)], 1, 0))
    rounded_ref[:length] = jnp.where(first, early[2], late[2])
    rounded_ref[length:] = jnp.where(first, late[2], early[2])
    cumul_ref[...] = jnp.where(first, cumul[0], cumul[1])
    scores_ref[...] = jnp.where(first, scores[0], scores[1])
    state_ref[...] = jnp.where(first, 0.0, state)
    normed_ref[...] = jnp.where(first, early[0], late[0])
    scale_ref[...] = jnp.where(first, early[1], late[1])


def share_kernel(begin, own_ref, received_ref, rounded_ref, *outs):
    at = 0
    for out in outs:
        rows = out.shape[0]
        left = jnp.concatenate(
            [own_ref[begin + at:begin + at + rows], received_ref[at:at + rows].astype(BF16)], axis=1
        )
        out[...] = jnp.dot(left, rounded_ref[...], preferred_element_type=F32)
        at += rows


def exchanged(value, count, bits):
    pairs = [
        (device * 2 + core, (device ^ (1 << bits[core])) * 2 + core)
        for device in range(count)
        for core in range(2)
    ]
    return lax.ppermute(value, BOTH, pairs)


def halving(kept, sent, plan, count, beside):
    stages = len(plan[0][1][0])
    joined = 3
    for stage in range(joined):
        arrived = [
            exchanged(part, count, [order[stage] for order in orders])
            for part, (_, orders) in zip(sent, plan)
        ]
        if stage in beside:
            arrived = beside[stage](arrived)
        half = [len(part) // 2 if stage + 1 < stages else len(part) for part in kept]
        sums = [
            (old[:size] + new[:size], old[size:] + new[size:])
            for old, new, size in zip(kept, arrived, half)
        ]
        kept = [pair[0] for pair in sums]
        sent = [pair[1] for pair in sums]
    for stage in range(joined, stages):
        sizes = [len(part) for part in sent]
        new = exchanged(jnp.concatenate(sent), count, [stage] * 2)
        if stage in beside:
            new = beside[stage](new)
        starts = [sum(sizes[:index]) for index in range(len(sizes))]
        sums = [part + new[at:at + size] for part, at, size in zip(kept, starts, sizes)]
        kept = [part[: len(part) // 2] if stage + 1 < stages else part for part in sums]
        sent = [part[len(part) // 2:] for part in sums]
    return jnp.concatenate(kept)


def assemble_kernel(mine_ref, theirs_ref, out_ref):
    core = lax.axis_index("ctx")
    rows = mine_ref.shape[0]
    out_ref[pl.ds(pl.multiple_of(core * rows, 8), rows)] = mine_ref[...]
    out_ref[pl.ds(pl.multiple_of((1 - core) * rows, 8), rows)] = theirs_ref[...]


def shifted(value, axis, steps):
    count = lax.axis_size(axis)
    leading, last = (max(0, -steps), min(count, count - steps))
    return lax.ppermute(value, axis, [(source, source + steps) for source in range(leading, last)])


def body(queries, key_vectors, value_vectors, log_decay, out_weight, cotangent):
    length, width = queries.shape[1:]
    model = cotangent.shape[2]
    shards, count = lax.axis_size("ctx"), lax.axis_size("dp")
    square = (length, width)
    rows = model // count // 2
    flops = 8 * length * width * model
    paired = shards == 2 and count >= 16 and count & (count - 1) == 0 and rows % 16 == 0

    (lower,) = local_call(lower_kernel, [((length, length), BF16)], name="lower", flops=20 * flops)
    inputs = (queries, key_vectors, value_vectors, log_decay)
    *inputs, lower = lax.optimization_barrier((*inputs, lower))
    packed = jnp.concatenate([jnp.concatenate(inputs[:3]).astype(F32), inputs[3]])
    if paired:
        plan = halving_plan(count, rows)
        part_rows = rows * count // 2
        own, send_first, send_second = local_call(
            functools.partial(turn_kernel, count, plan),
            [((2 * part_rows, length), BF16), ((part_rows, length), F32), ((part_rows, length), F32)],
            cotangent,
            name="turn", flops=20 * flops,
            scratch=[pltpu.VMEM((model, length), F32)],
        )
        others = swap(packed)
        received_first = swap(send_first)
        cumul, scores, state_in, normed, scale_inv, rounded = local_call(
            joint_kernel,
            [
                (square, F32), ((length, length), F32), ((width, width), F32), (square, F32),
                (square, F32), ((2 * length, width), BF16),
            ],
            packed, others, lower,
            name="joint", flops=40 * flops,
        )
        rounded, send_second = lax.optimization_barrier((rounded, send_second))
        received_second = swap(send_second)
        sent = local_call(
            functools.partial(share_kernel, 0),
            [((count // 2 * part, width), F32) for part, _ in plan],
            own, received_first, rounded,
            name="sent_shares", flops=flops // 4,
        )
        kept = local_call(
            functools.partial(share_kernel, part_rows),
            [((count // 2 * part, width), F32) for part, _ in plan],
            own, received_second, rounded,
            name="kept_shares", flops=flops // 4,
        )
    else:
        (local_state,) = local_call(
            state_kernel, [((width, width), F32)], key_vectors, value_vectors, log_decay,
            name="state", flops=flops // 2,
        )
        state_in = shifted(local_state, "ctx", 1)
        within, scores, cumul = local_call(
            within_kernel,
            [(square, F32), ((length, length), F32), (square, F32)],
            queries, key_vectors, value_vectors, log_decay,
            name="within", flops=flops // 2,
        )
        device_decay = jnp.exp(cumul[-1])[:, None]
        for _ in range(shards - 2):
            state_in = shifted(local_state + device_decay * state_in, "ctx", 1)
        normed, scale_inv, rounded = local_call(
            normed_kernel, [(square, F32)] * 3, queries, cumul, within, state_in,
            name="normed", flops=flops // 4,
        )

    grad_query, grad_key_zero, grad_value_zero, gate, grad_sent = local_call(
        grads_kernel,
        [
            (queries.shape, BF16), (square, F32), (square, F32), (square, F32),
            ((width + 8, width), F32),
        ],
        packed, cumul, scores, state_in, normed, scale_inv,
        cotangent, out_weight,
        name="grads", flops=2 * flops,
    )
    later = swap(grad_sent) if paired else shifted(grad_sent, "ctx", -1)

    def finish(later):
        return local_call(
            finish_kernel,
            [(queries.shape, BF16), (queries.shape, BF16), (queries.shape, F32)],
            packed, cumul, grad_key_zero, grad_value_zero, gate, later,
            name="finish", flops=flops,
        )

    if paired:
        held = {}

        def beside_first(arrived):
            large, small = arrived
            small, held["query"] = lax.optimization_barrier((small, grad_query))
            return [large, small]

        def beside_third(arrived):
            large, small = arrived
            large, held["later"] = lax.optimization_barrier((large, later))
            return [large, small]

        def beside_last(arrived):
            key, value, decay = finish(held["later"])
            arrived, decay = lax.optimization_barrier((arrived, decay))
            held["finished"] = key, value, decay
            return arrived

        beside = {0: beside_first, 2: beside_third, 3: beside_last}
        mine = halving(kept, sent, plan, count, beside)
        grad_query = held["query"]
        grad_key, grad_value, grad_decay = held["finished"]
        (grad_weight,) = local_call(
            assemble_kernel, [((2 * rows, width), F32)], mine, swap(mine),
            name="assemble", flops=flops // 4,
        )
    else:
        for _ in range(shards - 2):
            grad_in = later[:width]
            own_sum = grad_sent[width:] - jnp.sum(grad_in * local_state, axis=-1)[None]
            later = shifted(
                jnp.concatenate([grad_sent[:width] + device_decay * grad_in, own_sum + later[width:]]),
                "ctx",
                -1,
            )
        grad_key, grad_value, grad_decay = finish(later)
        share = jnp.einsum(
            "td,tk->dk", cotangent[0], rounded.astype(BF16), preferred_element_type=F32
        )
        share = lax.psum_scatter(share, "dp", scatter_dimension=0, tiled=True)
        grad_weight = lax.psum(share, "ctx")

    return grad_query, grad_key, grad_value, grad_decay, grad_weight


def solution(mesh):
    placed = (
        P("dp", "ctx", None),
        P("dp", "ctx", None),
        P("dp", "ctx", None),
        P("dp", "ctx", None),
        P(),
        P("dp", "ctx", None),
    )
    return jax.shard_map(
        body,
        mesh=mesh,
        in_specs=placed,
        out_specs=(
            P("dp", "ctx", None),
            P("dp", "ctx", None),
            P("dp", "ctx", None),
            P("dp", "ctx", None),
            P("dp", None),
        ),
        check_vma=False,
    )
```

```python
import functools

import jax
import jax.numpy as jnp
from jax import lax
from jax.experimental import pallas as pl
from jax.experimental.pallas import tpu as pltpu
from jax.sharding import PartitionSpec as P

EPSILON = 1e-05
VMEM_BYTES = 24 * 1024 * 1024
F32 = jnp.float32
BF16 = jnp.bfloat16
BOTH = ("dp", "ctx")


def split(value, parts):
    if value.dtype == BF16:
        return [value]
    pieces = []
    for index in range(parts):
        piece = value.astype(BF16)
        pieces.append(piece)
        if index + 1 < parts:
            value = value - piece.astype(F32)
    return pieces


def product(left, right, left_axis, right_axis):
    dims = (((left_axis,), (right_axis,)), ((), ()))
    most = max(len(left), len(right))
    total = None
    for order in reversed(range(most)):
        for i, l in enumerate(left):
            j = order - i
            if 0 <= j < len(right):
                term = lax.dot_general(l, right[j], dims, preferred_element_type=F32)
                total = term if total is None else total + term
    return total


def lower_mask(length):
    rows = lax.broadcasted_iota(jnp.int32, (length, length), 0)
    columns = lax.broadcasted_iota(jnp.int32, (length, length), 1)
    return rows >= columns


def cumulate(decay):
    lower = lower_mask(decay.shape[0]).astype(F32).astype(BF16)
    return product([lower], split(decay, 3), 1, 0)


def state_kernel(key_ref, value_ref, decay_ref, state_ref):
    cumul = cumulate(decay_ref[0])
    to_end = jnp.exp(cumul[-1:] - cumul)
    key_to_end = key_ref[0].astype(F32) * to_end
    state_ref[...] = product(split(key_to_end, 2), [value_ref[0]], 0, 0)


def within_kernel(query_ref, key_ref, value_ref, decay_ref, within_ref, scores_ref, cumul_ref):
    cumul = cumulate(decay_ref[0])
    cumul_ref[...] = cumul
    query_scaled = query_ref[0].astype(F32) * jnp.exp(cumul)
    key_scaled = key_ref[0].astype(F32) * jnp.exp(-cumul)
    scores = product(split(query_scaled, 2), split(key_scaled, 2), 1, 1)
    scores = jnp.where(lower_mask(cumul.shape[0]), scores, 0.0)
    scores_ref[...] = scores
    within_ref[...] = product(split(scores, 2), [value_ref[0]], 1, 0)


def normed_kernel(query_ref, cumul_ref, within_ref, state_ref, normed_ref, scale_ref, rounded_ref):
    query_scaled = query_ref[0].astype(F32) * jnp.exp(cumul_ref[...])
    output = within_ref[...] + product(split(query_scaled, 2), split(state_ref[...], 2), 1, 0)
    scale_inv = lax.rsqrt(jnp.mean(output * output, axis=-1, keepdims=True) + EPSILON)
    normed = output * scale_inv
    normed_ref[...] = normed
    scale_ref[...] = jnp.broadcast_to(scale_inv, normed.shape)
    rounded_ref[...] = normed.astype(BF16).astype(F32)


def grads_kernel(
    packed_ref, cumul_ref, scores_ref, state_ref, normed_ref, scale_ref,
    upstream_ref, weight_ref,
    grad_query_ref, grad_key_ref, grad_value_ref, gate_ref, sent_ref,
):
    query = packed_ref[0]
    key = packed_ref[1]
    value = packed_ref[2].astype(BF16)
    cumul = cumul_ref[...]
    rising = jnp.exp(cumul)
    falling = jnp.exp(-cumul)
    normed = normed_ref[...]
    grad_normed = jnp.dot(upstream_ref[0], weight_ref[...], preferred_element_type=F32)
    grad_output = scale_ref[...] * (
        grad_normed - normed * jnp.mean(grad_normed * normed, axis=-1, keepdims=True)
    )
    grad_output = split(grad_output, 2)
    query_scaled = split(query * rising, 2)
    key_scaled = split(key * falling, 2)
    pairs = product(grad_output, [value], 1, 1)
    pairs = split(jnp.where(lower_mask(cumul.shape[0]), pairs, 0.0), 2)
    grad_query = rising * (
        product(pairs, key_scaled, 1, 0) + product(grad_output, split(state_ref[...], 2), 1, 1)
    )
    grad_query_ref[0] = grad_query.astype(BF16)
    grad_key = falling * product(pairs, query_scaled, 0, 0)
    grad_key_ref[...] = grad_key
    grad_value_ref[...] = product(split(scores_ref[...], 2), grad_output, 0, 0)
    gate = query * grad_query - key * grad_key
    gate_ref[...] = gate
    width = query.shape[1]
    sent_ref[:width] = product(query_scaled, grad_output, 0, 0)
    sent_ref[width:] = jnp.broadcast_to(
        jnp.sum(gate, axis=0, keepdims=True), (sent_ref.shape[0] - width, width)
    )


def finish_kernel(
    packed_ref, cumul_ref, grad_key_ref, grad_value_ref, gate_ref, later_ref,
    key_out_ref, value_out_ref, decay_out_ref,
):
    key = packed_ref[1]
    cumul = cumul_ref[...]
    width = key.shape[1]
    to_end = jnp.exp(cumul[-1:] - cumul)
    last = lax.axis_index("ctx") == lax.axis_size("ctx") - 1
    later = jnp.where(last, 0.0, later_ref[...])
    grad_in = split(later[:width], 2)
    extra = to_end * product([packed_ref[2].astype(BF16)], grad_in, 1, 1)
    key_out_ref[0] = (grad_key_ref[...] + extra).astype(BF16)
    grad_value = grad_value_ref[...] + product(split(key * to_end, 2), grad_in, 1, 0)
    value_out_ref[0] = grad_value.astype(BF16)
    gate = gate_ref[...] - key * extra
    lower = lower_mask(cumul.shape[0]).astype(F32).astype(BF16)
    decay_out_ref[0] = product([lower], split(gate, 3), 0, 0) + later[width:width + 1]


def local_call(kernel, shapes, *operands, name, flops, scratch=(), space=pltpu.VMEM, limit=VMEM_BYTES):
    outs = [jax.ShapeDtypeStruct(shape, dtype) for shape, dtype in shapes]
    moved = sum(array.size * array.dtype.itemsize for array in [*operands, *outs])
    return pl.pallas_call(
        kernel,
        out_shape=outs,
        in_specs=[pl.BlockSpec(memory_space=space)] * len(operands),
        scratch_shapes=list(scratch),
        compiler_params=pltpu.CompilerParams(vmem_limit_bytes=limit),
        cost_estimate=pl.CostEstimate(flops=flops, bytes_accessed=moved, transcendentals=0),
        name=name,
    )(*operands)


def swap(value):
    return lax.ppermute(value, "ctx", [(0, 1), (1, 0)])


def halving_plan(count, rows):
    rest = list(range(3, count.bit_length() - 2))
    last = rows // 32 * 16
    return [
        (rows - last, ([0, 2, 1] + rest, [1, 2, 0] + rest)),
        (last, ([0, 1, 2] + rest, [2, 1, 0] + rest)),
    ]


def relative(place, order):
    top = len(order) - 1
    return sum(((place >> (top - step)) & 1) << bit for step, bit in enumerate(order))


def lower_kernel(lower_ref):
    lower_ref[...] = lower_mask(lower_ref.shape[0]).astype(F32).astype(BF16)


def turn_kernel(count, plan, upstream_ref, own_ref, first_ref, second_ref, turned):
    me, core = lax.axis_index("dp"), lax.axis_index("ctx")
    model = turned.shape[0]
    lanes = 128
    for start in range(0, model, lanes):
        turned[start:start + lanes] = jnp.transpose(upstream_ref[0, :, start:start + lanes].astype(F32))
    share = model // count
    places = count // 2
    at = 0
    for ref, part in ((first_ref, range(places // 2, places)), (second_ref, range(places // 2))):
        offset = sent = 0
        for rows, orders in plan:
            for place in part:
                masks = [relative(place, orders[0]), relative(place, orders[1]) + places]
                mine = me ^ (masks[0] + core * (masks[1] - masks[0]))
                other = me ^ (masks[1] + core * (masks[0] - masks[1]))
                begin = pl.multiple_of(mine * share + offset, 16)
                own_ref[at:at + rows] = turned[pl.ds(begin, rows)].astype(BF16)
                begin = pl.multiple_of(other * share + offset, 16)
                ref[sent:sent + rows] = turned[pl.ds(begin, rows)]
                at += rows
                sent += rows
            offset += rows


def joined(pairs, left_axis, right_axis):
    lefts, rights = [], []
    for left, left_parts, right, right_parts in pairs:
        left, right = split(left, left_parts), split(right, right_parts)
        for i in range(left_parts):
            for j in range(right_parts):
                if i + j < max(left_parts, right_parts):
                    lefts.append(left[i])
                    rights.append(right[j])
    return lax.dot_general(
        jnp.concatenate(lefts, axis=left_axis),
        jnp.concatenate(rights, axis=right_axis),
        (((left_axis,), (right_axis,)), ((), ())),
        preferred_element_type=F32,
    )


def joint_kernel(
    own_ref, other_ref, lower_ref,
    cumul_ref, scores_ref, state_ref, normed_ref, scale_ref, rounded_ref,
):
    first = lax.axis_index("ctx") == 0
    length, width = cumul_ref.shape
    lower = lower_mask(length)

    def normalized(output):
        scale_inv = lax.rsqrt(jnp.mean(output * output, axis=-1, keepdims=True) + EPSILON)
        normed = output * scale_inv
        return normed, jnp.broadcast_to(scale_inv, normed.shape), normed.astype(BF16)

    query, key, value, decay = [
        [jnp.where(first, own_ref[i], other_ref[i]), jnp.where(first, other_ref[i], own_ref[i])]
        for i in range(4)
    ]
    cumuls = joined([(lower_ref[...], 1, jnp.concatenate(decay, axis=1), 3)], 1, 0)
    cumul = [cumuls[:, :width], cumuls[:, width:]]
    scaled = [q * jnp.exp(c) for q, c in zip(query, cumul)]
    scores = [
        jnp.where(lower, joined([(q, 2, k * jnp.exp(-c), 2)], 1, 1), 0.0)
        for q, k, c in zip(scaled, key, cumul)
    ]
    to_end = jnp.exp(cumul[0][-1:] - cumul[0])
    state = joined([(key[0] * to_end, 2, value[0], 1)], 0, 0)
    early = normalized(joined([(scores[0], 2, value[0], 1)], 1, 0))
    late = normalized(joined([(scores[1], 2, value[1], 1), (scaled[1], 2, state, 2)], 1, 0))
    rounded_ref[:length] = jnp.where(first, early[2], late[2])
    rounded_ref[length:] = jnp.where(first, late[2], early[2])
    cumul_ref[...] = jnp.where(first, cumul[0], cumul[1])
    scores_ref[...] = jnp.where(first, scores[0], scores[1])
    state_ref[...] = jnp.where(first, 0.0, state)
    normed_ref[...] = jnp.where(first, early[0], late[0])
    scale_ref[...] = jnp.where(first, early[1], late[1])


def share_kernel(begin, own_ref, received_ref, rounded_ref, *outs):
    at = 0
    for out in outs:
        rows = out.shape[0]
        left = jnp.concatenate(
            [own_ref[begin + at:begin + at + rows], received_ref[at:at + rows].astype(BF16)], axis=1
        )
        out[...] = jnp.dot(left, rounded_ref[...], preferred_element_type=F32)
        at += rows


def exchanged(value, count, bits):
    pairs = [
        (device * 2 + core, (device ^ (1 << bits[core])) * 2 + core)
        for device in range(count)
        for core in range(2)
    ]
    return lax.ppermute(value, BOTH, pairs)


def halving(kept, sent, plan, count, beside):
    stages = len(plan[0][1][0])
    joined = 3
    for stage in range(joined):
        arrived = [
            exchanged(part, count, [order[stage] for order in orders])
            for part, (_, orders) in zip(sent, plan)
        ]
        if stage in beside:
            arrived = beside[stage](arrived)
        half = [len(part) // 2 if stage + 1 < stages else len(part) for part in kept]
        sums = [
            (old[:size] + new[:size], old[size:] + new[size:])
            for old, new, size in zip(kept, arrived, half)
        ]
        kept = [pair[0] for pair in sums]
        sent = [pair[1] for pair in sums]
    for stage in range(joined, stages):
        sizes = [len(part) for part in sent]
        new = exchanged(jnp.concatenate(sent), count, [stage] * 2)
        if stage in beside:
            new = beside[stage](new)
        starts = [sum(sizes[:index]) for index in range(len(sizes))]
        sums = [part + new[at:at + size] for part, at, size in zip(kept, starts, sizes)]
        kept = [part[: len(part) // 2] if stage + 1 < stages else part for part in sums]
        sent = [part[len(part) // 2:] for part in sums]
    return jnp.concatenate(kept)


def pick_kernel(near_ref, far_ref, out_ref):
    out_ref[...] = jnp.where(lax.axis_index("ctx") == 0, near_ref[...], far_ref[...])


def add_kernel(mine_ref, theirs_ref, out_ref):
    out_ref[...] = mine_ref[...] + theirs_ref[...]


def shifted(value, axis, steps):
    count = lax.axis_size(axis)
    leading, last = (max(0, -steps), min(count, count - steps))
    return lax.ppermute(value, axis, [(source, source + steps) for source in range(leading, last)])


def body(queries, key_vectors, value_vectors, log_decay, out_weight, cotangent):
    length, width = queries.shape[1:]
    model = cotangent.shape[2]
    shards, count = lax.axis_size("ctx"), lax.axis_size("dp")
    square = (length, width)
    rows = model // count
    flops = 8 * length * width * model
    paired = shards == 2 and count >= 16 and count & (count - 1) == 0 and rows % 32 == 0

    (lower,) = local_call(lower_kernel, [((length, length), BF16)], name="lower", flops=20 * flops)
    inputs = (queries, key_vectors, value_vectors, log_decay)
    *inputs, lower = lax.optimization_barrier((*inputs, lower))
    packed = jnp.concatenate([jnp.concatenate(inputs[:3]).astype(F32), inputs[3]])
    if paired:
        plan = halving_plan(count, rows)
        part_rows = rows * count // 4
        own, send_first, send_second = local_call(
            functools.partial(turn_kernel, count, plan),
            [((2 * part_rows, length), BF16), ((part_rows, length), F32), ((part_rows, length), F32)],
            cotangent,
            name="turn", flops=20 * flops,
            scratch=[pltpu.VMEM((model, length), F32)],
        )
        others = swap(packed)
        received_first = swap(send_first)
        cumul, scores, state_in, normed, scale_inv, rounded = local_call(
            joint_kernel,
            [
                (square, F32), ((length, length), F32), ((width, width), F32), (square, F32),
                (square, F32), ((2 * length, width), BF16),
            ],
            packed, others, lower,
            name="joint", flops=40 * flops,
        )
        rounded, send_second = lax.optimization_barrier((rounded, send_second))
        received_second = swap(send_second)
        sent = local_call(
            functools.partial(share_kernel, 0),
            [((count // 4 * part, width), F32) for part, _ in plan],
            own, received_first, rounded,
            name="sent_shares", flops=flops // 4,
        )
        kept = local_call(
            functools.partial(share_kernel, part_rows),
            [((count // 4 * part, width), F32) for part, _ in plan],
            own, received_second, rounded,
            name="kept_shares", flops=flops // 4,
        )
    else:
        (local_state,) = local_call(
            state_kernel, [((width, width), F32)], key_vectors, value_vectors, log_decay,
            name="state", flops=flops // 2,
        )
        state_in = shifted(local_state, "ctx", 1)
        within, scores, cumul = local_call(
            within_kernel,
            [(square, F32), ((length, length), F32), (square, F32)],
            queries, key_vectors, value_vectors, log_decay,
            name="within", flops=flops // 2,
        )
        device_decay = jnp.exp(cumul[-1])[:, None]
        for _ in range(shards - 2):
            state_in = shifted(local_state + device_decay * state_in, "ctx", 1)
        normed, scale_inv, rounded = local_call(
            normed_kernel, [(square, F32)] * 3, queries, cumul, within, state_in,
            name="normed", flops=flops // 4,
        )

    grad_query, grad_key_zero, grad_value_zero, gate, grad_sent = local_call(
        grads_kernel,
        [
            (queries.shape, BF16), (square, F32), (square, F32), (square, F32),
            ((width + 8, width), F32),
        ],
        packed, cumul, scores, state_in, normed, scale_inv,
        cotangent, out_weight,
        name="grads", flops=2 * flops,
    )
    later = swap(grad_sent) if paired else shifted(grad_sent, "ctx", -1)

    def finish(later):
        return local_call(
            finish_kernel,
            [(queries.shape, BF16), (queries.shape, BF16), (queries.shape, F32)],
            packed, cumul, grad_key_zero, grad_value_zero, gate, later,
            name="finish", flops=flops,
        )

    if paired:
        held = {}

        def beside_first(arrived):
            large, small = arrived
            small, held["query"] = lax.optimization_barrier((small, grad_query))
            return [large, small]

        def beside_third(arrived):
            large, small = arrived
            large, held["later"] = lax.optimization_barrier((large, later))
            return [large, small]

        beside = {0: beside_first, 2: beside_third}
        near = halving(kept, sent, plan, count, beside)
        far = lax.ppermute(
            near, BOTH, [(device * 2 + 1, (device ^ (count // 2)) * 2 + 1) for device in range(count)]
        )
        grad_key, grad_value, grad_decay = finish(held["later"])
        far, grad_decay = lax.optimization_barrier((far, grad_decay))
        (mine,) = local_call(
            pick_kernel, [((rows, width), F32)], near, far, name="pick", flops=flops // 4
        )
        (grad_weight,) = local_call(
            add_kernel, [((rows, width), F32)], mine, swap(mine), name="add", flops=flops // 4
        )
        grad_query = held["query"]
    else:
        for _ in range(shards - 2):
            grad_in = later[:width]
            own_sum = grad_sent[width:] - jnp.sum(grad_in * local_state, axis=-1)[None]
            later = shifted(
                jnp.concatenate([grad_sent[:width] + device_decay * grad_in, own_sum + later[width:]]),
                "ctx",
                -1,
            )
        grad_key, grad_value, grad_decay = finish(later)
        share = jnp.einsum(
            "td,tk->dk", cotangent[0], rounded.astype(BF16), preferred_element_type=F32
        )
        share = lax.psum_scatter(share, "dp", scatter_dimension=0, tiled=True)
        grad_weight = lax.psum(share, "ctx")

    return grad_query, grad_key, grad_value, grad_decay, grad_weight


def solution(mesh):
    placed = (
        P("dp", "ctx", None),
        P("dp", "ctx", None),
        P("dp", "ctx", None),
        P("dp", "ctx", None),
        P(),
        P("dp", "ctx", None),
    )
    return jax.shard_map(
        body,
        mesh=mesh,
        in_specs=placed,
        out_specs=(
            P("dp", "ctx", None),
            P("dp", "ctx", None),
            P("dp", "ctx", None),
            P("dp", "ctx", None),
            P("dp", None),
        ),
        check_vma=False,
    )
```

```python
import functools

import jax
import jax.numpy as jnp
from jax import lax
from jax.experimental import pallas as pl
from jax.experimental.pallas import tpu as pltpu
from jax.sharding import PartitionSpec as P

EPSILON = 1e-05
VMEM_BYTES = 24 * 1024 * 1024
F32 = jnp.float32
BF16 = jnp.bfloat16
BOTH = ("dp", "ctx")


def split(value, parts):
    if value.dtype == BF16:
        return [value]
    pieces = []
    for index in range(parts):
        piece = value.astype(BF16)
        pieces.append(piece)
        if index + 1 < parts:
            value = value - piece.astype(F32)
    return pieces


def product(left, right, left_axis, right_axis):
    dims = (((left_axis,), (right_axis,)), ((), ()))
    most = max(len(left), len(right))
    total = None
    for order in reversed(range(most)):
        for i, l in enumerate(left):
            j = order - i
            if 0 <= j < len(right):
                term = lax.dot_general(l, right[j], dims, preferred_element_type=F32)
                total = term if total is None else total + term
    return total


def lower_mask(length):
    rows = lax.broadcasted_iota(jnp.int32, (length, length), 0)
    columns = lax.broadcasted_iota(jnp.int32, (length, length), 1)
    return rows >= columns


def cumulate(decay):
    lower = lower_mask(decay.shape[0]).astype(F32).astype(BF16)
    return product([lower], split(decay, 3), 1, 0)


def state_kernel(key_ref, value_ref, decay_ref, state_ref):
    cumul = cumulate(decay_ref[0])
    to_end = jnp.exp(cumul[-1:] - cumul)
    key_to_end = key_ref[0].astype(F32) * to_end
    state_ref[...] = product(split(key_to_end, 2), [value_ref[0]], 0, 0)


def within_kernel(query_ref, key_ref, value_ref, decay_ref, within_ref, scores_ref, cumul_ref):
    cumul = cumulate(decay_ref[0])
    cumul_ref[...] = cumul
    query_scaled = query_ref[0].astype(F32) * jnp.exp(cumul)
    key_scaled = key_ref[0].astype(F32) * jnp.exp(-cumul)
    scores = product(split(query_scaled, 2), split(key_scaled, 2), 1, 1)
    scores = jnp.where(lower_mask(cumul.shape[0]), scores, 0.0)
    scores_ref[...] = scores
    within_ref[...] = product(split(scores, 2), [value_ref[0]], 1, 0)


def normed_kernel(query_ref, cumul_ref, within_ref, state_ref, normed_ref, scale_ref, rounded_ref):
    query_scaled = query_ref[0].astype(F32) * jnp.exp(cumul_ref[...])
    output = within_ref[...] + product(split(query_scaled, 2), split(state_ref[...], 2), 1, 0)
    scale_inv = lax.rsqrt(jnp.mean(output * output, axis=-1, keepdims=True) + EPSILON)
    normed = output * scale_inv
    normed_ref[...] = normed
    scale_ref[...] = jnp.broadcast_to(scale_inv, normed.shape)
    rounded_ref[...] = normed.astype(BF16).astype(F32)


def grads_kernel(
    packed_ref, cumul_ref, scores_ref, state_ref, normed_ref, scale_ref,
    upstream_ref, weight_ref,
    grad_query_ref, grad_key_ref, grad_value_ref, gate_ref, sent_ref,
):
    query = packed_ref[0]
    key = packed_ref[1]
    value = packed_ref[2].astype(BF16)
    cumul = cumul_ref[...]
    rising = jnp.exp(cumul)
    falling = jnp.exp(-cumul)
    normed = normed_ref[...]
    grad_normed = jnp.dot(upstream_ref[0], weight_ref[...], preferred_element_type=F32)
    grad_output = scale_ref[...] * (
        grad_normed - normed * jnp.mean(grad_normed * normed, axis=-1, keepdims=True)
    )
    grad_output = split(grad_output, 2)
    query_scaled = split(query * rising, 2)
    key_scaled = split(key * falling, 2)
    pairs = product(grad_output, [value], 1, 1)
    pairs = split(jnp.where(lower_mask(cumul.shape[0]), pairs, 0.0), 2)
    grad_query = rising * (
        product(pairs, key_scaled, 1, 0) + product(grad_output, split(state_ref[...], 2), 1, 1)
    )
    grad_query_ref[0] = grad_query.astype(BF16)
    grad_key = falling * product(pairs, query_scaled, 0, 0)
    grad_key_ref[...] = grad_key
    grad_value_ref[...] = product(split(scores_ref[...], 2), grad_output, 0, 0)
    gate = query * grad_query - key * grad_key
    gate_ref[...] = gate
    width = query.shape[1]
    sent_ref[:width] = product(query_scaled, grad_output, 0, 0)
    sent_ref[width:] = jnp.broadcast_to(
        jnp.sum(gate, axis=0, keepdims=True), (sent_ref.shape[0] - width, width)
    )


def finish_kernel(
    packed_ref, cumul_ref, grad_key_ref, grad_value_ref, gate_ref, later_ref,
    key_out_ref, value_out_ref, decay_out_ref,
):
    key = packed_ref[1]
    cumul = cumul_ref[...]
    width = key.shape[1]
    to_end = jnp.exp(cumul[-1:] - cumul)
    last = lax.axis_index("ctx") == lax.axis_size("ctx") - 1
    later = jnp.where(last, 0.0, later_ref[...])
    grad_in = split(later[:width], 2)
    extra = to_end * product([packed_ref[2].astype(BF16)], grad_in, 1, 1)
    key_out_ref[0] = (grad_key_ref[...] + extra).astype(BF16)
    grad_value = grad_value_ref[...] + product(split(key * to_end, 2), grad_in, 1, 0)
    value_out_ref[0] = grad_value.astype(BF16)
    gate = gate_ref[...] - key * extra
    lower = lower_mask(cumul.shape[0]).astype(F32).astype(BF16)
    decay_out_ref[0] = product([lower], split(gate, 3), 0, 0) + later[width:width + 1]


def local_call(kernel, shapes, *operands, name, flops, scratch=(), space=pltpu.VMEM, limit=VMEM_BYTES):
    outs = [jax.ShapeDtypeStruct(shape, dtype) for shape, dtype in shapes]
    moved = sum(array.size * array.dtype.itemsize for array in [*operands, *outs])
    return pl.pallas_call(
        kernel,
        out_shape=outs,
        in_specs=[pl.BlockSpec(memory_space=space)] * len(operands),
        scratch_shapes=list(scratch),
        compiler_params=pltpu.CompilerParams(vmem_limit_bytes=limit),
        cost_estimate=pl.CostEstimate(flops=flops, bytes_accessed=moved, transcendentals=0),
        name=name,
    )(*operands)


def swap(value):
    return lax.ppermute(value, "ctx", [(0, 1), (1, 0)])


def halving_plan(count, rows):
    bits = count.bit_length() - 1
    last = rows // 32 * 16
    rest = list(range(3, bits))
    return [
        (rows - last, ([0, 1, 2] + rest, [1, 0, 2] + rest)),
        (last, ([2, 0, 1] + rest, [1, 2, 0] + rest)),
    ]


def relative(place, order):
    top = len(order) - 1
    return sum(((place >> (top - step)) & 1) << bit for step, bit in enumerate(order))


def lower_kernel(lower_ref):
    lower_ref[...] = lower_mask(lower_ref.shape[0]).astype(F32).astype(BF16)


def rows_of(count, plan, me, core, part, share):
    half = share // 2
    offset = 0
    for rows, orders in plan:
        for place in part:
            masks = [relative(place, order) for order in orders]
            owner = me ^ (masks[0] + core * (masks[1] - masks[0]))
            yield pl.multiple_of(owner * share + core * half + offset, 16), rows
        offset += rows


def turn_kernel(count, plan, upstream_ref, turned_ref, first_ref):
    me, core = lax.axis_index("dp"), lax.axis_index("ctx")
    model = turned_ref.shape[0]
    lanes = 128
    for start in range(0, model, lanes):
        turned_ref[start:start + lanes] = jnp.transpose(
            upstream_ref[0, :, start:start + lanes].astype(F32)
        )
    at = 0
    for begin, rows in rows_of(count, plan, me, 1 - core, range(count // 2, count), model // count):
        first_ref[at:at + rows] = turned_ref[pl.ds(begin, rows)]
        at += rows


def rest_kernel(count, plan, turned_ref, own_ref, second_ref):
    me, core = lax.axis_index("dp"), lax.axis_index("ctx")
    share = turned_ref.shape[0] // count
    at = 0
    for part in (range(count // 2, count), range(count // 2)):
        for begin, rows in rows_of(count, plan, me, core, part, share):
            own_ref[at:at + rows] = turned_ref[pl.ds(begin, rows)].astype(BF16)
            at += rows
    at = 0
    for begin, rows in rows_of(count, plan, me, 1 - core, range(count // 2), share):
        second_ref[at:at + rows] = turned_ref[pl.ds(begin, rows)]
        at += rows


def joined(pairs, left_axis, right_axis):
    lefts, rights = [], []
    for left, left_parts, right, right_parts in pairs:
        left, right = split(left, left_parts), split(right, right_parts)
        for i in range(left_parts):
            for j in range(right_parts):
                if i + j < max(left_parts, right_parts):
                    lefts.append(left[i])
                    rights.append(right[j])
    return lax.dot_general(
        jnp.concatenate(lefts, axis=left_axis),
        jnp.concatenate(rights, axis=right_axis),
        (((left_axis,), (right_axis,)), ((), ())),
        preferred_element_type=F32,
    )


def joint_kernel(
    own_ref, other_ref, lower_ref,
    cumul_ref, scores_ref, state_ref, normed_ref, scale_ref, rounded_ref,
):
    first = lax.axis_index("ctx") == 0
    length, width = cumul_ref.shape
    lower = lower_mask(length)

    def normalized(output):
        scale_inv = lax.rsqrt(jnp.mean(output * output, axis=-1, keepdims=True) + EPSILON)
        normed = output * scale_inv
        return normed, jnp.broadcast_to(scale_inv, normed.shape), normed.astype(BF16)

    query, key, value, decay = [
        [jnp.where(first, own_ref[i], other_ref[i]), jnp.where(first, other_ref[i], own_ref[i])]
        for i in range(4)
    ]
    cumuls = joined([(lower_ref[...], 1, jnp.concatenate(decay, axis=1), 3)], 1, 0)
    cumul = [cumuls[:, :width], cumuls[:, width:]]
    scaled = [q * jnp.exp(c) for q, c in zip(query, cumul)]
    scores = [
        jnp.where(lower, joined([(q, 2, k * jnp.exp(-c), 2)], 1, 1), 0.0)
        for q, k, c in zip(scaled, key, cumul)
    ]
    to_end = jnp.exp(cumul[0][-1:] - cumul[0])
    state = joined([(key[0] * to_end, 2, value[0], 1)], 0, 0)
    early = normalized(joined([(scores[0], 2, value[0], 1)], 1, 0))
    late = normalized(joined([(scores[1], 2, value[1], 1), (scaled[1], 2, state, 2)], 1, 0))
    rounded_ref[:length] = jnp.where(first, early[2], late[2])
    rounded_ref[length:] = jnp.where(first, late[2], early[2])
    cumul_ref[...] = jnp.where(first, cumul[0], cumul[1])
    scores_ref[...] = jnp.where(first, scores[0], scores[1])
    state_ref[...] = jnp.where(first, 0.0, state)
    normed_ref[...] = jnp.where(first, early[0], late[0])
    scale_ref[...] = jnp.where(first, early[1], late[1])


def share_kernel(begin, own_ref, received_ref, rounded_ref, *outs):
    at = 0
    for out in outs:
        rows = out.shape[0]
        left = jnp.concatenate(
            [own_ref[begin + at:begin + at + rows], received_ref[at:at + rows].astype(BF16)], axis=1
        )
        out[...] = jnp.dot(left, rounded_ref[...], preferred_element_type=F32)
        at += rows


def exchanged(value, count, bits):
    pairs = [
        (device * 2 + core, (device ^ (1 << bits[core])) * 2 + core)
        for device in range(count)
        for core in range(2)
    ]
    return lax.ppermute(value, BOTH, pairs)


def halving(kept, sent, plan, count, beside):
    stages = len(plan[0][1][0])
    joined = 3
    for stage in range(joined):
        arrived = [
            exchanged(part, count, [order[stage] for order in orders])
            for part, (_, orders) in zip(sent, plan)
        ]
        if stage in beside:
            arrived = beside[stage](arrived)
        half = [len(part) // 2 if stage + 1 < stages else len(part) for part in kept]
        sums = [
            (old[:size] + new[:size], old[size:] + new[size:])
            for old, new, size in zip(kept, arrived, half)
        ]
        kept = [pair[0] for pair in sums]
        sent = [pair[1] for pair in sums]
    for stage in range(joined, stages):
        sizes = [len(part) for part in sent]
        new = exchanged(jnp.concatenate(sent), count, [stage] * 2)
        if stage in beside:
            new = beside[stage](new)
        starts = [sum(sizes[:index]) for index in range(len(sizes))]
        sums = [part + new[at:at + size] for part, at, size in zip(kept, starts, sizes)]
        kept = [part[: len(part) // 2] if stage + 1 < stages else part for part in sums]
        sent = [part[len(part) // 2:] for part in sums]
    return jnp.concatenate(kept)


def assemble_kernel(mine_ref, theirs_ref, out_ref):
    core = lax.axis_index("ctx")
    rows = mine_ref.shape[0]
    out_ref[pl.ds(pl.multiple_of(core * rows, 8), rows)] = mine_ref[...]
    out_ref[pl.ds(pl.multiple_of((1 - core) * rows, 8), rows)] = theirs_ref[...]


def shifted(value, axis, steps):
    count = lax.axis_size(axis)
    leading, last = (max(0, -steps), min(count, count - steps))
    return lax.ppermute(value, axis, [(source, source + steps) for source in range(leading, last)])


def body(queries, key_vectors, value_vectors, log_decay, out_weight, cotangent):
    length, width = queries.shape[1:]
    model = cotangent.shape[2]
    shards, count = lax.axis_size("ctx"), lax.axis_size("dp")
    square = (length, width)
    rows = model // count // 2
    flops = 8 * length * width * model
    paired = shards == 2 and count >= 16 and count & (count - 1) == 0 and rows % 16 == 0

    (lower,) = local_call(lower_kernel, [((length, length), BF16)], name="lower", flops=20 * flops)
    inputs = (queries, key_vectors, value_vectors, log_decay)
    *inputs, lower = lax.optimization_barrier((*inputs, lower))
    packed = jnp.concatenate([jnp.concatenate(inputs[:3]).astype(F32), inputs[3]])
    if paired:
        plan = halving_plan(count, rows)
        part_rows = rows * count // 2
        turned, send_first = local_call(
            functools.partial(turn_kernel, count, plan),
            [((model, length), F32), ((part_rows, length), F32)],
            cotangent,
            name="turn", flops=20 * flops,
        )
        own, send_second = local_call(
            functools.partial(rest_kernel, count, plan),
            [((2 * part_rows, length), BF16), ((part_rows, length), F32)],
            turned,
            name="rest", flops=flops,
        )
        others = swap(packed)
        received_first = swap(send_first)
        cumul, scores, state_in, normed, scale_inv, rounded = local_call(
            joint_kernel,
            [
                (square, F32), ((length, length), F32), ((width, width), F32), (square, F32),
                (square, F32), ((2 * length, width), BF16),
            ],
            packed, others, lower,
            name="joint", flops=40 * flops,
        )
        rounded, send_second = lax.optimization_barrier((rounded, send_second))
        received_second = swap(send_second)
        sent = local_call(
            functools.partial(share_kernel, 0),
            [((count // 2 * part, width), F32) for part, _ in plan],
            own, received_first, rounded,
            name="sent_shares", flops=flops // 4,
        )
        kept = local_call(
            functools.partial(share_kernel, part_rows),
            [((count // 2 * part, width), F32) for part, _ in plan],
            own, received_second, rounded,
            name="kept_shares", flops=flops // 4,
        )
    else:
        (local_state,) = local_call(
            state_kernel, [((width, width), F32)], key_vectors, value_vectors, log_decay,
            name="state", flops=flops // 2,
        )
        state_in = shifted(local_state, "ctx", 1)
        within, scores, cumul = local_call(
            within_kernel,
            [(square, F32), ((length, length), F32), (square, F32)],
            queries, key_vectors, value_vectors, log_decay,
            name="within", flops=flops // 2,
        )
        device_decay = jnp.exp(cumul[-1])[:, None]
        for _ in range(shards - 2):
            state_in = shifted(local_state + device_decay * state_in, "ctx", 1)
        normed, scale_inv, rounded = local_call(
            normed_kernel, [(square, F32)] * 3, queries, cumul, within, state_in,
            name="normed", flops=flops // 4,
        )

    grad_query, grad_key_zero, grad_value_zero, gate, grad_sent = local_call(
        grads_kernel,
        [
            (queries.shape, BF16), (square, F32), (square, F32), (square, F32),
            ((width + 8, width), F32),
        ],
        packed, cumul, scores, state_in, normed, scale_inv,
        cotangent, out_weight,
        name="grads", flops=2 * flops,
    )
    later = swap(grad_sent) if paired else shifted(grad_sent, "ctx", -1)

    def finish(later):
        return local_call(
            finish_kernel,
            [(queries.shape, BF16), (queries.shape, BF16), (queries.shape, F32)],
            packed, cumul, grad_key_zero, grad_value_zero, gate, later,
            name="finish", flops=flops,
        )

    if paired:
        held = {}

        def beside_first(arrived):
            large, small = arrived
            large, held["query"] = lax.optimization_barrier((large, grad_query))
            return [large, small]

        def beside_third(arrived):
            large, small = arrived
            large, held["later"] = lax.optimization_barrier((large, later))
            return [large, small]

        def beside_last(arrived):
            key, value, decay = finish(held["later"])
            arrived, decay = lax.optimization_barrier((arrived, decay))
            held["finished"] = key, value, decay
            return arrived

        beside = {0: beside_first, 2: beside_third, 3: beside_last}
        mine = halving(kept, sent, plan, count, beside)
        grad_query = held["query"]
        grad_key, grad_value, grad_decay = held["finished"]
        (grad_weight,) = local_call(
            assemble_kernel, [((2 * rows, width), F32)], mine, swap(mine),
            name="assemble", flops=flops // 4,
        )
    else:
        for _ in range(shards - 2):
            grad_in = later[:width]
            own_sum = grad_sent[width:] - jnp.sum(grad_in * local_state, axis=-1)[None]
            later = shifted(
                jnp.concatenate([grad_sent[:width] + device_decay * grad_in, own_sum + later[width:]]),
                "ctx",
                -1,
            )
        grad_key, grad_value, grad_decay = finish(later)
        share = jnp.einsum(
            "td,tk->dk", cotangent[0], rounded.astype(BF16), preferred_element_type=F32
        )
        share = lax.psum_scatter(share, "dp", scatter_dimension=0, tiled=True)
        grad_weight = lax.psum(share, "ctx")

    return grad_query, grad_key, grad_value, grad_decay, grad_weight


def solution(mesh):
    placed = (
        P("dp", "ctx", None),
        P("dp", "ctx", None),
        P("dp", "ctx", None),
        P("dp", "ctx", None),
        P(),
        P("dp", "ctx", None),
    )
    return jax.shard_map(
        body,
        mesh=mesh,
        in_specs=placed,
        out_specs=(
            P("dp", "ctx", None),
            P("dp", "ctx", None),
            P("dp", "ctx", None),
            P("dp", "ctx", None),
            P("dp", None),
        ),
        check_vma=False,
    )
```

```python
import functools

import jax
import jax.numpy as jnp
from jax import lax
from jax.experimental import pallas as pl
from jax.experimental.pallas import tpu as pltpu
from jax.sharding import PartitionSpec as P

EPSILON = 1e-05
VMEM_BYTES = 24 * 1024 * 1024
F32 = jnp.float32
BF16 = jnp.bfloat16
BOTH = ("dp", "ctx")


def split(value, parts):
    if value.dtype == BF16:
        return [value]
    pieces = []
    for index in range(parts):
        piece = value.astype(BF16)
        pieces.append(piece)
        if index + 1 < parts:
            value = value - piece.astype(F32)
    return pieces


def product(left, right, left_axis, right_axis):
    dims = (((left_axis,), (right_axis,)), ((), ()))
    most = max(len(left), len(right))
    total = None
    for order in reversed(range(most)):
        for i, l in enumerate(left):
            j = order - i
            if 0 <= j < len(right):
                term = lax.dot_general(l, right[j], dims, preferred_element_type=F32)
                total = term if total is None else total + term
    return total


def lower_mask(length):
    rows = lax.broadcasted_iota(jnp.int32, (length, length), 0)
    columns = lax.broadcasted_iota(jnp.int32, (length, length), 1)
    return rows >= columns


def cumulate(decay):
    lower = lower_mask(decay.shape[0]).astype(F32).astype(BF16)
    return product([lower], split(decay, 3), 1, 0)


def state_kernel(key_ref, value_ref, decay_ref, state_ref):
    cumul = cumulate(decay_ref[0])
    to_end = jnp.exp(cumul[-1:] - cumul)
    key_to_end = key_ref[0].astype(F32) * to_end
    state_ref[...] = product(split(key_to_end, 2), [value_ref[0]], 0, 0)


def within_kernel(query_ref, key_ref, value_ref, decay_ref, within_ref, scores_ref, cumul_ref):
    cumul = cumulate(decay_ref[0])
    cumul_ref[...] = cumul
    query_scaled = query_ref[0].astype(F32) * jnp.exp(cumul)
    key_scaled = key_ref[0].astype(F32) * jnp.exp(-cumul)
    scores = product(split(query_scaled, 2), split(key_scaled, 2), 1, 1)
    scores = jnp.where(lower_mask(cumul.shape[0]), scores, 0.0)
    scores_ref[...] = scores
    within_ref[...] = product(split(scores, 2), [value_ref[0]], 1, 0)


def normed_kernel(query_ref, cumul_ref, within_ref, state_ref, normed_ref, scale_ref, rounded_ref):
    query_scaled = query_ref[0].astype(F32) * jnp.exp(cumul_ref[...])
    output = within_ref[...] + product(split(query_scaled, 2), split(state_ref[...], 2), 1, 0)
    scale_inv = lax.rsqrt(jnp.mean(output * output, axis=-1, keepdims=True) + EPSILON)
    normed = output * scale_inv
    normed_ref[...] = normed
    scale_ref[...] = jnp.broadcast_to(scale_inv, normed.shape)
    rounded_ref[...] = normed.astype(BF16).astype(F32)


def grads_kernel(
    packed_ref, cumul_ref, scores_ref, state_ref, normed_ref, scale_ref,
    upstream_ref, weight_ref,
    grad_query_ref, grad_key_ref, grad_value_ref, gate_ref, sent_ref,
):
    query = packed_ref[0]
    key = packed_ref[1]
    value = packed_ref[2].astype(BF16)
    cumul = cumul_ref[...]
    rising = jnp.exp(cumul)
    falling = jnp.exp(-cumul)
    normed = normed_ref[...]
    grad_normed = jnp.dot(upstream_ref[0], weight_ref[...], preferred_element_type=F32)
    grad_output = scale_ref[...] * (
        grad_normed - normed * jnp.mean(grad_normed * normed, axis=-1, keepdims=True)
    )
    grad_output = split(grad_output, 2)
    query_scaled = split(query * rising, 2)
    key_scaled = split(key * falling, 2)
    pairs = product(grad_output, [value], 1, 1)
    pairs = split(jnp.where(lower_mask(cumul.shape[0]), pairs, 0.0), 2)
    grad_query = rising * (
        product(pairs, key_scaled, 1, 0) + product(grad_output, split(state_ref[...], 2), 1, 1)
    )
    grad_query_ref[0] = grad_query.astype(BF16)
    grad_key = falling * product(pairs, query_scaled, 0, 0)
    grad_key_ref[...] = grad_key
    grad_value_ref[...] = product(split(scores_ref[...], 2), grad_output, 0, 0)
    gate = query * grad_query - key * grad_key
    gate_ref[...] = gate
    width = query.shape[1]
    sent_ref[:width] = product(query_scaled, grad_output, 0, 0)
    sent_ref[width:] = jnp.broadcast_to(
        jnp.sum(gate, axis=0, keepdims=True), (sent_ref.shape[0] - width, width)
    )


def finish_kernel(
    packed_ref, cumul_ref, grad_key_ref, grad_value_ref, gate_ref, later_ref,
    key_out_ref, value_out_ref, decay_out_ref,
):
    key = packed_ref[1]
    cumul = cumul_ref[...]
    width = key.shape[1]
    to_end = jnp.exp(cumul[-1:] - cumul)
    last = lax.axis_index("ctx") == lax.axis_size("ctx") - 1
    later = jnp.where(last, 0.0, later_ref[...])
    grad_in = split(later[:width], 2)
    extra = to_end * product([packed_ref[2].astype(BF16)], grad_in, 1, 1)
    key_out_ref[0] = (grad_key_ref[...] + extra).astype(BF16)
    grad_value = grad_value_ref[...] + product(split(key * to_end, 2), grad_in, 1, 0)
    value_out_ref[0] = grad_value.astype(BF16)
    gate = gate_ref[...] - key * extra
    lower = lower_mask(cumul.shape[0]).astype(F32).astype(BF16)
    decay_out_ref[0] = product([lower], split(gate, 3), 0, 0) + later[width:width + 1]


def local_call(kernel, shapes, *operands, name, flops, scratch=(), space=pltpu.VMEM, limit=VMEM_BYTES):
    outs = [jax.ShapeDtypeStruct(shape, dtype) for shape, dtype in shapes]
    moved = sum(array.size * array.dtype.itemsize for array in [*operands, *outs])
    return pl.pallas_call(
        kernel,
        out_shape=outs,
        in_specs=[pl.BlockSpec(memory_space=space)] * len(operands),
        scratch_shapes=list(scratch),
        compiler_params=pltpu.CompilerParams(vmem_limit_bytes=limit),
        cost_estimate=pl.CostEstimate(flops=flops, bytes_accessed=moved, transcendentals=0),
        name=name,
    )(*operands)


def swap(value):
    return lax.ppermute(value, "ctx", [(0, 1), (1, 0)])


def halving_plan(count, rows):
    bits = count.bit_length() - 1
    last = rows // 32 * 16
    rest = list(range(3, bits))
    return [
        (rows - last, ([0, 1, 2] + rest, [1, 0, 2] + rest)),
        (last, ([2, 0, 1] + rest, [1, 2, 0] + rest)),
    ]


def relative(place, order):
    top = len(order) - 1
    return sum(((place >> (top - step)) & 1) << bit for step, bit in enumerate(order))


def lower_kernel(lower_ref):
    lower_ref[...] = lower_mask(lower_ref.shape[0]).astype(F32).astype(BF16)


def rows_of(count, plan, me, core, part, share):
    half = share // 2
    offset = 0
    for rows, orders in plan:
        for place in part:
            masks = [relative(place, order) for order in orders]
            owner = me ^ (masks[0] + core * (masks[1] - masks[0]))
            yield pl.multiple_of(owner * share + core * half + offset, 16), rows
        offset += rows


def turn_kernel(count, plan, upstream_ref, turned_ref, first_ref):
    me, core = lax.axis_index("dp"), lax.axis_index("ctx")
    model = turned_ref.shape[0]
    lanes = 128
    for start in range(0, model, lanes):
        turned_ref[start:start + lanes] = jnp.transpose(
            upstream_ref[0, :, start:start + lanes].astype(F32)
        )
    at = 0
    for begin, rows in rows_of(count, plan, me, 1 - core, range(count // 2, count), model // count):
        first_ref[at:at + rows] = turned_ref[pl.ds(begin, rows)]
        at += rows


def rest_kernel(count, plan, turned_ref, own_ref, second_ref):
    me, core = lax.axis_index("dp"), lax.axis_index("ctx")
    share = turned_ref.shape[0] // count
    at = 0
    for part in (range(count // 2, count), range(count // 2)):
        for begin, rows in rows_of(count, plan, me, core, part, share):
            own_ref[at:at + rows] = turned_ref[pl.ds(begin, rows)].astype(BF16)
            at += rows
    at = 0
    for begin, rows in rows_of(count, plan, me, 1 - core, range(count // 2), share):
        second_ref[at:at + rows] = turned_ref[pl.ds(begin, rows)]
        at += rows


def joined(pairs, left_axis, right_axis):
    lefts, rights = [], []
    for left, left_parts, right, right_parts in pairs:
        left, right = split(left, left_parts), split(right, right_parts)
        for i in range(left_parts):
            for j in range(right_parts):
                if i + j < max(left_parts, right_parts):
                    lefts.append(left[i])
                    rights.append(right[j])
    return lax.dot_general(
        jnp.concatenate(lefts, axis=left_axis),
        jnp.concatenate(rights, axis=right_axis),
        (((left_axis,), (right_axis,)), ((), ())),
        preferred_element_type=F32,
    )


def joint_kernel(
    own_ref, other_ref, lower_ref,
    cumul_ref, scores_ref, state_ref, normed_ref, scale_ref, rounded_ref,
):
    first = lax.axis_index("ctx") == 0
    length, width = cumul_ref.shape
    lower = lower_mask(length)

    def normalized(output):
        scale_inv = lax.rsqrt(jnp.mean(output * output, axis=-1, keepdims=True) + EPSILON)
        normed = output * scale_inv
        return normed, jnp.broadcast_to(scale_inv, normed.shape), normed.astype(BF16)

    query, key, value, decay = [
        [jnp.where(first, own_ref[i], other_ref[i]), jnp.where(first, other_ref[i], own_ref[i])]
        for i in range(4)
    ]
    cumuls = joined([(lower_ref[...], 1, jnp.concatenate(decay, axis=1), 3)], 1, 0)
    cumul = [cumuls[:, :width], cumuls[:, width:]]
    scaled = [q * jnp.exp(c) for q, c in zip(query, cumul)]
    scores = [
        jnp.where(lower, joined([(q, 2, k * jnp.exp(-c), 2)], 1, 1), 0.0)
        for q, k, c in zip(scaled, key, cumul)
    ]
    to_end = jnp.exp(cumul[0][-1:] - cumul[0])
    state = joined([(key[0] * to_end, 2, value[0], 1)], 0, 0)
    early = normalized(joined([(scores[0], 2, value[0], 1)], 1, 0))
    late = normalized(joined([(scores[1], 2, value[1], 1), (scaled[1], 2, state, 2)], 1, 0))
    rounded_ref[:length] = jnp.where(first, early[2], late[2])
    rounded_ref[length:] = jnp.where(first, late[2], early[2])
    cumul_ref[...] = jnp.where(first, cumul[0], cumul[1])
    scores_ref[...] = jnp.where(first, scores[0], scores[1])
    state_ref[...] = jnp.where(first, 0.0, state)
    normed_ref[...] = jnp.where(first, early[0], late[0])
    scale_ref[...] = jnp.where(first, early[1], late[1])


def share_kernel(begin, own_ref, received_ref, rounded_ref, *outs):
    at = 0
    for out in outs:
        rows = out.shape[0]
        left = jnp.concatenate(
            [own_ref[begin + at:begin + at + rows], received_ref[at:at + rows].astype(BF16)], axis=1
        )
        out[...] = jnp.dot(left, rounded_ref[...], preferred_element_type=F32)
        at += rows


def own_part_kernel(own_ref, rounded_ref, *outs):
    at = 0
    for out in outs:
        rows = out.shape[0]
        out[...] = jnp.dot(
            own_ref[at:at + rows], rounded_ref[: rounded_ref.shape[0] // 2], preferred_element_type=F32
        )
        at += rows


def add_part_kernel(received_ref, rounded_ref, *refs):
    at = 0
    for part, out in zip(refs[: len(refs) // 2], refs[len(refs) // 2:]):
        rows = out.shape[0]
        out[...] = part[...] + jnp.dot(
            received_ref[at:at + rows].astype(BF16), rounded_ref[rounded_ref.shape[0] // 2:],
            preferred_element_type=F32,
        )
        at += rows


def exchanged(value, count, bits):
    pairs = [
        (device * 2 + core, (device ^ (1 << bits[core])) * 2 + core)
        for device in range(count)
        for core in range(2)
    ]
    return lax.ppermute(value, BOTH, pairs)


def halving(kept, sent, plan, count, beside):
    stages = len(plan[0][1][0])
    joined = 3
    for stage in range(joined):
        arrived = [
            exchanged(part, count, [order[stage] for order in orders])
            for part, (_, orders) in zip(sent, plan)
        ]
        if stage in beside:
            arrived = beside[stage](arrived)
        half = [len(part) // 2 if stage + 1 < stages else len(part) for part in kept]
        sums = [
            (old[:size] + new[:size], old[size:] + new[size:])
            for old, new, size in zip(kept, arrived, half)
        ]
        kept = [pair[0] for pair in sums]
        sent = [pair[1] for pair in sums]
    for stage in range(joined, stages):
        sizes = [len(part) for part in sent]
        new = exchanged(jnp.concatenate(sent), count, [stage] * 2)
        if stage in beside:
            new = beside[stage](new)
        starts = [sum(sizes[:index]) for index in range(len(sizes))]
        sums = [part + new[at:at + size] for part, at, size in zip(kept, starts, sizes)]
        kept = [part[: len(part) // 2] if stage + 1 < stages else part for part in sums]
        sent = [part[len(part) // 2:] for part in sums]
    return jnp.concatenate(kept)


def assemble_kernel(mine_ref, theirs_ref, out_ref):
    core = lax.axis_index("ctx")
    rows = mine_ref.shape[0]
    out_ref[pl.ds(pl.multiple_of(core * rows, 8), rows)] = mine_ref[...]
    out_ref[pl.ds(pl.multiple_of((1 - core) * rows, 8), rows)] = theirs_ref[...]


def shifted(value, axis, steps):
    count = lax.axis_size(axis)
    leading, last = (max(0, -steps), min(count, count - steps))
    return lax.ppermute(value, axis, [(source, source + steps) for source in range(leading, last)])


def body(queries, key_vectors, value_vectors, log_decay, out_weight, cotangent):
    length, width = queries.shape[1:]
    model = cotangent.shape[2]
    shards, count = lax.axis_size("ctx"), lax.axis_size("dp")
    square = (length, width)
    rows = model // count // 2
    flops = 8 * length * width * model
    paired = shards == 2 and count >= 16 and count & (count - 1) == 0 and rows % 16 == 0

    (lower,) = local_call(lower_kernel, [((length, length), BF16)], name="lower", flops=20 * flops)
    inputs = (queries, key_vectors, value_vectors, log_decay)
    *inputs, lower = lax.optimization_barrier((*inputs, lower))
    packed = jnp.concatenate([jnp.concatenate(inputs[:3]).astype(F32), inputs[3]])
    if paired:
        plan = halving_plan(count, rows)
        part_rows = rows * count // 2
        turned, send_first = local_call(
            functools.partial(turn_kernel, count, plan),
            [((model, length), F32), ((part_rows, length), F32)],
            cotangent,
            name="turn", flops=20 * flops,
        )
        own, send_second = local_call(
            functools.partial(rest_kernel, count, plan),
            [((2 * part_rows, length), BF16), ((part_rows, length), F32)],
            turned,
            name="rest", flops=flops,
        )
        others = swap(packed)
        received_first = swap(send_first)
        cumul, scores, state_in, normed, scale_inv, rounded = local_call(
            joint_kernel,
            [
                (square, F32), ((length, length), F32), ((width, width), F32), (square, F32),
                (square, F32), ((2 * length, width), BF16),
            ],
            packed, others, lower,
            name="joint", flops=40 * flops,
        )
        rounded, send_second = lax.optimization_barrier((rounded, send_second))
        received_second = swap(send_second)
        part_shapes = [((count // 2 * part, width), F32) for part, _ in plan]
        own_part = local_call(
            own_part_kernel, part_shapes, own, rounded, name="own_part", flops=flops // 4
        )
        sent = local_call(
            add_part_kernel, part_shapes, received_first, rounded, *own_part,
            name="sent_shares", flops=flops // 4,
        )
        kept = local_call(
            functools.partial(share_kernel, part_rows),
            [((count // 2 * part, width), F32) for part, _ in plan],
            own, received_second, rounded,
            name="kept_shares", flops=flops // 4,
        )
    else:
        (local_state,) = local_call(
            state_kernel, [((width, width), F32)], key_vectors, value_vectors, log_decay,
            name="state", flops=flops // 2,
        )
        state_in = shifted(local_state, "ctx", 1)
        within, scores, cumul = local_call(
            within_kernel,
            [(square, F32), ((length, length), F32), (square, F32)],
            queries, key_vectors, value_vectors, log_decay,
            name="within", flops=flops // 2,
        )
        device_decay = jnp.exp(cumul[-1])[:, None]
        for _ in range(shards - 2):
            state_in = shifted(local_state + device_decay * state_in, "ctx", 1)
        normed, scale_inv, rounded = local_call(
            normed_kernel, [(square, F32)] * 3, queries, cumul, within, state_in,
            name="normed", flops=flops // 4,
        )

    grad_query, grad_key_zero, grad_value_zero, gate, grad_sent = local_call(
        grads_kernel,
        [
            (queries.shape, BF16), (square, F32), (square, F32), (square, F32),
            ((width + 8, width), F32),
        ],
        packed, cumul, scores, state_in, normed, scale_inv,
        cotangent, out_weight,
        name="grads", flops=2 * flops,
    )
    later = swap(grad_sent) if paired else shifted(grad_sent, "ctx", -1)

    def finish(later):
        return local_call(
            finish_kernel,
            [(queries.shape, BF16), (queries.shape, BF16), (queries.shape, F32)],
            packed, cumul, grad_key_zero, grad_value_zero, gate, later,
            name="finish", flops=flops,
        )

    if paired:
        held = {}

        def beside_first(arrived):
            large, small = arrived
            large, held["query"] = lax.optimization_barrier((large, grad_query))
            return [large, small]

        def beside_third(arrived):
            large, small = arrived
            large, held["later"] = lax.optimization_barrier((large, later))
            return [large, small]

        def beside_last(arrived):
            key, value, decay = finish(held["later"])
            arrived, decay = lax.optimization_barrier((arrived, decay))
            held["finished"] = key, value, decay
            return arrived

        beside = {0: beside_first, 2: beside_third, 3: beside_last}
        mine = halving(kept, sent, plan, count, beside)
        grad_query = held["query"]
        grad_key, grad_value, grad_decay = held["finished"]
        (grad_weight,) = local_call(
            assemble_kernel, [((2 * rows, width), F32)], mine, swap(mine),
            name="assemble", flops=flops // 4,
        )
    else:
        for _ in range(shards - 2):
            grad_in = later[:width]
            own_sum = grad_sent[width:] - jnp.sum(grad_in * local_state, axis=-1)[None]
            later = shifted(
                jnp.concatenate([grad_sent[:width] + device_decay * grad_in, own_sum + later[width:]]),
                "ctx",
                -1,
            )
        grad_key, grad_value, grad_decay = finish(later)
        share = jnp.einsum(
            "td,tk->dk", cotangent[0], rounded.astype(BF16), preferred_element_type=F32
        )
        share = lax.psum_scatter(share, "dp", scatter_dimension=0, tiled=True)
        grad_weight = lax.psum(share, "ctx")

    return grad_query, grad_key, grad_value, grad_decay, grad_weight


def solution(mesh):
    placed = (
        P("dp", "ctx", None),
        P("dp", "ctx", None),
        P("dp", "ctx", None),
        P("dp", "ctx", None),
        P(),
        P("dp", "ctx", None),
    )
    return jax.shard_map(
        body,
        mesh=mesh,
        in_specs=placed,
        out_specs=(
            P("dp", "ctx", None),
            P("dp", "ctx", None),
            P("dp", "ctx", None),
            P("dp", "ctx", None),
            P("dp", None),
        ),
        check_vma=False,
    )
```

```python
import functools

import jax
import jax.numpy as jnp
from jax import lax
from jax.experimental import pallas as pl
from jax.experimental.pallas import tpu as pltpu
from jax.sharding import PartitionSpec as P

EPSILON = 1e-05
VMEM_BYTES = 24 * 1024 * 1024
F32 = jnp.float32
BF16 = jnp.bfloat16
BOTH = ("dp", "ctx")


def split(value, parts):
    if value.dtype == BF16:
        return [value]
    pieces = []
    for index in range(parts):
        piece = value.astype(BF16)
        pieces.append(piece)
        if index + 1 < parts:
            value = value - piece.astype(F32)
    return pieces


def product(left, right, left_axis, right_axis):
    dims = (((left_axis,), (right_axis,)), ((), ()))
    most = max(len(left), len(right))
    total = None
    for order in reversed(range(most)):
        for i, l in enumerate(left):
            j = order - i
            if 0 <= j < len(right):
                term = lax.dot_general(l, right[j], dims, preferred_element_type=F32)
                total = term if total is None else total + term
    return total


def lower_mask(length):
    rows = lax.broadcasted_iota(jnp.int32, (length, length), 0)
    columns = lax.broadcasted_iota(jnp.int32, (length, length), 1)
    return rows >= columns


def cumulate(decay):
    lower = lower_mask(decay.shape[0]).astype(F32).astype(BF16)
    return product([lower], split(decay, 3), 1, 0)


def state_kernel(key_ref, value_ref, decay_ref, state_ref):
    cumul = cumulate(decay_ref[0])
    to_end = jnp.exp(cumul[-1:] - cumul)
    key_to_end = key_ref[0].astype(F32) * to_end
    state_ref[...] = product(split(key_to_end, 2), [value_ref[0]], 0, 0)


def within_kernel(query_ref, key_ref, value_ref, decay_ref, within_ref, scores_ref, cumul_ref):
    cumul = cumulate(decay_ref[0])
    cumul_ref[...] = cumul
    query_scaled = query_ref[0].astype(F32) * jnp.exp(cumul)
    key_scaled = key_ref[0].astype(F32) * jnp.exp(-cumul)
    scores = product(split(query_scaled, 2), split(key_scaled, 2), 1, 1)
    scores = jnp.where(lower_mask(cumul.shape[0]), scores, 0.0)
    scores_ref[...] = scores
    within_ref[...] = product(split(scores, 2), [value_ref[0]], 1, 0)


def normed_kernel(query_ref, cumul_ref, within_ref, state_ref, normed_ref, scale_ref, rounded_ref):
    query_scaled = query_ref[0].astype(F32) * jnp.exp(cumul_ref[...])
    output = within_ref[...] + product(split(query_scaled, 2), split(state_ref[...], 2), 1, 0)
    scale_inv = lax.rsqrt(jnp.mean(output * output, axis=-1, keepdims=True) + EPSILON)
    normed = output * scale_inv
    normed_ref[...] = normed
    scale_ref[...] = jnp.broadcast_to(scale_inv, normed.shape)
    rounded_ref[...] = normed.astype(BF16).astype(F32)


def grads_kernel(
    packed_ref, cumul_ref, scores_ref, state_ref, normed_ref, scale_ref,
    upstream_ref, weight_ref,
    grad_query_ref, grad_key_ref, grad_value_ref, gate_ref, sent_ref,
):
    query = packed_ref[0]
    key = packed_ref[1]
    value = packed_ref[2].astype(BF16)
    cumul = cumul_ref[...]
    rising = jnp.exp(cumul)
    falling = jnp.exp(-cumul)
    normed = normed_ref[...]
    grad_normed = jnp.dot(upstream_ref[0], weight_ref[...], preferred_element_type=F32)
    grad_output = scale_ref[...] * (
        grad_normed - normed * jnp.mean(grad_normed * normed, axis=-1, keepdims=True)
    )
    grad_output = split(grad_output, 2)
    query_scaled = split(query * rising, 2)
    key_scaled = split(key * falling, 2)
    pairs = product(grad_output, [value], 1, 1)
    pairs = split(jnp.where(lower_mask(cumul.shape[0]), pairs, 0.0), 2)
    grad_query = rising * (
        product(pairs, key_scaled, 1, 0) + product(grad_output, split(state_ref[...], 2), 1, 1)
    )
    grad_query_ref[0] = grad_query.astype(BF16)
    grad_key = falling * product(pairs, query_scaled, 0, 0)
    grad_key_ref[...] = grad_key
    grad_value_ref[...] = product(split(scores_ref[...], 2), grad_output, 0, 0)
    gate = query * grad_query - key * grad_key
    gate_ref[...] = gate
    width = query.shape[1]
    sent_ref[:width] = product(query_scaled, grad_output, 0, 0)
    sent_ref[width:] = jnp.broadcast_to(
        jnp.sum(gate, axis=0, keepdims=True), (sent_ref.shape[0] - width, width)
    )


def finish_kernel(
    packed_ref, cumul_ref, grad_key_ref, grad_value_ref, gate_ref, later_ref,
    key_out_ref, value_out_ref, decay_out_ref,
):
    key = packed_ref[1]
    cumul = cumul_ref[...]
    width = key.shape[1]
    to_end = jnp.exp(cumul[-1:] - cumul)
    last = lax.axis_index("ctx") == lax.axis_size("ctx") - 1
    later = jnp.where(last, 0.0, later_ref[...])
    grad_in = split(later[:width], 2)
    extra = to_end * product([packed_ref[2].astype(BF16)], grad_in, 1, 1)
    key_out_ref[0] = (grad_key_ref[...] + extra).astype(BF16)
    grad_value = grad_value_ref[...] + product(split(key * to_end, 2), grad_in, 1, 0)
    value_out_ref[0] = grad_value.astype(BF16)
    gate = gate_ref[...] - key * extra
    lower = lower_mask(cumul.shape[0]).astype(F32).astype(BF16)
    decay_out_ref[0] = product([lower], split(gate, 3), 0, 0) + later[width:width + 1]


def local_call(kernel, shapes, *operands, name, flops, scratch=(), space=pltpu.VMEM, limit=VMEM_BYTES):
    outs = [jax.ShapeDtypeStruct(shape, dtype) for shape, dtype in shapes]
    moved = sum(array.size * array.dtype.itemsize for array in [*operands, *outs])
    return pl.pallas_call(
        kernel,
        out_shape=outs,
        in_specs=[pl.BlockSpec(memory_space=space)] * len(operands),
        scratch_shapes=list(scratch),
        compiler_params=pltpu.CompilerParams(vmem_limit_bytes=limit),
        cost_estimate=pl.CostEstimate(flops=flops, bytes_accessed=moved, transcendentals=0),
        name=name,
    )(*operands)


def swap(value):
    return lax.ppermute(value, "ctx", [(0, 1), (1, 0)])


def halving_plan(count, rows):
    bits = count.bit_length() - 1
    last = rows // 32 * 16
    rest = list(range(3, bits))
    return [
        (rows - last, ([0, 1, 2] + rest, [1, 0, 2] + rest)),
        (last, ([2, 0, 1] + rest, [1, 2, 0] + rest)),
    ]


def relative(place, order):
    top = len(order) - 1
    return sum(((place >> (top - step)) & 1) << bit for step, bit in enumerate(order))


def lower_kernel(lower_ref):
    lower_ref[...] = lower_mask(lower_ref.shape[0]).astype(F32).astype(BF16)


def rows_of(count, plan, me, core, part, share):
    half = share // 2
    offset = 0
    for rows, orders in plan:
        for place in part:
            masks = [relative(place, order) for order in orders]
            owner = me ^ (masks[0] + core * (masks[1] - masks[0]))
            yield pl.multiple_of(owner * share + core * half + offset, 16), rows
        offset += rows


def turn_kernel(count, plan, upstream_ref, turned_ref, first_ref):
    me, core = lax.axis_index("dp"), lax.axis_index("ctx")
    model = turned_ref.shape[0]
    lanes = 128
    for start in range(0, model, lanes):
        turned_ref[start:start + lanes] = jnp.transpose(
            upstream_ref[0, :, start:start + lanes].astype(F32)
        )
    at = 0
    for begin, rows in rows_of(count, plan, me, 1 - core, range(count // 2, count), model // count):
        first_ref[at:at + rows] = turned_ref[pl.ds(begin, rows)]
        at += rows


def rest_kernel(count, plan, turned_ref, own_ref, second_ref):
    me, core = lax.axis_index("dp"), lax.axis_index("ctx")
    share = turned_ref.shape[0] // count
    at = 0
    for part in (range(count // 2, count), range(count // 2)):
        for begin, rows in rows_of(count, plan, me, core, part, share):
            own_ref[at:at + rows] = turned_ref[pl.ds(begin, rows)].astype(BF16)
            at += rows
    at = 0
    for begin, rows in rows_of(count, plan, me, 1 - core, range(count // 2), share):
        second_ref[at:at + rows] = turned_ref[pl.ds(begin, rows)]
        at += rows


def joined(pairs, left_axis, right_axis):
    lefts, rights = [], []
    for left, left_parts, right, right_parts in pairs:
        left, right = split(left, left_parts), split(right, right_parts)
        for i in range(left_parts):
            for j in range(right_parts):
                if i + j < max(left_parts, right_parts):
                    lefts.append(left[i])
                    rights.append(right[j])
    return lax.dot_general(
        jnp.concatenate(lefts, axis=left_axis),
        jnp.concatenate(rights, axis=right_axis),
        (((left_axis,), (right_axis,)), ((), ())),
        preferred_element_type=F32,
    )


def joint_kernel(
    own_ref, other_ref, lower_ref,
    cumul_ref, scores_ref, state_ref, normed_ref, scale_ref, rounded_ref,
):
    first = lax.axis_index("ctx") == 0
    length, width = cumul_ref.shape
    lower = lower_mask(length)

    def normalized(output):
        scale_inv = lax.rsqrt(jnp.mean(output * output, axis=-1, keepdims=True) + EPSILON)
        normed = output * scale_inv
        return normed, jnp.broadcast_to(scale_inv, normed.shape), normed.astype(BF16)

    query, key, value, decay = [
        [jnp.where(first, own_ref[i], other_ref[i]), jnp.where(first, other_ref[i], own_ref[i])]
        for i in range(4)
    ]
    cumuls = joined([(lower_ref[...], 1, jnp.concatenate(decay, axis=1), 3)], 1, 0)
    cumul = [cumuls[:, :width], cumuls[:, width:]]
    scaled = [q * jnp.exp(c) for q, c in zip(query, cumul)]
    scores = [
        jnp.where(lower, joined([(q, 2, k * jnp.exp(-c), 2)], 1, 1), 0.0)
        for q, k, c in zip(scaled, key, cumul)
    ]
    to_end = jnp.exp(cumul[0][-1:] - cumul[0])
    state = joined([(key[0] * to_end, 2, value[0], 1)], 0, 0)
    early = normalized(joined([(scores[0], 2, value[0], 1)], 1, 0))
    late = normalized(joined([(scores[1], 2, value[1], 1), (scaled[1], 2, state, 2)], 1, 0))
    rounded_ref[:length] = jnp.where(first, early[2], late[2])
    rounded_ref[length:] = jnp.where(first, late[2], early[2])
    cumul_ref[...] = jnp.where(first, cumul[0], cumul[1])
    scores_ref[...] = jnp.where(first, scores[0], scores[1])
    state_ref[...] = jnp.where(first, 0.0, state)
    normed_ref[...] = jnp.where(first, early[0], late[0])
    scale_ref[...] = jnp.where(first, early[1], late[1])


def share_kernel(begin, own_ref, received_ref, rounded_ref, *outs):
    at = 0
    for out in outs:
        rows = out.shape[0]
        left = jnp.concatenate(
            [own_ref[begin + at:begin + at + rows], received_ref[at:at + rows].astype(BF16)], axis=1
        )
        out[...] = jnp.dot(left, rounded_ref[...], preferred_element_type=F32)
        at += rows


def own_part_kernel(own_ref, rounded_ref, *outs):
    at = 0
    for out in outs:
        rows = out.shape[0]
        out[...] = jnp.dot(
            own_ref[at:at + rows], rounded_ref[: rounded_ref.shape[0] // 2], preferred_element_type=F32
        )
        at += rows


def add_part_kernel(begin, received_ref, rounded_ref, *refs):
    at = begin
    for part, out in zip(refs[: len(refs) // 2], refs[len(refs) // 2:]):
        rows = out.shape[0]
        out[...] = part[...] + jnp.dot(
            received_ref[at:at + rows].astype(BF16), rounded_ref[rounded_ref.shape[0] // 2:],
            preferred_element_type=F32,
        )
        at += rows


def exchanged(value, count, bits):
    pairs = [
        (device * 2 + core, (device ^ (1 << bits[core])) * 2 + core)
        for device in range(count)
        for core in range(2)
    ]
    return lax.ppermute(value, BOTH, pairs)


def halving(kept, sent, plan, count, beside):
    stages = len(plan[0][1][0])
    joined = 3
    for stage in range(joined):
        arrived = [
            exchanged(part, count, [order[stage] for order in orders])
            for part, (_, orders) in zip(sent, plan)
        ]
        if stage in beside:
            arrived = beside[stage](arrived)
        half = [len(part) // 2 if stage + 1 < stages else len(part) for part in kept]
        sums = [
            (old[:size] + new[:size], old[size:] + new[size:])
            for old, new, size in zip(kept, arrived, half)
        ]
        kept = [pair[0] for pair in sums]
        sent = [pair[1] for pair in sums]
    for stage in range(joined, stages):
        sizes = [len(part) for part in sent]
        new = exchanged(jnp.concatenate(sent), count, [stage] * 2)
        if stage in beside:
            new = beside[stage](new)
        starts = [sum(sizes[:index]) for index in range(len(sizes))]
        sums = [part + new[at:at + size] for part, at, size in zip(kept, starts, sizes)]
        kept = [part[: len(part) // 2] if stage + 1 < stages else part for part in sums]
        sent = [part[len(part) // 2:] for part in sums]
    return jnp.concatenate(kept)


def assemble_kernel(mine_ref, theirs_ref, out_ref):
    core = lax.axis_index("ctx")
    rows = mine_ref.shape[0]
    out_ref[pl.ds(pl.multiple_of(core * rows, 8), rows)] = mine_ref[...]
    out_ref[pl.ds(pl.multiple_of((1 - core) * rows, 8), rows)] = theirs_ref[...]


def shifted(value, axis, steps):
    count = lax.axis_size(axis)
    leading, last = (max(0, -steps), min(count, count - steps))
    return lax.ppermute(value, axis, [(source, source + steps) for source in range(leading, last)])


def body(queries, key_vectors, value_vectors, log_decay, out_weight, cotangent):
    length, width = queries.shape[1:]
    model = cotangent.shape[2]
    shards, count = lax.axis_size("ctx"), lax.axis_size("dp")
    square = (length, width)
    rows = model // count // 2
    flops = 8 * length * width * model
    paired = shards == 2 and count >= 16 and count & (count - 1) == 0 and rows % 16 == 0

    (lower,) = local_call(lower_kernel, [((length, length), BF16)], name="lower", flops=20 * flops)
    inputs = (queries, key_vectors, value_vectors, log_decay)
    *inputs, lower = lax.optimization_barrier((*inputs, lower))
    packed = jnp.concatenate([jnp.concatenate(inputs[:3]).astype(F32), inputs[3]])
    if paired:
        plan = halving_plan(count, rows)
        part_rows = rows * count // 2
        turned, send_first = local_call(
            functools.partial(turn_kernel, count, plan),
            [((model, length), F32), ((part_rows, length), F32)],
            cotangent,
            name="turn", flops=20 * flops,
        )
        own, send_second = local_call(
            functools.partial(rest_kernel, count, plan),
            [((2 * part_rows, length), BF16), ((part_rows, length), F32)],
            turned,
            name="rest", flops=flops,
        )
        others = swap(packed)
        received_first = swap(send_first)
        cumul, scores, state_in, normed, scale_inv, rounded = local_call(
            joint_kernel,
            [
                (square, F32), ((length, length), F32), ((width, width), F32), (square, F32),
                (square, F32), ((2 * length, width), BF16),
            ],
            packed, others, lower,
            name="joint", flops=40 * flops,
        )
        rounded, send_second = lax.optimization_barrier((rounded, send_second))
        received_second = swap(send_second)
        part_shapes = [((count // 2 * part, width), F32) for part, _ in plan]
        own_part = local_call(
            own_part_kernel, part_shapes, own, rounded, name="own_part", flops=flops // 4
        )
        sent = []
        begin = 0
        for part, shape in zip(own_part, part_shapes):
            sent += local_call(
                functools.partial(add_part_kernel, begin), [shape], received_first, rounded, part,
                name="sent_share", flops=flops // 4,
            )
            begin += shape[0][0]
        kept = local_call(
            functools.partial(share_kernel, part_rows),
            [((count // 2 * part, width), F32) for part, _ in plan],
            own, received_second, rounded,
            name="kept_shares", flops=flops // 4,
        )
    else:
        (local_state,) = local_call(
            state_kernel, [((width, width), F32)], key_vectors, value_vectors, log_decay,
            name="state", flops=flops // 2,
        )
        state_in = shifted(local_state, "ctx", 1)
        within, scores, cumul = local_call(
            within_kernel,
            [(square, F32), ((length, length), F32), (square, F32)],
            queries, key_vectors, value_vectors, log_decay,
            name="within", flops=flops // 2,
        )
        device_decay = jnp.exp(cumul[-1])[:, None]
        for _ in range(shards - 2):
            state_in = shifted(local_state + device_decay * state_in, "ctx", 1)
        normed, scale_inv, rounded = local_call(
            normed_kernel, [(square, F32)] * 3, queries, cumul, within, state_in,
            name="normed", flops=flops // 4,
        )

    grad_query, grad_key_zero, grad_value_zero, gate, grad_sent = local_call(
        grads_kernel,
        [
            (queries.shape, BF16), (square, F32), (square, F32), (square, F32),
            ((width + 8, width), F32),
        ],
        packed, cumul, scores, state_in, normed, scale_inv,
        cotangent, out_weight,
        name="grads", flops=2 * flops,
    )
    later = swap(grad_sent) if paired else shifted(grad_sent, "ctx", -1)

    def finish(later):
        return local_call(
            finish_kernel,
            [(queries.shape, BF16), (queries.shape, BF16), (queries.shape, F32)],
            packed, cumul, grad_key_zero, grad_value_zero, gate, later,
            name="finish", flops=flops,
        )

    if paired:
        held = {}

        def beside_first(arrived):
            large, small = arrived
            large, held["query"] = lax.optimization_barrier((large, grad_query))
            return [large, small]

        def beside_third(arrived):
            large, small = arrived
            large, held["later"] = lax.optimization_barrier((large, later))
            return [large, small]

        def beside_last(arrived):
            key, value, decay = finish(held["later"])
            arrived, decay = lax.optimization_barrier((arrived, decay))
            held["finished"] = key, value, decay
            return arrived

        beside = {0: beside_first, 2: beside_third, 3: beside_last}
        mine = halving(kept, sent, plan, count, beside)
        grad_query = held["query"]
        grad_key, grad_value, grad_decay = held["finished"]
        (grad_weight,) = local_call(
            assemble_kernel, [((2 * rows, width), F32)], mine, swap(mine),
            name="assemble", flops=flops // 4,
        )
    else:
        for _ in range(shards - 2):
            grad_in = later[:width]
            own_sum = grad_sent[width:] - jnp.sum(grad_in * local_state, axis=-1)[None]
            later = shifted(
                jnp.concatenate([grad_sent[:width] + device_decay * grad_in, own_sum + later[width:]]),
                "ctx",
                -1,
            )
        grad_key, grad_value, grad_decay = finish(later)
        share = jnp.einsum(
            "td,tk->dk", cotangent[0], rounded.astype(BF16), preferred_element_type=F32
        )
        share = lax.psum_scatter(share, "dp", scatter_dimension=0, tiled=True)
        grad_weight = lax.psum(share, "ctx")

    return grad_query, grad_key, grad_value, grad_decay, grad_weight


def solution(mesh):
    placed = (
        P("dp", "ctx", None),
        P("dp", "ctx", None),
        P("dp", "ctx", None),
        P("dp", "ctx", None),
        P(),
        P("dp", "ctx", None),
    )
    return jax.shard_map(
        body,
        mesh=mesh,
        in_specs=placed,
        out_specs=(
            P("dp", "ctx", None),
            P("dp", "ctx", None),
            P("dp", "ctx", None),
            P("dp", "ctx", None),
            P("dp", None),
        ),
        check_vma=False,
    )
```

```python
import functools

import jax
import jax.numpy as jnp
from jax import lax
from jax.experimental import pallas as pl
from jax.experimental.pallas import tpu as pltpu
from jax.sharding import PartitionSpec as P

EPSILON = 1e-05
VMEM_BYTES = 24 * 1024 * 1024
F32 = jnp.float32
BF16 = jnp.bfloat16
BOTH = ("dp", "ctx")


def split(value, parts):
    if value.dtype == BF16:
        return [value]
    pieces = []
    for index in range(parts):
        piece = value.astype(BF16)
        pieces.append(piece)
        if index + 1 < parts:
            value = value - piece.astype(F32)
    return pieces


def product(left, right, left_axis, right_axis):
    dims = (((left_axis,), (right_axis,)), ((), ()))
    most = max(len(left), len(right))
    total = None
    for order in reversed(range(most)):
        for i, l in enumerate(left):
            j = order - i
            if 0 <= j < len(right):
                term = lax.dot_general(l, right[j], dims, preferred_element_type=F32)
                total = term if total is None else total + term
    return total


def lower_mask(length):
    rows = lax.broadcasted_iota(jnp.int32, (length, length), 0)
    columns = lax.broadcasted_iota(jnp.int32, (length, length), 1)
    return rows >= columns


def cumulate(decay):
    lower = lower_mask(decay.shape[0]).astype(F32).astype(BF16)
    return product([lower], split(decay, 3), 1, 0)


def state_kernel(key_ref, value_ref, decay_ref, state_ref):
    cumul = cumulate(decay_ref[0])
    to_end = jnp.exp(cumul[-1:] - cumul)
    key_to_end = key_ref[0].astype(F32) * to_end
    state_ref[...] = product(split(key_to_end, 3), [value_ref[0]], 0, 0)


def within_kernel(query_ref, key_ref, value_ref, decay_ref, within_ref, scores_ref, cumul_ref):
    cumul = cumulate(decay_ref[0])
    cumul_ref[...] = cumul
    query_scaled = query_ref[0].astype(F32) * jnp.exp(cumul)
    key_scaled = key_ref[0].astype(F32) * jnp.exp(-cumul)
    scores = product(split(query_scaled, 3), split(key_scaled, 3), 1, 1)
    scores = jnp.where(lower_mask(cumul.shape[0]), scores, 0.0)
    scores_ref[...] = scores
    within_ref[...] = product(split(scores, 3), [value_ref[0]], 1, 0)


def normed_kernel(query_ref, cumul_ref, within_ref, state_ref, normed_ref, scale_ref, rounded_ref):
    query_scaled = query_ref[0].astype(F32) * jnp.exp(cumul_ref[...])
    output = within_ref[...] + product(split(query_scaled, 3), split(state_ref[...], 3), 1, 0)
    scale_inv = lax.rsqrt(jnp.mean(output * output, axis=-1, keepdims=True) + EPSILON)
    normed = output * scale_inv
    normed_ref[...] = normed
    scale_ref[...] = jnp.broadcast_to(scale_inv, normed.shape)
    rounded_ref[...] = normed.astype(BF16).astype(F32)


def grads_kernel(
    packed_ref, cumul_ref, scores_ref, state_ref, normed_ref, scale_ref,
    upstream_ref, weight_ref,
    grad_query_ref, grad_key_ref, grad_value_ref, gate_ref, sent_ref,
):
    query = packed_ref[0]
    key = packed_ref[1]
    value = packed_ref[2].astype(BF16)
    cumul = cumul_ref[...]
    rising = jnp.exp(cumul)
    falling = jnp.exp(-cumul)
    normed = normed_ref[...]
    grad_normed = jnp.dot(upstream_ref[0], weight_ref[...], preferred_element_type=F32)
    grad_output = scale_ref[...] * (
        grad_normed - normed * jnp.mean(grad_normed * normed, axis=-1, keepdims=True)
    )
    grad_output = split(grad_output, 3)
    query_scaled = split(query * rising, 3)
    key_scaled = split(key * falling, 3)
    pairs = product(grad_output, [value], 1, 1)
    pairs = split(jnp.where(lower_mask(cumul.shape[0]), pairs, 0.0), 3)
    grad_query = rising * (
        product(pairs, key_scaled, 1, 0) + product(grad_output, split(state_ref[...], 3), 1, 1)
    )
    grad_query_ref[0] = grad_query.astype(BF16)
    grad_key = falling * product(pairs, query_scaled, 0, 0)
    grad_key_ref[...] = grad_key
    grad_value_ref[...] = product(split(scores_ref[...], 3), grad_output, 0, 0)
    gate = query * grad_query - key * grad_key
    gate_ref[...] = gate
    width = query.shape[1]
    sent_ref[:width] = product(query_scaled, grad_output, 0, 0)
    sent_ref[width:] = jnp.broadcast_to(
        jnp.sum(gate, axis=0, keepdims=True), (sent_ref.shape[0] - width, width)
    )


def finish_kernel(
    packed_ref, cumul_ref, grad_key_ref, grad_value_ref, gate_ref, later_ref,
    key_out_ref, value_out_ref, decay_out_ref,
):
    key = packed_ref[1]
    cumul = cumul_ref[...]
    width = key.shape[1]
    to_end = jnp.exp(cumul[-1:] - cumul)
    last = lax.axis_index("ctx") == lax.axis_size("ctx") - 1
    later = jnp.where(last, 0.0, later_ref[...])
    grad_in = split(later[:width], 3)
    extra = to_end * product([packed_ref[2].astype(BF16)], grad_in, 1, 1)
    key_out_ref[0] = (grad_key_ref[...] + extra).astype(BF16)
    grad_value = grad_value_ref[...] + product(split(key * to_end, 3), grad_in, 1, 0)
    value_out_ref[0] = grad_value.astype(BF16)
    gate = gate_ref[...] - key * extra
    lower = lower_mask(cumul.shape[0]).astype(F32).astype(BF16)
    decay_out_ref[0] = product([lower], split(gate, 3), 0, 0) + later[width:width + 1]


def local_call(kernel, shapes, *operands, name, flops, scratch=(), space=pltpu.VMEM, limit=VMEM_BYTES):
    outs = [jax.ShapeDtypeStruct(shape, dtype) for shape, dtype in shapes]
    moved = sum(array.size * array.dtype.itemsize for array in [*operands, *outs])
    return pl.pallas_call(
        kernel,
        out_shape=outs,
        in_specs=[pl.BlockSpec(memory_space=space)] * len(operands),
        scratch_shapes=list(scratch),
        compiler_params=pltpu.CompilerParams(vmem_limit_bytes=limit),
        cost_estimate=pl.CostEstimate(flops=flops, bytes_accessed=moved, transcendentals=0),
        name=name,
    )(*operands)


def swap(value):
    return lax.ppermute(value, "ctx", [(0, 1), (1, 0)])


def halving_plan(count, rows):
    bits = count.bit_length() - 1
    last = rows // 32 * 16
    rest = list(range(3, bits))
    return [
        (rows - last, ([0, 1, 2] + rest, [1, 0, 2] + rest)),
        (last, ([2, 0, 1] + rest, [1, 2, 0] + rest)),
    ]


def relative(place, order):
    top = len(order) - 1
    return sum(((place >> (top - step)) & 1) << bit for step, bit in enumerate(order))


def lower_kernel(lower_ref):
    lower_ref[...] = lower_mask(lower_ref.shape[0]).astype(F32).astype(BF16)


def rows_of(count, plan, me, core, part, share):
    half = share // 2
    offset = 0
    for rows, orders in plan:
        for place in part:
            masks = [relative(place, order) for order in orders]
            owner = me ^ (masks[0] + core * (masks[1] - masks[0]))
            yield pl.multiple_of(owner * share + core * half + offset, 16), rows
        offset += rows


def turn_kernel(count, plan, upstream_ref, turned_ref, first_ref):
    me, core = lax.axis_index("dp"), lax.axis_index("ctx")
    model = turned_ref.shape[0]
    lanes = 128
    for start in range(0, model, lanes):
        turned_ref[start:start + lanes] = jnp.transpose(
            upstream_ref[0, :, start:start + lanes].astype(F32)
        )
    at = 0
    for begin, rows in rows_of(count, plan, me, 1 - core, range(count // 2, count), model // count):
        first_ref[at:at + rows] = turned_ref[pl.ds(begin, rows)]
        at += rows


def rest_kernel(count, plan, turned_ref, own_ref, second_ref):
    me, core = lax.axis_index("dp"), lax.axis_index("ctx")
    share = turned_ref.shape[0] // count
    at = 0
    for part in (range(count // 2, count), range(count // 2)):
        for begin, rows in rows_of(count, plan, me, core, part, share):
            own_ref[at:at + rows] = turned_ref[pl.ds(begin, rows)].astype(BF16)
            at += rows
    at = 0
    for begin, rows in rows_of(count, plan, me, 1 - core, range(count // 2), share):
        second_ref[at:at + rows] = turned_ref[pl.ds(begin, rows)]
        at += rows


def joined(pairs, left_axis, right_axis):
    lefts, rights = [], []
    for left, left_parts, right, right_parts in pairs:
        left, right = split(left, left_parts), split(right, right_parts)
        for i in range(left_parts):
            for j in range(right_parts):
                if i + j < max(left_parts, right_parts):
                    lefts.append(left[i])
                    rights.append(right[j])
    return lax.dot_general(
        jnp.concatenate(lefts, axis=left_axis),
        jnp.concatenate(rights, axis=right_axis),
        (((left_axis,), (right_axis,)), ((), ())),
        preferred_element_type=F32,
    )


def joint_kernel(
    own_ref, other_ref, lower_ref,
    cumul_ref, scores_ref, state_ref, normed_ref, scale_ref, rounded_ref,
):
    first = lax.axis_index("ctx") == 0
    length, width = cumul_ref.shape
    lower = lower_mask(length)

    def normalized(output):
        scale_inv = lax.rsqrt(jnp.mean(output * output, axis=-1, keepdims=True) + EPSILON)
        normed = output * scale_inv
        return normed, jnp.broadcast_to(scale_inv, normed.shape), normed.astype(BF16)

    query, key, value, decay = [
        [jnp.where(first, own_ref[i], other_ref[i]), jnp.where(first, other_ref[i], own_ref[i])]
        for i in range(4)
    ]
    cumuls = joined([(lower_ref[...], 1, jnp.concatenate(decay, axis=1), 3)], 1, 0)
    cumul = [cumuls[:, :width], cumuls[:, width:]]
    scaled = [q * jnp.exp(c) for q, c in zip(query, cumul)]
    scores = [
        jnp.where(lower, joined([(q, 3, k * jnp.exp(-c), 3)], 1, 1), 0.0)
        for q, k, c in zip(scaled, key, cumul)
    ]
    to_end = jnp.exp(cumul[0][-1:] - cumul[0])
    state = joined([(key[0] * to_end, 3, value[0], 1)], 0, 0)
    early = normalized(joined([(scores[0], 3, value[0], 1)], 1, 0))
    late = normalized(joined([(scores[1], 3, value[1], 1), (scaled[1], 3, state, 3)], 1, 0))
    rounded_ref[:length] = jnp.where(first, early[2], late[2])
    rounded_ref[length:] = jnp.where(first, late[2], early[2])
    cumul_ref[...] = jnp.where(first, cumul[0], cumul[1])
    scores_ref[...] = jnp.where(first, scores[0], scores[1])
    state_ref[...] = jnp.where(first, 0.0, state)
    normed_ref[...] = jnp.where(first, early[0], late[0])
    scale_ref[...] = jnp.where(first, early[1], late[1])


def share_kernel(begin, own_ref, received_ref, rounded_ref, *outs):
    at = 0
    for out in outs:
        rows = out.shape[0]
        left = jnp.concatenate(
            [own_ref[begin + at:begin + at + rows], received_ref[at:at + rows].astype(BF16)], axis=1
        )
        out[...] = jnp.dot(left, rounded_ref[...], preferred_element_type=F32)
        at += rows


def own_part_kernel(own_ref, rounded_ref, *outs):
    at = 0
    for out in outs:
        rows = out.shape[0]
        out[...] = jnp.dot(
            own_ref[at:at + rows], rounded_ref[: rounded_ref.shape[0] // 2], preferred_element_type=F32
        )
        at += rows


def add_part_kernel(received_ref, rounded_ref, *refs):
    at = 0
    for part, out in zip(refs[: len(refs) // 2], refs[len(refs) // 2:]):
        rows = out.shape[0]
        out[...] = part[...] + jnp.dot(
            received_ref[at:at + rows].astype(BF16), rounded_ref[rounded_ref.shape[0] // 2:],
            preferred_element_type=F32,
        )
        at += rows


def exchanged(value, count, bits):
    pairs = [
        (device * 2 + core, (device ^ (1 << bits[core])) * 2 + core)
        for device in range(count)
        for core in range(2)
    ]
    return lax.ppermute(value, BOTH, pairs)


def halving(kept, sent, plan, count, beside):
    stages = len(plan[0][1][0])
    joined = 3
    for stage in range(joined):
        arrived = [
            exchanged(part, count, [order[stage] for order in orders])
            for part, (_, orders) in zip(sent, plan)
        ]
        if stage in beside:
            arrived = beside[stage](arrived)
        half = [len(part) // 2 if stage + 1 < stages else len(part) for part in kept]
        sums = [
            (old[:size] + new[:size], old[size:] + new[size:])
            for old, new, size in zip(kept, arrived, half)
        ]
        kept = [pair[0] for pair in sums]
        sent = [pair[1] for pair in sums]
    for stage in range(joined, stages):
        sizes = [len(part) for part in sent]
        new = exchanged(jnp.concatenate(sent), count, [stage] * 2)
        if stage in beside:
            new = beside[stage](new)
        starts = [sum(sizes[:index]) for index in range(len(sizes))]
        sums = [part + new[at:at + size] for part, at, size in zip(kept, starts, sizes)]
        kept = [part[: len(part) // 2] if stage + 1 < stages else part for part in sums]
        sent = [part[len(part) // 2:] for part in sums]
    return jnp.concatenate(kept)


def assemble_kernel(mine_ref, theirs_ref, out_ref):
    core = lax.axis_index("ctx")
    rows = mine_ref.shape[0]
    out_ref[pl.ds(pl.multiple_of(core * rows, 8), rows)] = mine_ref[...]
    out_ref[pl.ds(pl.multiple_of((1 - core) * rows, 8), rows)] = theirs_ref[...]


def shifted(value, axis, steps):
    count = lax.axis_size(axis)
    leading, last = (max(0, -steps), min(count, count - steps))
    return lax.ppermute(value, axis, [(source, source + steps) for source in range(leading, last)])


def body(queries, key_vectors, value_vectors, log_decay, out_weight, cotangent):
    length, width = queries.shape[1:]
    model = cotangent.shape[2]
    shards, count = lax.axis_size("ctx"), lax.axis_size("dp")
    square = (length, width)
    rows = model // count // 2
    flops = 8 * length * width * model
    paired = shards == 2 and count >= 16 and count & (count - 1) == 0 and rows % 16 == 0

    (lower,) = local_call(lower_kernel, [((length, length), BF16)], name="lower", flops=20 * flops)
    inputs = (queries, key_vectors, value_vectors, log_decay)
    *inputs, lower = lax.optimization_barrier((*inputs, lower))
    packed = jnp.concatenate([jnp.concatenate(inputs[:3]).astype(F32), inputs[3]])
    if paired:
        plan = halving_plan(count, rows)
        part_rows = rows * count // 2
        turned, send_first = local_call(
            functools.partial(turn_kernel, count, plan),
            [((model, length), F32), ((part_rows, length), F32)],
            cotangent,
            name="turn", flops=20 * flops,
        )
        own, send_second = local_call(
            functools.partial(rest_kernel, count, plan),
            [((2 * part_rows, length), BF16), ((part_rows, length), F32)],
            turned,
            name="rest", flops=flops,
        )
        others = swap(packed)
        received_first = swap(send_first)
        cumul, scores, state_in, normed, scale_inv, rounded = local_call(
            joint_kernel,
            [
                (square, F32), ((length, length), F32), ((width, width), F32), (square, F32),
                (square, F32), ((2 * length, width), BF16),
            ],
            packed, others, lower,
            name="joint", flops=40 * flops,
        )
        rounded, send_second = lax.optimization_barrier((rounded, send_second))
        received_second = swap(send_second)
        part_shapes = [((count // 2 * part, width), F32) for part, _ in plan]
        own_part = local_call(
            own_part_kernel, part_shapes, own, rounded, name="own_part", flops=flops // 4
        )
        sent = local_call(
            add_part_kernel, part_shapes, received_first, rounded, *own_part,
            name="sent_shares", flops=flops // 4,
        )
        kept = local_call(
            functools.partial(share_kernel, part_rows),
            [((count // 2 * part, width), F32) for part, _ in plan],
            own, received_second, rounded,
            name="kept_shares", flops=flops // 4,
        )
    else:
        (local_state,) = local_call(
            state_kernel, [((width, width), F32)], key_vectors, value_vectors, log_decay,
            name="state", flops=flops // 2,
        )
        state_in = shifted(local_state, "ctx", 1)
        within, scores, cumul = local_call(
            within_kernel,
            [(square, F32), ((length, length), F32), (square, F32)],
            queries, key_vectors, value_vectors, log_decay,
            name="within", flops=flops // 2,
        )
        device_decay = jnp.exp(cumul[-1])[:, None]
        for _ in range(shards - 2):
            state_in = shifted(local_state + device_decay * state_in, "ctx", 1)
        normed, scale_inv, rounded = local_call(
            normed_kernel, [(square, F32)] * 3, queries, cumul, within, state_in,
            name="normed", flops=flops // 4,
        )

    grad_query, grad_key_zero, grad_value_zero, gate, grad_sent = local_call(
        grads_kernel,
        [
            (queries.shape, BF16), (square, F32), (square, F32), (square, F32),
            ((width + 8, width), F32),
        ],
        packed, cumul, scores, state_in, normed, scale_inv,
        cotangent, out_weight,
        name="grads", flops=2 * flops,
    )
    later = swap(grad_sent) if paired else shifted(grad_sent, "ctx", -1)

    def finish(later):
        return local_call(
            finish_kernel,
            [(queries.shape, BF16), (queries.shape, BF16), (queries.shape, F32)],
            packed, cumul, grad_key_zero, grad_value_zero, gate, later,
            name="finish", flops=flops,
        )

    if paired:
        held = {}

        def beside_first(arrived):
            large, small = arrived
            large, held["query"] = lax.optimization_barrier((large, grad_query))
            return [large, small]

        def beside_third(arrived):
            large, small = arrived
            large, held["later"] = lax.optimization_barrier((large, later))
            return [large, small]

        def beside_last(arrived):
            key, value, decay = finish(held["later"])
            arrived, decay = lax.optimization_barrier((arrived, decay))
            held["finished"] = key, value, decay
            return arrived

        beside = {0: beside_first, 2: beside_third, 3: beside_last}
        mine = halving(kept, sent, plan, count, beside)
        grad_query = held["query"]
        grad_key, grad_value, grad_decay = held["finished"]
        (grad_weight,) = local_call(
            assemble_kernel, [((2 * rows, width), F32)], mine, swap(mine),
            name="assemble", flops=flops // 4,
        )
    else:
        for _ in range(shards - 2):
            grad_in = later[:width]
            own_sum = grad_sent[width:] - jnp.sum(grad_in * local_state, axis=-1)[None]
            later = shifted(
                jnp.concatenate([grad_sent[:width] + device_decay * grad_in, own_sum + later[width:]]),
                "ctx",
                -1,
            )
        grad_key, grad_value, grad_decay = finish(later)
        share = jnp.einsum(
            "td,tk->dk", cotangent[0], rounded.astype(BF16), preferred_element_type=F32
        )
        share = lax.psum_scatter(share, "dp", scatter_dimension=0, tiled=True)
        grad_weight = lax.psum(share, "ctx")

    return grad_query, grad_key, grad_value, grad_decay, grad_weight


def solution(mesh):
    placed = (
        P("dp", "ctx", None),
        P("dp", "ctx", None),
        P("dp", "ctx", None),
        P("dp", "ctx", None),
        P(),
        P("dp", "ctx", None),
    )
    return jax.shard_map(
        body,
        mesh=mesh,
        in_specs=placed,
        out_specs=(
            P("dp", "ctx", None),
            P("dp", "ctx", None),
            P("dp", "ctx", None),
            P("dp", "ctx", None),
            P("dp", None),
        ),
        check_vma=False,
    )
```
